32 devices in a mesh: dp: 16 (over z, y, core), seq: 2 (over x).
Axes of the slice: x: 2, y: 2, z: 4, core: 2. Of those that a mesh axis runs over, the one named last changes fastest.
Arguments:
- patches: bfloat16 [64, 256, 48], P('dp', 'seq'), may hold values from -4 to 4
- labels: int32 [64], P('dp'), may hold values from 0 to 1023
- valid_mask: int32 [64, 256], P('dp', 'seq'), may hold values 0 or 1
- class_slot: int32 [1024], replicated, may hold values from 0 to 1023, each once
- w_patch: bfloat16 [48, 768], replicated, may hold values from -0.875 to 0.875
- b_patch: bfloat16 [768], replicated, may hold values from -4 to 4
- pos_embed: bfloat16 [256, 768], replicated, may hold values from -4 to 4
- class_embed: bfloat16 [1024, 768], replicated, may hold values from -4 to 4
- norm1_gain: bfloat16 [768], replicated, may hold values from 0.5 to 1.5
- norm1_shift: bfloat16 [768], replicated, may hold values from -4 to 4
- w_qkv: bfloat16 [768, 2304], replicated, may hold values from -0.21875 to 0.21875
- w_out: bfloat16 [768, 768], replicated, may hold values from -0.875 to 0.875
- norm2_gain: bfloat16 [768], replicated, may hold values from 0.5 to 1.5
- norm2_shift: bfloat16 [768], replicated, may hold values from -4 to 4
- w_fc1: bfloat16 [768, 3072], replicated, may hold values from -0.21875 to 0.21875
- b_fc1: bfloat16 [3072], replicated, may hold values from -4 to 4
- w_fc2: bfloat16 [3072, 768], replicated, may hold values from -0.109375 to 0.109375
- b_fc2: bfloat16 [768], replicated, may hold values from -4 to 4
- final_gain: bfloat16 [768], replicated, may hold values from 0.5 to 1.5
- final_shift: bfloat16 [768], replicated, may hold values from -4 to 4
- w_head: bfloat16 [768, 96], replicated, may hold values from -0.109375 to 0.109375
- b_head: bfloat16 [96], replicated, may hold values from -3 to 3
- cot_latent: float32 [64, 256, 48], P('dp', 'seq'), may hold values from -6 to 6
- cot_logdet: float32 [64], P('dp'), may hold values from -4 to 4
Outputs:
- latent: float32 [64, 256, 48], P('dp', 'seq')
- logdet: float32 [64], P('dp')
- grad_patches: float32 [64, 256, 48], P('dp', 'seq')
- grad_w_patch: float32 [48, 768], replicated
- grad_b_patch: float32 [768], replicated
- grad_pos_embed: float32 [256, 768], replicated
- grad_class_embed: float32 [1024, 768], P(('dp', 'seq'))
- grad_norm1_gain: float32 [768], replicated
- grad_norm1_shift: float32 [768], replicated
- grad_w_qkv: float32 [768, 2304], replicated
- grad_w_out: float32 [768, 768], replicated
- grad_norm2_gain: float32 [768], replicated
- grad_norm2_shift: float32 [768], replicated
- grad_w_fc1: float32 [768, 3072], P(None, ('dp', 'seq'))
- grad_b_fc1: float32 [3072], P(('dp', 'seq'))
- grad_w_fc2: float32 [3072, 768], P(('dp', 'seq'))
- grad_b_fc2: float32 [768], replicated
- grad_final_gain: float32 [768], replicated
- grad_final_shift: float32 [768], replicated
- grad_w_head: float32 [768, 96], replicated
- grad_b_head: float32 [96], replicated
- mean_logscale: float32 [], replicated
- max_logscale: float32 [], replicated
The draws below stay inside these ranges and needn't reach their ends.
Inputs may be any that keep to these rules, and one draw needn't show every extreme that they name: `class_slot`: each row number appears exactly once.
All inputs are finite; a program needn't handle non-finite values. No bound on the sum of `valid_mask` on one device may be relied on, other than what follows from the above.
Results may differ from the reference program's by a relative error of at most 0.009.
Values may be sent and summed in bfloat16 or wider, within the bound.
No kernel may reach another device: no remote copies, remote signals or barrier semaphores. Data moves between devices by JAX's collectives and lax.ppermute only.
A program may use at most 192 MiB of HBM per device.

```python
import math
import jax
import jax.numpy as jnp
from jax import lax

D = 768
HEADS = 12
HEAD_DIM = 64
FF = 3072
P_SIZE = 48
S = 256
CLASSES = 1024
ITEMS = 64


def place_ends(result, rng, least, largest):
    longest = result.shape.index(max(result.shape))
    spots = []
    for shift in (0, 1):
        where = [jax.random.randint(jax.random.fold_in(rng, axis), (), 0, length) for axis, length in enumerate(result.shape)]
        where[longest] = (where[longest] + shift) % result.shape[longest]
        spots.append(tuple(where))
    return result.at[spots[0]].set(least).at[spots[1]].set(largest)


def levels(key, dims, pieces, low, top_value):
    loudness, own = 1.0, jax.random.fold_in(key, 6)
    for position, blocks in pieces:
        heights = jnp.exp(jax.random.uniform(jax.random.fold_in(own, position), (blocks,), jnp.float32, low / len(pieces), top_value / len(pieces)))
        loudness = loudness * jnp.repeat(heights, dims[position] // blocks).reshape([-1 if axis == position else 1 for axis in range(len(dims))])
    return loudness


def normal_values(rng, shape, deviation, most, shards=(), dtype=jnp.bfloat16):
    entries = deviation * jax.random.normal(rng, shape, jnp.float32)
    if shards:
        entries = entries * levels(rng, shape, shards, -0.22, 0.18)
    return jnp.clip(entries, -most, most).astype(dtype)


def setup_inputs(seed: int = 0) -> dict:
    key_list = jax.random.split(jax.random.key(seed), 25)
    patches = normal_values(key_list[0], (ITEMS, S, P_SIZE), 1.0, 4.0, ((0, 16), (1, 2)))
    labels = place_ends(jax.random.randint(key_list[1], (ITEMS,), 0, CLASSES), jax.random.fold_in(key_list[1], 1), 0, CLASSES - 1).astype(jnp.int32)
    valid_mask = place_ends((jax.random.randint(key_list[2], (ITEMS, S), 0, 4) < 3).astype(jnp.int32), jax.random.fold_in(key_list[2], 1), 0, 1)
    class_slot = jax.random.permutation(key_list[3], CLASSES).astype(jnp.int32)
    w_patch = normal_values(key_list[4], (P_SIZE, D), P_SIZE ** -0.5, 0.875)
    b_patch = normal_values(key_list[5], (D,), 0.3, 4.0)
    pos_embed = normal_values(key_list[6], (S, D), 0.5, 4.0)
    class_embed = normal_values(key_list[7], (CLASSES, D), 0.5, 4.0)
    norm1_gain = jnp.clip(1.0 + 0.1 * jax.random.normal(key_list[8], (D,), jnp.float32), 0.5, 1.5).astype(jnp.bfloat16)
    norm1_shift = normal_values(key_list[9], (D,), 0.3, 4.0)
    w_qkv = normal_values(key_list[10], (D, 3 * D), D ** -0.5, 0.21875)
    w_out = normal_values(key_list[11], (D, D), (D // 16) ** -0.5, 0.875)
    norm2_gain = jnp.clip(1.0 + 0.1 * jax.random.normal(key_list[12], (D,), jnp.float32), 0.5, 1.5).astype(jnp.bfloat16)
    norm2_shift = normal_values(key_list[13], (D,), 0.3, 4.0)
    w_fc1 = normal_values(key_list[14], (D, FF), D ** -0.5, 0.21875)
    b_fc1 = normal_values(key_list[15], (FF,), 0.3, 4.0)
    w_fc2 = normal_values(key_list[16], (FF, D), FF ** -0.5, 0.109375)
    b_fc2 = normal_values(key_list[17], (D,), 0.3, 4.0)
    final_gain = jnp.clip(1.0 + 0.1 * jax.random.normal(key_list[18], (D,), jnp.float32), 0.5, 1.5).astype(jnp.bfloat16)
    final_shift = normal_values(key_list[19], (D,), 0.3, 4.0)
    w_head = normal_values(key_list[20], (D, 2 * P_SIZE), (4 * D) ** -0.5, 0.109375)
    b_head = normal_values(key_list[21], (2 * P_SIZE,), 0.2, 3.0)
    cot_latent = normal_values(key_list[22], (ITEMS, S, P_SIZE), 1.0, 6.0, ((0, 16), (1, 2)), jnp.float32)
    cot_logdet = normal_values(key_list[23], (ITEMS,), 1.0, 4.0, ((0, 16),), jnp.float32)
    return dict(patches=patches, labels=labels, valid_mask=valid_mask, class_slot=class_slot, w_patch=w_patch, b_patch=b_patch, pos_embed=pos_embed, class_embed=class_embed, norm1_gain=norm1_gain, norm1_shift=norm1_shift, w_qkv=w_qkv, w_out=w_out, norm2_gain=norm2_gain, norm2_shift=norm2_shift, w_fc1=w_fc1, b_fc1=b_fc1, w_fc2=w_fc2, b_fc2=b_fc2, final_gain=final_gain, final_shift=final_shift, w_head=w_head, b_head=b_head, cot_latent=cot_latent, cot_logdet=cot_logdet)


EPS = 1e-05
HIGH = lax.Precision.HIGHEST

@jax.custom_vjp
def low(v):
    return lax.optimization_barrier(v.astype(jnp.bfloat16)).astype(jnp.float32)

@jax.custom_vjp
def low_back(v):
    return v

def low_keep(v):
    return (low(v), None)

def low_pass(kept, grad):
    return (grad,)

def back_keep(v):
    return (v, None)

def back_low(kept, grad):
    return (low(grad),)
low.defvjp(low_keep, low_pass)
low_back.defvjp(back_keep, back_low)

def dense(left, right):
    return jnp.dot(left, right, precision=HIGH, preferred_element_type=jnp.float32)

def layer_norm(hidden, gain, offset):
    center = hidden - lax.optimization_barrier(jnp.mean(hidden, axis=-1, keepdims=True))
    spread = lax.optimization_barrier(jnp.mean(center * center, axis=-1, keepdims=True))
    return center * lax.rsqrt(spread + EPS) * gain + offset

def forward(params, patches, labels, valid_mask):
    w_patch, b_patch, pos_embed, class_embed, gain1, shift1, w_qkv, w_out, gain2, shift2, w_fc1, b_fc1, w_fc2, b_fc2, gainf, shiftf, w_head, b_head = params
    item_count = patches.shape[0]
    scale = 1.0 / math.sqrt(HEAD_DIM)
    shifted = jnp.concatenate([jnp.zeros((item_count, 1, P_SIZE), jnp.float32), patches[:, :-1, :]], axis=1)
    hidden = dense(shifted.reshape(-1, P_SIZE), w_patch).reshape(item_count, S, D)
    hidden = hidden + b_patch + pos_embed[None] + class_embed[labels][:, None, :]
    hidden = hidden.reshape(-1, D)
    normed1 = low(layer_norm(hidden, gain1, shift1))
    qkv = low(low_back(dense(normed1, w_qkv))).reshape(item_count, S, 3, HEADS, HEAD_DIM)
    query = qkv[:, :, 0]
    keys = qkv[:, :, 1]
    values = qkv[:, :, 2]
    scores = low_back(jnp.einsum('bqhd,bkhd->bhqk', query, keys, precision=HIGH) * scale)
    allowed = jnp.arange(S)[None, :] <= jnp.arange(S)[:, None]
    scores = jnp.where(allowed[None, None], scores, -1e+30)
    probs = low(jax.nn.softmax(scores, axis=-1))
    attended = low(low_back(jnp.einsum('bhqk,bkhd->bqhd', probs, values, precision=HIGH))).reshape(-1, D)
    hidden = hidden + low_back(dense(attended, w_out))
    normed2 = low(layer_norm(hidden, gain2, shift2))
    up_values = low_back(dense(normed2, w_fc1) + b_fc1)
    act_values = low(jax.nn.gelu(up_values, approximate=True))
    hidden = hidden + low_back(dense(act_values, w_fc2) + b_fc2)
    normed3 = low(layer_norm(hidden, gainf, shiftf))
    head_out = low_back(dense(normed3, w_head) + b_head).reshape(item_count, S, 2 * P_SIZE)
    shift_part = head_out[..., :P_SIZE]
    log_scale = head_out[..., P_SIZE:]
    valid_f = valid_mask.astype(jnp.float32)[..., None]
    moved = (patches - shift_part) * jnp.exp(-log_scale)
    latent = valid_f * moved + (1.0 - valid_f) * patches
    logdet = -lax.optimization_barrier(jnp.sum(valid_f * log_scale, axis=(1, 2)))
    return ((latent, logdet), log_scale)

def add_pair(first, second):
    return first + second

def reference(patches, labels, valid_mask, class_slot, w_patch, b_patch, pos_embed, class_embed, norm1_gain, norm1_shift, w_qkv, w_out, norm2_gain, norm2_shift, w_fc1, b_fc1, w_fc2, b_fc2, final_gain, final_shift, w_head, b_head, cot_latent, cot_logdet):
    params = tuple((value.astype(jnp.float32) for value in (w_patch, b_patch, pos_embed, class_embed, norm1_gain, norm1_shift, w_qkv, w_out, norm2_gain, norm2_shift, w_fc1, b_fc1, w_fc2, b_fc2, final_gain, final_shift, w_head, b_head)))
    group = 16
    blocks = patches.shape[0] // group

    def cut(value):
        return value.reshape((blocks, group) + value.shape[1:])

    def step(carry, block):
        grads, scale_sum, scale_top = carry
        inputs, block_labels, block_valid, block_cot, block_det = block

        def run(prm, xin):
            return forward(prm, xin, block_labels, block_valid)
        outputs, pull, log_scale = jax.vjp(run, params, inputs, has_aux=True)
        grad_params, grad_in = pull((block_cot, block_det))
        grads = jax.tree.map(add_pair, grads, grad_params)
        valid_f = block_valid.astype(jnp.float32)[..., None]
        scale_sum = scale_sum + jnp.sum(valid_f * log_scale)
        scale_top = jnp.maximum(scale_top, jnp.max(jnp.where(valid_f > 0, log_scale, -1e+30)))
        return ((grads, scale_sum, scale_top), (outputs[0], outputs[1], grad_in))
    init = (jax.tree.map(jnp.zeros_like, params), jnp.zeros((), jnp.float32), jnp.full((), -1e+30, jnp.float32))
    blocks_in = (cut(patches.astype(jnp.float32)), cut(labels), cut(valid_mask), cut(cot_latent.astype(jnp.float32)), cut(cot_logdet.astype(jnp.float32)))
    (grads, scale_sum, scale_top), (latent, logdet, grad_in) = lax.scan(step, init, blocks_in)
    latent = latent.reshape(patches.shape)
    logdet = logdet.reshape(patches.shape[0])
    grad_in = grad_in.reshape(patches.shape)
    count = jnp.sum(valid_mask.astype(jnp.float32)) * P_SIZE
    class_grad = grads[3]
    owned = jnp.zeros_like(class_grad).at[class_slot].set(class_grad)
    return (latent, logdet, grad_in, grads[0], grads[1], grads[2], owned, grads[4], grads[5], grads[6], grads[7], grads[8], grads[9], grads[10], grads[11], grads[12], grads[13], grads[14], grads[15], grads[16], grads[17], scale_sum / count, scale_top)
```

```python
import math

import jax
import jax.numpy as jnp
from jax import lax
from jax.sharding import PartitionSpec as P

HEADS = 12
EPS = 1e-05
bf16 = jnp.bfloat16
f32 = jnp.float32
AXES = ("dp", "seq")


def layer_norm(hidden, gain, offset):
    center = hidden - jnp.mean(hidden, axis=-1, keepdims=True)
    spread = jnp.mean(center * center, axis=-1, keepdims=True)
    return center * lax.rsqrt(spread + EPS) * gain + offset


def gelu_tanh(values):
    return jax.nn.gelu(values, approximate=True)


def dot(left, right, a=1, b=0):
    return lax.dot_general(
        left, right, (((a,), (b,)), ((), ())), preferred_element_type=f32
    )


class Cube:
    def __init__(self):
        self.size = lax.axis_size("dp") * lax.axis_size("seq")
        self.nbits = self.size.bit_length() - 1
        self.me = lax.axis_index("dp") * lax.axis_size("seq") + lax.axis_index("seq")
        self.bit = [(self.me >> k) & 1 for k in range(self.nbits)]

    def send(self, block, mask):
        return lax.ppermute(block, AXES, [(i, i ^ mask) for i in range(self.size)])

    def patterns(self, stage):
        out = []
        for m in range(1 << len(stage)):
            out.append({k: (m >> j) & 1 for j, k in enumerate(stage)})
        return out

    def start(self, full):
        rows = full.shape[0] // self.size
        return full.reshape((2,) * self.nbits + (rows, full.shape[1])), list(
            range(self.nbits - 1, -1, -1)
        )

    def pick(self, block, left, pattern):
        for k, m in pattern.items():
            axis = left.index(k)
            block = lax.dynamic_index_in_dim(block, self.bit[k] ^ m, axis, keepdims=False)
            left = [b for b in left if b != k]
        return block

    def scatter(self, block, left, stages):
        for stage in stages:
            total = None
            for pattern in self.patterns(stage):
                part = self.pick(block, left, pattern)
                mask = sum(m << k for k, m in pattern.items())
                if mask:
                    part = self.send(part.astype(bf16), mask).astype(f32)
                total = part if total is None else total + part
            block, left = total, [b for b in left if b not in stage]
        return block, left

    def add_up(self, block):
        for k in [1, 0] + list(range(2, self.nbits)):
            block = block + self.send(block, 1 << k)
        return block

    def gather(self, block, stages):
        order = []
        for stage in stages:
            parts = []
            for pattern in self.patterns(stage):
                mask = sum(m << k for k, m in pattern.items())
                parts.append(self.send(block, mask) if mask else block)
            block = jnp.stack(parts).reshape((2,) * len(stage) + block.shape)
            order = stage[::-1] + order
        for axis, k in enumerate(order):
            block = jnp.where(self.bit[k] == 1, jnp.flip(block, axis), block)
        want = list(range(self.nbits - 1, -1, -1))
        spots = [order.index(k) for k in want]
        rest = list(range(self.nbits, block.ndim))
        block = block.transpose(spots + rest)
        return block.reshape((self.size,) + block.shape[self.nbits :])


def split3(value):
    high = lax.reduce_precision(value, 8, 7)
    rest = value - high
    mid = lax.reduce_precision(rest, 8, 7)
    return [high, mid, rest - mid]


def local(
    patches, labels, valid_mask, class_slot, w_patch, b_patch, pos_embed, class_embed,
    norm1_gain, norm1_shift, w_qkv, w_out, norm2_gain, norm2_shift, w_fc1, b_fc1, w_fc2, b_fc2,
    final_gain, final_shift, w_head, b_head, cot_latent, cot_logdet,
):
    cube = Cube()
    seq_n = lax.axis_size("seq")
    assert seq_n == 2
    seq = lax.axis_index("seq")
    held, span, feat = patches.shape
    items = held // seq_n
    length = span * seq_n
    width = w_out.shape[0]
    head_dim = width // HEADS
    scale = 1.0 / math.sqrt(head_dim)
    rows = items * length
    classes = class_embed.shape[0]

    first = seq * items
    away = (1 - seq) * items
    packed = jnp.concatenate(
        [
            patches.transpose(0, 2, 1).astype(f32),
            cot_latent.transpose(0, 2, 1),
            jnp.broadcast_to(valid_mask.astype(f32)[:, None], (held, 8, span)),
        ],
        axis=1,
    )
    mine = lax.dynamic_slice_in_dim(packed, first, items, 0)
    came = cube.send(lax.dynamic_slice_in_dim(packed, away, items, 0), 1)
    low_half = jnp.where(seq == 0, mine, came)
    high_half = jnp.where(seq == 0, came, mine)
    whole = jnp.concatenate([low_half, high_half], axis=2).transpose(0, 2, 1)
    inputs = whole[:, :, :feat]
    cot = whole[:, :, feat : 2 * feat]
    valid_f = whole[:, :, 2 * feat : 2 * feat + 1]
    my_labels = lax.dynamic_slice_in_dim(labels, first, items, 0)
    my_det = lax.dynamic_slice_in_dim(cot_logdet, first, items, 0)
    class_rows = jnp.concatenate(
        [lax.dynamic_slice_in_dim(class_embed, my_labels[i], 1, 0) for i in range(items)]
    )
    slots = jnp.stack(
        [lax.dynamic_slice_in_dim(class_slot, my_labels[i], 1, 0)[0] for i in range(items)]
    )

    gain1, shift1 = norm1_gain.astype(f32), norm1_shift.astype(f32)
    gain2, shift2 = norm2_gain.astype(f32), norm2_shift.astype(f32)
    gainf, shiftf = final_gain.astype(f32), final_shift.astype(f32)

    shifted = jnp.concatenate(
        [jnp.zeros((items, 1, feat), f32), inputs[:, :-1]], axis=1
    ).astype(bf16)
    flat_in = shifted.reshape(rows, feat)
    hidden0 = dot(flat_in, w_patch).reshape(items, length, width)
    hidden0 = (
        hidden0
        + b_patch.astype(f32)
        + pos_embed.astype(f32)[None]
        + class_rows.astype(f32)[:, None]
    ).reshape(rows, width)
    normed1 = layer_norm(hidden0, gain1, shift1).astype(bf16)
    qkv = dot(normed1, w_qkv).astype(bf16).reshape(items, length, 3, HEADS, head_dim)
    query, keys, values = qkv[:, :, 0], qkv[:, :, 1], qkv[:, :, 2]
    allowed = jnp.arange(length)[None, :] <= jnp.arange(length)[:, None]
    scores = jnp.einsum("bqhd,bkhd->bhqk", query, keys, preferred_element_type=f32) * scale
    scores = jnp.where(allowed[None, None], scores, -1e30)
    probs = jax.nn.softmax(scores, axis=-1)
    probs_low = probs.astype(bf16)
    attended = (
        jnp.einsum("bhqk,bkhd->bqhd", probs_low, values, preferred_element_type=f32)
        .astype(bf16)
        .reshape(rows, width)
    )
    hidden1 = hidden0 + dot(attended, w_out)
    normed2 = layer_norm(hidden1, gain2, shift2).astype(bf16)
    up_values = dot(normed2, w_fc1) + b_fc1.astype(f32)
    act_values = gelu_tanh(up_values).astype(bf16)
    hidden2 = hidden1 + dot(act_values, w_fc2) + b_fc2.astype(f32)
    normed3 = layer_norm(hidden2, gainf, shiftf).astype(bf16)
    head_out = (dot(normed3, w_head) + b_head.astype(f32)).reshape(items, length, 2 * feat)
    shift_part, log_scale = head_out[..., :feat], head_out[..., feat:]
    inverse = jnp.exp(-log_scale)
    moved = (inputs - shift_part) * inverse
    latent = valid_f * moved + (1.0 - valid_f) * inputs
    logdet = -jnp.sum(valid_f * log_scale, axis=(1, 2))
    scale_count = jnp.sum(valid_f) * feat
    local_top = jnp.max(jnp.where(valid_f > 0, log_scale, -1e30))

    d_moved = valid_f * cot
    d_shift = -d_moved * inverse
    d_scale = -d_moved * moved - valid_f * my_det[:, None, None]
    d_head = jnp.concatenate([d_shift, d_scale], axis=-1).astype(bf16).reshape(rows, 2 * feat)
    grad_b_head = jnp.sum(d_head.astype(f32), axis=0)
    grad_w_head_t = dot(d_head, normed3, 0, 0)
    d_normed3 = dot(d_head, w_head, 1, 1)
    d_hidden2, g_fg, g_fs = jax.vjp(layer_norm, hidden2, gainf, shiftf)[1](d_normed3)
    d_mlp = d_hidden2.astype(bf16)
    g_b2 = jnp.sum(d_mlp.astype(f32), axis=0)
    grad_fc2 = dot(act_values, d_mlp, 0, 0)
    core = [1]
    late = [b for b in range(2, cube.nbits)]
    tail = [late[1:][i : i + 2] for i in range(0, len(late) - 1, 2)]
    singles = [[b] for b in late[1:]]
    own_fc2, _ = cube.scatter(*cube.start(grad_fc2), [core, [0], late[:1]] + singles)
    d_act = dot(d_mlp, w_fc2, 1, 1)
    d_up = jax.vjp(gelu_tanh, up_values)[1](d_act)[0].astype(bf16)
    g_b1 = jnp.sum(d_up.astype(f32), axis=0)
    grad_fc1_t = dot(d_up, normed2, 0, 0)
    own_fc1, _ = cube.scatter(*cube.start(grad_fc1_t), [core, late[:1], [0]] + singles)
    d_normed2 = dot(d_up, w_fc1, 1, 1)
    d_part1, g_n2g, g_n2s = jax.vjp(layer_norm, hidden1, gain2, shift2)[1](d_normed2)
    d_hidden1 = d_hidden2 + d_part1
    d_out = d_hidden1.astype(bf16)
    grad_out = dot(attended, d_out, 0, 0)
    d_attended = dot(d_out, w_out, 1, 1).astype(bf16).reshape(items, length, HEADS, head_dim)
    d_probs = jnp.einsum("bqhd,bkhd->bhqk", d_attended, values, preferred_element_type=f32)
    d_scores = (probs * (d_probs - jnp.sum(probs * d_probs, axis=-1, keepdims=True))).astype(bf16)
    d_query = jnp.einsum("bhqk,bkhd->bqhd", d_scores, keys, preferred_element_type=f32) * scale
    d_keys = jnp.einsum("bhqk,bqhd->bkhd", d_scores, query, preferred_element_type=f32) * scale
    d_values = jnp.einsum("bhqk,bqhd->bkhd", probs_low, d_attended, preferred_element_type=f32)
    d_qkv = jnp.stack([d_query, d_keys, d_values], axis=2).astype(bf16).reshape(rows, 3 * width)
    grad_q = dot(normed1, d_qkv[:, :width], 0, 0)
    grad_k = dot(normed1, d_qkv[:, width : 2 * width], 0, 0)
    grad_v = dot(normed1, d_qkv[:, 2 * width :], 0, 0)
    d_normed1 = dot(d_qkv, w_qkv, 1, 1)
    d_part0, g_n1g, g_n1s = jax.vjp(layer_norm, hidden0, gain1, shift1)[1](d_normed1)
    d_hidden0 = d_hidden1 + d_part0
    d_low = d_hidden0.astype(bf16)
    grad_patch = dot(flat_in, d_low, 0, 0)
    d_items = d_hidden0.reshape(items, length, width)
    pos_local = jnp.sum(d_items, axis=0)
    item_sums = jnp.sum(d_items, axis=1)
    g_bp = jnp.sum(item_sums, axis=0)
    d_shifted = dot(d_low, w_patch, 1, 1).reshape(items, length, feat)
    from_shift = jnp.concatenate([d_shifted[:, 1:], jnp.zeros((items, 1, feat), f32)], axis=1)
    grad_in = cot * (1.0 - valid_f) + d_moved * inverse + from_shift

    vectors = jnp.stack(
        [g_bp, g_n1g, g_n1s, g_n2g, g_n2s, g_b2, g_fg, g_fs]
        + [jnp.pad(grad_b_head, (0, width - 2 * feat))]
    )
    b1_rows = g_b1.reshape(-1, width)
    parts = [grad_q, grad_k, grad_v, grad_out, pos_local, grad_w_head_t, grad_patch]
    short = jnp.concatenate([vectors, b1_rows])
    short = cube.add_up(jnp.pad(short, ((0, -short.shape[0] % 8), (0, 0))))
    starts = [0]
    for part in parts:
        starts.append(starts[-1] + part.shape[0])
    chunk = -(-starts[-1] // (16 * cube.size)) * 16
    bulk = jnp.concatenate(parts + [jnp.zeros((chunk * cube.size - starts[-1], width), f32)])
    block, left = cube.start(bulk)
    half = chunk // 2
    one, left1 = cube.scatter(block[..., :half, :], left, [core, [0], late[:1]])
    two, _ = cube.scatter(block[..., half:, :], left, [core, late[:1], [0]])
    both = jnp.concatenate([one, two], axis=-2)
    own, _ = cube.scatter(both, left1, tail)

    scalars = jnp.concatenate(
        [
            jnp.stack(
                split3(jnp.sum(valid_f * log_scale))
                + split3(scale_count)
                + split3(local_top)
            ),
            (slots // 32).astype(f32),
            (slots % 32).astype(f32),
        ]
    )
    extra = jnp.concatenate(
        [item_sums, jnp.pad(scalars, (0, width - scalars.shape[0]))[None]]
    )
    extra = jnp.pad(extra, ((0, 16 - extra.shape[0]), (0, 0)))
    piece = jnp.concatenate([own, extra]).astype(bf16)
    back_tail = tail[::-1]
    gathered = cube.gather(piece, back_tail + [late[:1], [0], core]).astype(f32)
    full = gathered[:, :chunk].reshape(chunk * cube.size, width)
    got = [full[starts[i] : starts[i + 1]] for i in range(len(parts))]
    sums = gathered[:, chunk : chunk + items].reshape(-1, width)
    facts = gathered[:, chunk + items]
    scale_sum = jnp.sum(facts[:, 0] + facts[:, 1] + facts[:, 2])
    count = jnp.sum(facts[:, 3] + facts[:, 4] + facts[:, 5])
    top = jnp.max(facts[:, 6] + facts[:, 7] + facts[:, 8])
    all_slots = (facts[:, 9 : 9 + items] * 32 + facts[:, 9 + items : 9 + 2 * items]).reshape(-1)
    own_rows = classes // cube.size
    wanted = (cube.me * own_rows + jnp.arange(own_rows)).astype(f32)
    hot = (wanted[:, None] == all_slots[None, :]).astype(bf16)
    class_own = dot(hot, sums.astype(bf16))

    result = jnp.concatenate([latent, grad_in], axis=2).transpose(0, 2, 1)
    dets = jnp.broadcast_to(logdet[:, None, None], (items, 8, length))
    result = jnp.concatenate([result, dets], axis=1)
    keep = lax.dynamic_slice_in_dim(result, seq * span, span, 2)
    came = cube.send(lax.dynamic_slice_in_dim(result, (1 - seq) * span, span, 2), 1)
    out = jnp.where(
        seq == 0, jnp.concatenate([keep, came]), jnp.concatenate([came, keep])
    )
    latent_out = out[:, :feat].transpose(0, 2, 1)
    grad_out_in = out[:, feat : 2 * feat].transpose(0, 2, 1)
    logdet_out = out[:, 2 * feat, 0]
    vec = short[:9]
    ff_rows = own_fc1.shape[0]
    b1_own = lax.dynamic_slice_in_dim(short[9 : 9 + b1_rows.shape[0]].reshape(-1), cube.me * ff_rows, ff_rows, 0)
    return (
        latent_out,
        logdet_out,
        grad_out_in,
        got[6],
        vec[0],
        got[4],
        class_own,
        vec[1],
        vec[2],
        jnp.concatenate(got[:3], axis=1),
        got[3],
        vec[3],
        vec[4],
        own_fc1.T,
        b1_own,
        own_fc2,
        vec[5],
        vec[6],
        vec[7],
        got[5].T,
        vec[8, : 2 * feat],
        scale_sum / count,
        top,
    )


def solution(mesh):
    run, item, whole = P("dp", "seq", None), P("dp"), P()
    placed = (run, item, P("dp", "seq")) + (whole,) * 19 + (run, item)
    owned = P(AXES)
    return jax.shard_map(
        local,
        mesh=mesh,
        in_specs=placed,
        out_specs=(run, item, run, whole, whole, whole, P(AXES, None), whole, whole, whole, whole,
                   whole, whole, P(None, AXES), owned, P(AXES, None)) + (whole,) * 7,
        check_vma=False,
    )
```

```python
import math
from functools import partial

import jax
import jax.numpy as jnp
from jax import lax
from jax.experimental import pallas as pl
from jax.experimental.pallas import tpu as pltpu
from jax.sharding import PartitionSpec as P

HEADS = 12
EPS = 1e-05
GELU_A = math.sqrt(2.0 / math.pi)
GELU_B = 0.044715
bf16 = jnp.bfloat16
f32 = jnp.float32
AXES = ("dp", "seq")
ROW = dict(bp=0, n1g=1, n1s=2, n2g=3, n2s=4, b2=5, fg=6, fs=7, bh=8, b1=9)
VEC = dict(bp=0, n1g=1, n1s=2, n2g=3, n2s=4, b2=5, fg=6, fs=7, b1=8, cls=12)


def dot(left, right, a=1, b=0):
    return lax.dot_general(
        left, right, (((a,), (b,)), ((), ())), preferred_element_type=f32
    )


def call(body, outs, args, name, flops, limit, smem=()):
    specs = [
        pl.BlockSpec(memory_space=pltpu.SMEM if i in smem else pltpu.VMEM) for i in range(len(args))
    ]
    shapes = [jax.ShapeDtypeStruct(s, d) for s, d in outs]
    moved = sum(math.prod(s) * jnp.dtype(d).itemsize for s, d in outs)
    moved += sum(a.size * a.dtype.itemsize for a in args)
    return pl.pallas_call(
        body,
        out_shape=shapes,
        in_specs=specs,
        out_specs=[pl.BlockSpec(memory_space=pltpu.VMEM)] * len(outs),
        compiler_params=pltpu.CompilerParams(vmem_limit_bytes=limit * 2**20),
        cost_estimate=pl.CostEstimate(flops=int(flops), bytes_accessed=int(moved), transcendentals=0),
        name=name,
    )(*args)


def centered(hidden):
    center = hidden - jnp.mean(hidden, axis=-1, keepdims=True)
    spread = jnp.mean(center * center, axis=-1, keepdims=True)
    inverse = lax.rsqrt(spread + EPS)
    return center * inverse, inverse


def norm_pull(grad, unit, inverse, gain):
    scaled = grad * gain
    mean = jnp.mean(scaled, axis=-1, keepdims=True)
    along = jnp.mean(scaled * unit, axis=-1, keepdims=True)
    return inverse * (scaled - mean - unit * along)


def col_sum(values):
    return jnp.sum(values, axis=0, keepdims=True)


def both_halves(seq, own, came):
    low = jnp.where(seq == 0, own, came)
    high = jnp.where(seq == 0, came, own)
    return jnp.concatenate([low, high], axis=1)


def front_kernel(place, runs, came, vecs, pos, w_patch, w_qkv,
                 hidden0, normed1, qkv, shifted_t, attended, lse):
    seq = place[0]
    items = came.shape[0]
    feat = w_patch.shape[0]
    length = pos.shape[0]
    width = pos.shape[1]
    for i in range(items):
        rows = slice(i * length, (i + 1) * length)
        own = runs[seq * items + i].astype(f32)
        whole = both_halves(seq, own, came[i, :feat])
        lane = lax.broadcasted_iota(jnp.int32, whole.shape, 1)
        moved = jnp.where(lane == 0, 0.0, pltpu.roll(whole, 1, 1)).astype(bf16)
        shifted_t[:, rows] = moved
        base = vecs[VEC["bp"] : VEC["bp"] + 1] + vecs[VEC["cls"] + i : VEC["cls"] + i + 1]
        h0 = dot(moved, w_patch[...], 0, 0) + base + pos[...].astype(f32)
        hidden0[rows, :] = h0
        unit, _ = centered(h0)
        normed1[rows, :] = (
            unit * vecs[VEC["n1g"] : VEC["n1g"] + 1] + vecs[VEC["n1s"] : VEC["n1s"] + 1]
        ).astype(bf16)
    for j in range(3):
        cols = slice(j * width, (j + 1) * width)
        qkv[:, cols] = dot(normed1[...], w_qkv[:, cols]).astype(bf16)
    pairs = HEADS // 2
    key_at = lax.broadcasted_iota(jnp.int32, (length, length), 0)
    query_at = lax.broadcasted_iota(jnp.int32, (length, length), 1)
    allowed = key_at <= query_at

    def step(p, carry):
        for i in range(items):
            rows = slice(i * length, (i + 1) * length)
            col = pl.multiple_of(p * 128, 128)
            q = qkv[rows, pl.ds(col, 128)]
            k = qkv[rows, pl.ds(pl.multiple_of(width + p * 128, 128), 128)]
            v = qkv[rows, pl.ds(pl.multiple_of(2 * width + p * 128, 128), 128)]
            first = lax.broadcasted_iota(jnp.int32, q.shape, 1) < 64
            v_t = v.T
            outs = []
            for h in range(2):
                mine = first if h == 0 else ~first
                qh = jnp.where(mine, q * 0.125, jnp.zeros_like(q))
                s = jnp.where(allowed, dot(k, qh, 1, 1), -1e30)
                top = jnp.max(s, axis=0, keepdims=True)
                e = jnp.exp(s - top)
                total = jnp.sum(e, axis=0, keepdims=True)
                lse[i, pl.ds(p * 2 + h, 1), :] = top + jnp.log(total)
                probs = (e * (1.0 / total)).astype(bf16)
                outs.append(dot(v_t[h * 64 : (h + 1) * 64], probs))
            attended[rows, pl.ds(col, 128)] = jnp.concatenate(outs, axis=0).T.astype(bf16)
        return carry

    lax.fori_loop(0, pairs, step, 0)


def middle_kernel(place, det, hidden0, attended, w_out, vecs, w_fc1, w_fc2, w_head_t, b_head,
                  runs, cot_runs, valid_runs, came,
                  hidden1, normed2, act, slope, d_hidden2, part_in, lat_keep, lat_send,
                  short, grad_head_t, facts):
    seq = place[0]
    items = came.shape[0]
    feat = runs.shape[1]
    width = w_out.shape[0]
    span = came.shape[2]
    length = 2 * span

    def vec(name, k=0):
        return vecs[VEC[name] + k : VEC[name] + k + 1]

    hidden1[...] = hidden0[...] + dot(attended[...], w_out[...])
    for i in range(items):
        rows = slice(i * length, (i + 1) * length)
        unit, _ = centered(hidden1[rows, :])
        normed2[rows, :] = (unit * vec("n2g") + vec("n2s")).astype(bf16)
    total = None
    for j in range(w_fc1.shape[1] // width):
        cols = slice(j * width, (j + 1) * width)
        up = dot(normed2[...], w_fc1[:, cols]) + vec("b1", j)
        square = up * up
        half = 0.5 * jnp.tanh(up * (GELU_A + GELU_A * GELU_B * square)) + 0.5
        value = up * half
        act[:, cols] = value.astype(bf16)
        slope[:, cols] = (
            half + 2.0 * value * (1.0 - half) * (GELU_A + 3.0 * GELU_A * GELU_B * square)
        ).astype(bf16)
        part = dot(act[:, cols], w_fc2[cols, :])
        total = part if total is None else total + part
    hidden2 = hidden1[...] + total + vec("b2")
    unit, inverse_dev = centered(hidden2)
    normed3 = (unit * vec("fg") + vec("fs")).astype(bf16)
    head = dot(w_head_t[...], normed3, 1, 1) + b_head[...]
    short[...] = jnp.zeros(short.shape, f32)
    d_heads = []
    sums = [jnp.zeros((1, 1), f32), jnp.zeros((1, 1), f32), jnp.full((1, 1), -1e30, f32)]
    for i in range(items):
        cols = slice(i * length, (i + 1) * length)
        source = seq * items + i
        x = both_halves(seq, runs[source].astype(f32), came[i, :feat])
        cot = both_halves(seq, cot_runs[source], came[i, feat : 2 * feat])
        valid = both_halves(
            seq, valid_runs[source].astype(f32), came[i, 2 * feat : 2 * feat + 1]
        )
        shift_part = head[:feat, cols]
        log_scale = head[feat:, cols]
        inverse = jnp.exp(-log_scale)
        moved = (x - shift_part) * inverse
        latent = valid * moved + (1.0 - valid) * x
        d_moved = valid * cot
        d_heads.append(
            jnp.concatenate(
                [-d_moved * inverse, -d_moved * moved - valid * det[source]], axis=0
            ).astype(bf16)
        )
        part_in[:, cols] = cot * (1.0 - valid) + d_moved * inverse
        counted = valid * log_scale
        item_sum = jnp.sum(jnp.sum(counted, axis=1, keepdims=True), axis=0, keepdims=True)
        sums[0] = sums[0] + item_sum
        sums[1] = sums[1] + jnp.sum(valid, axis=1, keepdims=True) * feat
        tops = jnp.where(valid > 0, log_scale, -1e30)
        tops = jnp.max(jnp.max(tops, axis=1, keepdims=True), axis=0, keepdims=True)
        sums[2] = jnp.maximum(sums[2], tops)
        low, high = latent[:, :span], latent[:, span:]
        logdet = jnp.broadcast_to(-item_sum, (8, span))
        lat_keep[i, :feat] = jnp.where(seq == 0, low, high)
        lat_send[i, :feat] = jnp.where(seq == 0, high, low)
        lat_keep[i, feat:] = logdet
        lat_send[i, feat:] = logdet
    lane = lax.broadcasted_iota(jnp.int32, facts.shape, 1)
    row = jnp.zeros(facts.shape, f32)
    for k, value in enumerate(sums):
        for j in range(3):
            piece = value.astype(bf16).astype(f32)
            value = value - piece
            row = jnp.where(lane == 3 * k + j, piece, row)
    for i in range(items):
        slot = place[8 + i]
        row = jnp.where(lane == 9 + i, (slot // 32).astype(f32), row)
        row = jnp.where(lane == 9 + items + i, (slot % 32).astype(f32), row)
    facts[...] = row
    d_head = jnp.concatenate(d_heads, axis=1)
    grad_head_t[...] = dot(d_head, normed3)
    short[ROW["bh"] : ROW["bh"] + 1, : 2 * feat] = dot(
        jnp.ones((8, d_head.shape[1]), bf16), d_head, 1, 1
    )[:1]
    d_normed3 = dot(d_head, w_head_t[...], 0, 0)
    short[ROW["fg"] : ROW["fg"] + 1, :] = col_sum(d_normed3 * unit)
    short[ROW["fs"] : ROW["fs"] + 1, :] = col_sum(d_normed3)
    pulled = norm_pull(d_normed3, unit, inverse_dev, vec("fg"))
    d_hidden2[...] = pulled
    short[ROW["b2"] : ROW["b2"] + 1, :] = col_sum(pulled.astype(bf16).astype(f32))


def split_by(bit, block, keep, send, half):
    low, high = block[:half], block[half:]
    keep[...] = jnp.where(bit == 0, low, high).astype(keep.dtype)
    send[...] = jnp.where(bit == 0, high, low).astype(send.dtype)


def fc2_kernel(place, act, d_hidden2, keep, send):
    group = keep.shape[1]
    d_mlp = d_hidden2[...].astype(bf16)
    step = 384
    per = step // (2 * group)
    for j in range(act.shape[1] // step):
        block = dot(act[:, j * step : (j + 1) * step], d_mlp, 0, 0)
        for k in range(per):
            n = j * per + k
            split_by(place[1], block[2 * group * k : 2 * group * (k + 1)], keep.at[n], send.at[n], group)


def back_kernel(place, d_hidden2, w_fc2, slope, normed2, w_fc1, hidden1, vecs, attended, w_out,
                short_in, grad_head_t,
                keep, send, d_hidden1, short, out_keep, out_send, d_attended):
    group = keep.shape[1]
    width = w_out.shape[0]
    step = 384
    per = step // (2 * group)
    d_mlp = d_hidden2[...].astype(bf16)
    short[...] = short_in[...]
    gain = vecs[VEC["n2g"] : VEC["n2g"] + 1]
    total = None
    for j in range(w_fc1.shape[1] // width):
        cols = slice(j * width, (j + 1) * width)
        d_up = (dot(d_mlp, w_fc2[cols, :], 1, 1) * slope[:, cols].astype(f32)).astype(bf16)
        short[ROW["b1"] + j : ROW["b1"] + j + 1, :] = col_sum(d_up.astype(f32))
        for m in range(width // step):
            block = dot(d_up[:, m * step : (m + 1) * step], normed2[...], 0, 0)
            for k in range(per):
                n = (j * (width // step) + m) * per + k
                split_by(place[1], block[2 * group * k : 2 * group * (k + 1)], keep.at[n], send.at[n], group)
        part = dot(d_up, w_fc1[:, cols], 1, 1)
        total = part if total is None else total + part
    unit, inverse_dev = centered(hidden1[...])
    short[ROW["n2g"] : ROW["n2g"] + 1, :] = col_sum(total * unit)
    short[ROW["n2s"] : ROW["n2s"] + 1, :] = col_sum(total)
    h1 = d_hidden2[...] + norm_pull(total, unit, inverse_dev, gain)
    d_hidden1[...] = h1
    d_out = h1.astype(bf16)
    grad_out = dot(attended[...], d_out, 0, 0)
    half = out_keep.shape[0]
    rest = 2 * half - grad_out.shape[0] - grad_head_t.shape[0]
    block = jnp.concatenate([grad_out, grad_head_t[...], jnp.zeros((rest, width), f32)], axis=0)
    split_by(place[1], block, out_keep, out_send, half)
    d_attended[...] = dot(d_out, w_out[...], 1, 1).astype(bf16)


def attention_back_kernel(qkv, lse, d_attended, d_qkv):
    rows_all, width = d_attended.shape
    items = lse.shape[0]
    length = rows_all // items
    key_at = lax.broadcasted_iota(jnp.int32, (length, length), 0)
    query_at = lax.broadcasted_iota(jnp.int32, (length, length), 1)
    allowed = key_at <= query_at

    def step(p, carry):
        for i in range(items):
            rows = slice(i * length, (i + 1) * length)
            at = [pl.ds(pl.multiple_of(j * width + p * 128, 128), 128) for j in range(3)]
            q, k, v = (qkv[rows, at[j]] for j in range(3))
            q = q * 0.125
            d_o = d_attended[rows, at[0]]
            first = lax.broadcasted_iota(jnp.int32, q.shape, 1) < 64
            none = jnp.zeros_like(q)
            total = [None, None, None]
            for h in range(2):
                mine = first if h == 0 else ~first
                qh = jnp.where(mine, q, none)
                kh = jnp.where(mine, k * 0.125, none)
                dh = jnp.where(mine, d_o, none)
                s = jnp.where(allowed, dot(k, qh, 1, 1), -1e30)
                probs = jnp.exp(s - lse[i, pl.ds(p * 2 + h, 1), :])
                d_probs = dot(v, dh, 1, 1)
                delta = jnp.sum(probs * d_probs, axis=0, keepdims=True)
                d_s = (probs * (d_probs - delta)).astype(bf16)
                parts = [dot(d_s, kh, 0, 0), dot(d_s, qh), dot(probs.astype(bf16), dh)]
                total = [b if a is None else a + b for a, b in zip(total, parts)]
            for j in range(3):
                d_qkv[rows, at[j]] = total[j].astype(bf16)
        return carry

    lax.fori_loop(0, HEADS // 2, step, 0)


def qkv_kernel(place, normed1, d_qkv, keep, send):
    width = normed1.shape[1]
    half = keep.shape[0]
    core = place[1]
    step = 384
    for j in range(3):
        for m in range(width // step):
            block = dot(normed1[:, m * step : (m + 1) * step], d_qkv[:, j * width : (j + 1) * width], 0, 0)
            at = j * width + m * step
            inside = at % half

            @pl.when(core == at // half)
            def _():
                keep[inside : inside + step, :] = block

            @pl.when(core != at // half)
            def _():
                send[inside : inside + step, :] = block.astype(bf16)


def rest_kernel(place, d_qkv, w_qkv, hidden0, d_hidden1, vecs, shifted_t, w_patch, part_in, short_in, facts,
                keep, send, short, in_keep, in_send, extra):
    seq = place[0]
    width = hidden0.shape[1]
    items, feat, span = in_keep.shape
    length = 2 * span
    d_normed1 = dot(d_qkv[...], w_qkv[...], 1, 1)
    unit, inverse_dev = centered(hidden0[...])
    short[...] = short_in[...]
    short[ROW["n1g"] : ROW["n1g"] + 1, :] = col_sum(d_normed1 * unit)
    short[ROW["n1s"] : ROW["n1s"] + 1, :] = col_sum(d_normed1)
    d0 = d_hidden1[...] + norm_pull(d_normed1, unit, inverse_dev, vecs[VEC["n1g"] : VEC["n1g"] + 1])
    d_low = d0.astype(bf16)
    extra[...] = jnp.zeros(extra.shape, bf16)
    d_pos, whole = None, None
    for i in range(items):
        mine = d0[i * length : (i + 1) * length]
        d_pos = mine if d_pos is None else d_pos + mine
        item = col_sum(mine)
        whole = item if whole is None else whole + item
        extra[i : i + 1, :] = item.astype(bf16)
    extra[items : items + 1, :] = facts[...].astype(bf16)
    short[ROW["bp"] : ROW["bp"] + 1, :] = whole
    d_patch = dot(shifted_t[...], d_low)
    half = keep.shape[0]
    rest = 2 * half - d_pos.shape[0] - d_patch.shape[0]
    block = jnp.concatenate([d_pos, d_patch, jnp.zeros((rest, width), f32)], axis=0)
    split_by(place[1], block, keep, send.at[:half], half)
    short[...] = put_short(send, half, short[...])
    d_shift = dot(w_patch[...], d_low, 1, 1)
    for i in range(items):
        cols = slice(i * length, (i + 1) * length)
        moved = d_shift[:, cols]
        lane = lax.broadcasted_iota(jnp.int32, moved.shape, 1)
        back = jnp.where(lane == length - 1, 0.0, pltpu.roll(moved, length - 1, 1))
        grad = part_in[:, cols] + back
        in_keep[i] = jnp.where(seq == 0, grad[:, :span], grad[:, span:])
        in_send[i] = jnp.where(seq == 0, grad[:, span:], grad[:, :span])


def put_short(send, at, short):
    n = short.shape[0]
    high = short.astype(bf16)
    low = (short - high.astype(f32)).astype(bf16)
    send[at : at + n, :] = high
    send[at + n : at + 2 * n, :] = low
    return high.astype(f32) + low.astype(f32)


def take_short(came, at, n):
    return came[at : at + n, :].astype(f32) + came[at + n : at + 2 * n, :].astype(f32)


def add_split_kernel(bits, place, *refs):
    n = len(bits)
    for t, bit in enumerate(bits):
        keep, came, kept, send = refs[t], refs[n + t], refs[2 * n + t], refs[3 * n + t]
        mine = place[1 + bit - 1] if bit else place[0]
        for a in range(keep.shape[0]):
            kept[a] = keep[a, mine] + came[a, mine].astype(f32)
            send[a] = (keep[a, 1 - mine] + came[a, 1 - mine].astype(f32)).astype(bf16)


def add_split(place, bits, keeps, cames, name):
    outs = []
    for keep in keeps:
        a, _, b, w = keep.shape
        outs.append(((a, b, w), f32))
    for keep in keeps:
        a, _, b, w = keep.shape
        outs.append(((a, b, w), bf16))
    got = call(
        partial(add_split_kernel, bits), outs, [place] + list(keeps) + list(cames), name, 1e6, 4, smem=(0,)
    )
    return got[: len(keeps)], got[len(keeps) :]


def add_kernel(keep, came, out):
    out[...] = keep[...] + came[...].astype(f32)


def bulk0_kernel(place, qk, qc, ek, ec, lk, lc, short_in, keep_a, keep_b, send_a, send_b, short):
    x, y = place[0], place[2]
    na, nb = keep_a.shape[0], keep_b.shape[0]
    nq, ne, nl = qk.shape[0], ek.shape[0], lk.shape[0]
    ns = short.shape[0]
    total = short_in[...] + take_short(lc, nl, ns)
    mine, away = pl.ds(pl.multiple_of(x * na, na), na), pl.ds(pl.multiple_of((1 - x) * na, na), na)
    keep_a[...] = qk[mine, :] + qc[mine, :].astype(f32)
    send_a[...] = (qk[away, :] + qc[away, :].astype(f32)).astype(bf16)
    low = 2 * na
    parts = [
        qk[low:nq, :] + qc[low:nq, :].astype(f32),
        ek[...] + ec[...].astype(f32),
        lk[...] + lc[:nl, :].astype(f32),
    ]
    block = jnp.concatenate(parts, axis=0)
    split_by(y, block, keep_b, send_b.at[:nb], nb)
    short[...] = put_short(send_b, nb, total)


def bulk1_kernel(place, ka, ca, kb, cb, short_in, keep_a, keep_b, send_a, send_b, short):
    x, y = place[0], place[2]
    na, nb = keep_a.shape[0], keep_b.shape[0]
    ns = short.shape[0]
    total = short_in[...] + take_short(cb, 2 * nb, ns)
    for bit, n, k, c, keep, send in ((y, na, ka, ca, keep_a, send_a), (x, nb, kb, cb, keep_b, send_b)):
        mine, away = pl.ds(pl.multiple_of(bit * n, n), n), pl.ds(pl.multiple_of((1 - bit) * n, n), n)
        keep[...] = k[mine, :] + c[mine, :].astype(f32)
        send[:n, :] = (k[away, :] + c[away, :].astype(f32)).astype(bf16)
    short[...] = put_short(send_b, nb, total)


def bulk2_kernel(place, ka, ca, kb, cb, short_in, keep, send1, send2, send3, short):
    z = place[3] + 2 * place[4]
    na, nb = ka.shape[0] // 4, kb.shape[0] // 4
    ns = short.shape[0]
    total = short_in[...] + take_short(cb, 4 * nb, ns)
    for m, out in enumerate((keep, send1, send2, send3)):
        at = z ^ m
        ra = pl.ds(pl.multiple_of(at * na, na), na)
        rb = pl.ds(pl.multiple_of(at * nb, nb), nb)
        out[:na, :] = (ka[ra, :] + ca[ra, :].astype(f32)).astype(out.dtype)
        out[na : na + nb, :] = (kb[rb, :] + cb[rb, :].astype(f32)).astype(out.dtype)
        if m:
            short[...] = put_short(out, na + nb, total)


def bulk3_kernel(keep, c1, c2, c3, short_in, extra, piece, short):
    n = keep.shape[0]
    ns = short.shape[0]
    total = keep[...]
    for c in (c1, c2, c3):
        total = total + c[:n, :].astype(f32)
    piece[:n, :] = total.astype(bf16)
    piece[n:, :] = extra[...]
    short[...] = (short_in[...] + take_short(c1, n, ns)) + (take_short(c2, n, ns) + take_short(c3, n, ns))


def join0_kernel(place, own, c1, c2, c3, part_a, part_b):
    z = place[3] + 2 * place[4]
    na, nb = part_a.shape[0] // 4, part_b.shape[0] // 4
    for m, c in enumerate((own, c1, c2, c3)):
        at = z ^ m
        part_a[pl.ds(pl.multiple_of(at * na, na), na), :] = c[:na, :]
        part_b[pl.ds(pl.multiple_of(at * nb, nb), nb), :] = c[na:, :]


def join1_kernel(place, own_a, came_a, own_b, came_b, part_a, part_b):
    x, y = place[0], place[2]
    n = own_a.shape[0]
    for bit, own, came, part in ((y, own_a, came_a, part_a), (x, own_b, came_b, part_b)):
        part[pl.ds(pl.multiple_of(bit * n, n), n), :] = own[...]
        part[pl.ds(pl.multiple_of((1 - bit) * n, n), n), :] = came[...]


def last_kernel(geo, place, *refs):
    quarters = refs[:8]
    g_qkv, g_out, g_pos, g_head, g_patch, extras, full = refs[8:]
    x, core, y = place[0], place[1], place[2]
    nb, ne = geo["nb"], geo["extra"]
    n = quarters[0].shape[0]
    for c in range(2):
        which = core if c == 0 else 1 - core
        for t, (bit, other) in enumerate(((x, 1 - x), (y, 1 - y))):
            own, came = quarters[4 * c + 2 * t], quarters[4 * c + 2 * t + 1]
            full[which, t, bit] = own[...]
            full[which, t, other] = came[...]
    width = g_out.shape[0]
    na = 2 * n

    def rows_b(c):
        out = []
        for k in range(2):
            for j in range(8):
                block = full[c, 1, k, j * (nb + ne) : (j + 1) * (nb + ne), :]
                out.append(block[:nb])
                extras[c, k * 8 + j] = block[nb:]
        return jnp.concatenate(out, axis=0)

    flat_b = [rows_b(c) for c in range(2)]
    half_q = geo["half_q"]
    left = half_q - na
    for c in range(2):
        for at in range(0, half_q, 128):
            q = c * half_q + at
            third, row = q // width, q % width
            if at < na:
                block = full[c, 0, at // n, at % n : at % n + 128, :]
            else:
                block = flat_b[c][at - na : at - na + 128]
            g_qkv[row : row + 128, third * width : (third + 1) * width] = block.astype(f32)
    half_e, half_l = geo["half_e"], geo["half_l"]
    early = [flat_b[c][left : left + half_e].astype(f32) for c in range(2)]
    later = [flat_b[c][left + half_e : left + half_e + half_l].astype(f32) for c in range(2)]
    g_out[:half_e, :] = early[0]
    g_out[half_e:, :] = early[1][: width - half_e]
    g_head[...] = early[1][width - half_e : width - half_e + g_head.shape[0]]
    length, feat = g_pos.shape[0], g_patch.shape[0]
    g_pos[:half_l, :] = later[0]
    g_pos[half_l:, :] = later[1][: length - half_l]
    g_patch[...] = later[1][length - half_l : length - half_l + feat]


class Cube:
    def __init__(self):
        self.size = lax.axis_size("dp") * lax.axis_size("seq")
        self.nbits = self.size.bit_length() - 1
        self.me = lax.axis_index("dp") * lax.axis_size("seq") + lax.axis_index("seq")
        self.bit = [(self.me >> k) & 1 for k in range(self.nbits)]

    def send(self, block, mask):
        return lax.ppermute(block, AXES, [(i, i ^ mask) for i in range(self.size)])

    def start(self, full, bits):
        rows = full.shape[0] >> len(bits)
        return full.reshape((2,) * len(bits) + (rows, full.shape[1])), list(bits)

    def scatter(self, block, left):
        for bit in list(left):
            axis = left.index(bit)
            mine = lax.dynamic_index_in_dim(block, self.bit[bit], axis, keepdims=False)
            away = lax.dynamic_index_in_dim(block, 1 - self.bit[bit], axis, keepdims=False)
            block = mine + self.send(away.astype(bf16), 1 << bit).astype(f32)
            left = [b for b in left if b != bit]
        return block

    def add_up(self, block, bits):
        for k in bits:
            block = block + self.send(block, 1 << k)
        return block

    def gather(self, block, bits):
        for k in reversed(bits):
            came = self.send(block, 1 << k)
            block = jnp.where(self.bit[k] == 0, jnp.stack([block, came]), jnp.stack([came, block]))
        return block


def tie(value, *others):
    return lax.optimization_barrier((value,) + others)[0]


def local(
    patches, labels, valid_mask, class_slot, w_patch, b_patch, pos_embed, class_embed,
    norm1_gain, norm1_shift, w_qkv, w_out, norm2_gain, norm2_shift, w_fc1, b_fc1, w_fc2, b_fc2,
    final_gain, final_shift, w_head, b_head, cot_latent, cot_logdet,
):
    cube = Cube()
    seq_n = lax.axis_size("seq")
    assert seq_n == 2
    seq = lax.axis_index("seq")
    held, span, feat = patches.shape
    items = held // seq_n
    length = span * seq_n
    width = w_out.shape[0]
    ff = w_fc1.shape[1]
    rows = items * length
    classes = class_embed.shape[0]
    chunk = ff // cube.size
    group = 2 * chunk
    fast = cube.size == 32

    runs = patches.transpose(0, 2, 1)
    cot_runs = cot_latent.transpose(0, 2, 1)
    first = seq * items
    away = (1 - seq) * items
    packed = jnp.concatenate(
        [
            lax.dynamic_slice_in_dim(runs, away, items, 0).astype(f32),
            lax.dynamic_slice_in_dim(cot_runs, away, items, 0),
            jnp.broadcast_to(
                lax.dynamic_slice_in_dim(valid_mask, away, items, 0).astype(f32)[:, None],
                (items, 8, span),
            ),
        ],
        axis=1,
    )
    came = cube.send(packed, 1)
    my_labels = [lax.dynamic_index_in_dim(labels, first + i, 0, keepdims=False) for i in range(items)]
    slots = [lax.dynamic_index_in_dim(class_slot, at, 0, keepdims=False) for at in my_labels]
    bits = (cube.bit + [0] * 8)[:8]
    place = jnp.stack([jnp.asarray(v, jnp.int32) for v in bits + slots])
    vectors = [b_patch, norm1_gain, norm1_shift, norm2_gain, norm2_shift, b_fc2, final_gain, final_shift]
    vecs = jnp.concatenate(
        [v[None] for v in vectors]
        + [b_fc1.reshape(-1, width)]
        + [lax.dynamic_slice_in_dim(class_embed, at, 1, 0) for at in my_labels]
    )
    vecs = jnp.pad(vecs.astype(f32), ((0, -vecs.shape[0] % 8), (0, 0)))
    w_head_t = w_head.T
    b_head_col = b_head.astype(f32)[:, None]
    valid_runs = valid_mask[:, None, :]

    big = 2.0 * rows * width * ff
    hidden0, normed1, qkv, shifted_t, attended, lse = call(
        front_kernel,
        [((rows, width), f32), ((rows, width), bf16), ((rows, 3 * width), bf16), ((feat, rows), bf16),
         ((rows, width), bf16), ((items, HEADS, length), f32)],
        [place, runs, came, vecs, pos_embed, w_patch, w_qkv],
        "front", big, 16, smem=(0,),
    )
    n_short = 16
    (hidden1, normed2, act, slope, d_hidden2, part_in, lat_keep, lat_send, short, grad_head_t, facts) = call(
        middle_kernel,
        [((rows, width), f32), ((rows, width), bf16), ((rows, ff), bf16), ((rows, ff), bf16),
         ((rows, width), f32), ((feat, rows), f32), ((items, feat + 8, span), f32),
         ((items, feat + 8, span), f32), ((n_short, width), f32), ((2 * feat, width), f32),
         ((1, width), f32)],
        [place, cot_logdet, hidden0, attended, w_out, vecs, w_fc1, w_fc2, w_head_t, b_head_col,
         runs, cot_runs, valid_runs, came],
        "middle", 2.5 * big, 24, smem=(0, 1),
    )
    groups = ff // (2 * group)
    keep2, send2 = call(
        fc2_kernel, [((groups, group, width), f32), ((groups, group, width), bf16)],
        [place, act, d_hidden2], "fc2", big, 12, smem=(0,),
    )
    came2 = cube.send(send2, 2)
    half_e, half_l, half_q = 448, 192, 3 * width // 2
    keep1, send1, d_hidden1, short, ekeep, esend, d_attended = call(
        back_kernel,
        [((groups, group, width), f32), ((groups, group, width), bf16), ((rows, width), f32),
         ((n_short, width), f32), ((half_e, width), f32), ((half_e, width), bf16), ((rows, width), bf16)],
        [place, d_hidden2, w_fc2, slope, normed2, w_fc1, hidden1, vecs, attended, w_out, short, grad_head_t],
        "back", 3.5 * big, 24, smem=(0,),
    )
    came1 = cube.send(send1, 2)
    ecame = cube.send(esend, 2)
    if fast:
        (k2,), (s2,) = add_split(
            place, (0,), [keep2.reshape(8, 2, chunk, width)], [came2.reshape(8, 2, chunk, width)], "fc2_core"
        )
        c2 = cube.send(s2, 1)
        d_attended = tie(d_attended, s2)
    (d_qkv,) = call(
        attention_back_kernel, [((rows, 3 * width), bf16)], [qkv, lse, d_attended],
        "attention_back", big, 16,
    )
    qkeep, qsend = call(
        qkv_kernel, [((half_q, width), f32), ((half_q, width), bf16)], [place, normed1, d_qkv],
        "qkv_grad", 0.75 * big, 12, smem=(0,),
    )
    qcame = cube.send(qsend, 2)
    if fast:
        (k1,), (s1,) = add_split(
            place, (2,), [keep1.reshape(4, 2, group, width)], [came1.reshape(4, 2, group, width)], "fc1_core"
        )
        c1 = cube.send(s1, 4)
    lkeep, lsend, short, in_keep, in_send, extra = call(
        rest_kernel,
        [((half_l, width), f32), ((half_l + 2 * n_short, width), bf16), ((n_short, width), f32),
         ((items, feat, span), f32), ((items, feat, span), f32), ((16, width), bf16)],
        [place, d_qkv, w_qkv, hidden0, d_hidden1, vecs, shifted_t, w_patch, part_in, short, facts],
        "rest", 0.9 * big, 16, smem=(0,),
    )
    lcame = cube.send(lsend, 2)

    back_send = jnp.concatenate([lat_send, in_send], axis=1)
    back_keep = jnp.concatenate([lat_keep, in_keep], axis=1)
    back_came = cube.send(back_send, 1)

    if fast:
        na, nb = 512, 384
        ns2 = 2 * n_short
        ka, kb, sa, sb, short = call(
            bulk0_kernel,
            [((na, width), f32), ((nb, width), f32), ((na, width), bf16), ((nb + ns2, width), bf16),
             ((n_short, width), f32)],
            [place, qkeep, qcame, ekeep, ecame, lkeep, lcame, short], "bulk0", 1e6, 8, smem=(0,),
        )
        ca, cb = cube.send(sa, 1), cube.send(sb, 4)
        na, nb = 256, 192
        ka, kb, sa, sb, short = call(
            bulk1_kernel,
            [((na, width), f32), ((nb, width), f32), ((na, width), bf16), ((nb + ns2, width), bf16),
             ((n_short, width), f32)],
            [place, ka, ca, kb, cb, short], "bulk1", 1e6, 6, smem=(0,),
        )
        ca, cb = cube.send(sa, 4), cube.send(sb, 1)
        na, nb = 64, 48
        n = na + nb
        keep, z1, z2, z3, short = call(
            bulk2_kernel,
            [((n, width), f32)] + [((n + ns2, width), bf16)] * 3 + [((n_short, width), f32)],
            [place, ka, ca, kb, cb, short], "bulk2", 1e6, 6, smem=(0,),
        )
        z1, z2, z3 = cube.send(z1, 8), cube.send(z2, 16), cube.send(z3, 24)
        (k2, k1), (s2, s1) = add_split(
            place, (2, 0),
            [k2.reshape(4, 2, chunk, width), k1.reshape(4, 2, chunk, width)],
            [c2.reshape(4, 2, chunk, width), c1.reshape(4, 2, chunk, width)], "fc_second",
        )
        c2, c1 = cube.send(s2, 4), cube.send(s1, 1)
        piece, short = call(
            bulk3_kernel, [((n + 16, width), bf16), ((n_short, width), f32)],
            [keep, z1, z2, z3, short, extra], "bulk3", 1e6, 4,
        )
        g1, g2, g3 = cube.send(piece, 8), cube.send(piece, 16), cube.send(piece, 24)
        (kf,), (sf,) = add_split_pair(place, 3, k2, k1, c2, c1, "fc_third")
        cf = cube.send(sf, 8)
        part_a, part_b = call(
            join0_kernel, [((4 * na, width), bf16), ((4 * (nb + 16), width), bf16)],
            [place, piece, g1, g2, g3], "join0", 1e6, 4, smem=(0,),
        )
        ca, cb = cube.send(part_a, 4), cube.send(part_b, 1)
        part_a, part_b = call(
            join1_kernel, [((8 * na, width), bf16), ((8 * (nb + 16), width), bf16)],
            [place, part_a, ca, part_b, cb], "join1", 1e6, 4, smem=(0,),
        )
        (kf,), (sf,) = add_split(
            place, (4,), [kf.reshape(1, 2, 2 * chunk, width)], [cf.reshape(1, 2, 2 * chunk, width)], "fc_fourth"
        )
        cf = cube.send(sf, 16)
        ca, cb = cube.send(part_a, 1), cube.send(part_b, 4)
        quarters = [part_a, ca, part_b, cb]
        quarters = quarters + [cube.send(q, 2) for q in quarters]
        geo = dict(nb=nb, extra=16, half_q=half_q, half_e=half_e, half_l=half_l)
        g_qkv, g_out, g_pos, g_head_t, g_patch, extras = last_call(
            geo, place, quarters, width, length, feat
        )
        (own,) = call(add_kernel, [((1, 2 * chunk, width), f32)], [kf, cf], "fc_last", 1e6, 4)
        own_fc2, own_fc1 = own[0, :chunk], own[0, chunk:]
        extras = extras.reshape(2, 2, 2, 4, 16, width)[:, :, :, :, : items + 1]
        extras = extras.transpose(3, 1, 0, 2, 4, 5).reshape(cube.size, items + 1, width).astype(f32)
    else:
        rest = [0] + list(range(2, cube.nbits))
        upper = list(range(cube.nbits - 1, 1, -1)) + [0]

        def owned(keep, came):
            total = (keep + came.astype(f32)).reshape(-1, width)
            return cube.scatter(*cube.start(total, upper))

        own_fc2, own_fc1 = owned(keep2, came2), owned(keep1, came1)
        full = jnp.concatenate(
            [qkeep + qcame.astype(f32), ekeep + ecame.astype(f32), lkeep + lcame[:half_l].astype(f32)]
        )
        n_full = full.shape[0]
        full = jnp.pad(full, ((0, -n_full % (cube.size * 8)), (0, 0)))
        own = cube.scatter(*cube.start(full, upper))
        n_own = own.shape[0]
        got = cube.gather(jnp.concatenate([own.astype(bf16), extra]), [1] + upper)
        halves = got[..., :n_own, :].reshape(2, -1, width)[:, :n_full].astype(f32)
        short = cube.add_up(short, [1] + rest)
        q = halves[:, :half_q].reshape(3, width, width)
        g_qkv = jnp.concatenate([q[0], q[1], q[2]], axis=1)
        e = halves[:, half_q : half_q + half_e].reshape(-1, width)
        g_out, g_head_t = e[:width], e[width : width + 2 * feat]
        later = halves[:, half_q + half_e :].reshape(-1, width)
        g_pos, g_patch = later[:length], later[length : length + feat]
        extras = got[..., n_own : n_own + items + 1, :]
        extras = jnp.moveaxis(extras, 0, cube.nbits - 2)
        extras = extras.reshape(cube.size, items + 1, width).astype(f32)

    sums = extras[:, :items].reshape(-1, width)
    facts = extras[:, items]
    scale_sum = jnp.sum(facts[:, 0] + facts[:, 1] + facts[:, 2])
    count = jnp.sum(facts[:, 3] + facts[:, 4] + facts[:, 5])
    top = jnp.max(facts[:, 6] + facts[:, 7] + facts[:, 8])
    all_slots = (facts[:, 9 : 9 + items] * 32 + facts[:, 9 + items : 9 + 2 * items]).reshape(-1)
    own_rows = classes // cube.size
    wanted = (cube.me * own_rows + jnp.arange(own_rows)).astype(f32)
    hot = (wanted[:, None] == all_slots[None, :]).astype(bf16)
    class_own = dot(hot, sums.astype(bf16))

    out = jnp.where(
        seq == 0, jnp.concatenate([back_keep, back_came]), jnp.concatenate([back_came, back_keep])
    )
    latent_out = out[:, :feat].transpose(0, 2, 1)
    logdet_out = out[:, feat, 0]
    grad_in_out = out[:, feat + 8 :].transpose(0, 2, 1)
    b1_all = short[ROW["b1"] : ROW["b1"] + ff // width].reshape(-1)
    b1_own = lax.dynamic_slice_in_dim(b1_all, cube.me * chunk, chunk, 0)
    vec = {name: short[at] for name, at in ROW.items()}
    return (
        latent_out, logdet_out, grad_in_out, g_patch, vec["bp"], g_pos, class_own,
        vec["n1g"], vec["n1s"], g_qkv, g_out, vec["n2g"], vec["n2s"], own_fc1.T, b1_own, own_fc2,
        vec["b2"], vec["fg"], vec["fs"], g_head_t.T, vec["bh"][: 2 * feat], scale_sum / count, top,
    )


def pair_kernel(bit, place, ka, kb, ca, cb, kept, send):
    mine = place[bit]
    n = ka.shape[2]
    for t, (k, c) in enumerate(((ka, ca), (kb, cb))):
        for a in range(k.shape[0]):
            kept[a, t * n : (t + 1) * n] = k[a, mine] + c[a, mine].astype(f32)
            send[a, t * n : (t + 1) * n] = (k[a, 1 - mine] + c[a, 1 - mine].astype(f32)).astype(bf16)


def add_split_pair(place, bit, ka, kb, ca, cb, name):
    n, w = ka.shape[1:]
    args = [v.reshape(2, 2, n, w) for v in (ka, kb, ca, cb)]
    kept, send = call(
        partial(pair_kernel, bit), [((2, 2 * n, w), f32), ((2, 2 * n, w), bf16)], [place] + args, name, 1e6, 4,
        smem=(0,),
    )
    return (kept,), (send,)


def last_call(geo, place, quarters, width, length, feat):
    n = quarters[0].shape[0]
    outs = [
        ((width, 3 * width), f32), ((width, width), f32), ((length, width), f32),
        ((2 * feat, width), f32), ((feat, width), f32), ((2, 16, geo["extra"], width), bf16),
    ]
    return pl.pallas_call(
        partial(last_kernel, geo),
        out_shape=[jax.ShapeDtypeStruct(s, d) for s, d in outs],
        in_specs=[pl.BlockSpec(memory_space=pltpu.SMEM)] + [pl.BlockSpec(memory_space=pltpu.VMEM)] * 8,
        out_specs=[pl.BlockSpec(memory_space=pltpu.VMEM)] * len(outs),
        scratch_shapes=[pltpu.VMEM((2, 2, 2, n, width), bf16)],
        compiler_params=pltpu.CompilerParams(vmem_limit_bytes=24 * 2**20),
        cost_estimate=pl.CostEstimate(flops=10**6, bytes_accessed=20 * 10**6, transcendentals=0),
        name="last",
    )(place, *quarters)


def solution(mesh):
    run, item, whole = P("dp", "seq", None), P("dp"), P()
    placed = (run, item, P("dp", "seq")) + (whole,) * 19 + (run, item)
    owned = P(AXES)
    return jax.shard_map(
        local,
        mesh=mesh,
        in_specs=placed,
        out_specs=(run, item, run, whole, whole, whole, P(AXES, None), whole, whole, whole, whole,
                   whole, whole, P(None, AXES), owned, P(AXES, None)) + (whole,) * 7,
        check_vma=False,
    )
```

```python
import math
from functools import partial

import jax
import jax.numpy as jnp
from jax import lax
from jax.experimental import pallas as pl
from jax.experimental.pallas import tpu as pltpu
from jax.sharding import PartitionSpec as P

HEADS = 12
EPS = 1e-05
GELU_A = math.sqrt(2.0 / math.pi)
GELU_B = 0.044715
bf16 = jnp.bfloat16
f32 = jnp.float32
AXES = ("dp", "seq")
ROW = dict(bp=0, n1g=1, n1s=2, n2g=3, n2s=4, b2=5, fg=6, fs=7, bh=8, b1=9)


def dot(left, right, a=1, b=0):
    return lax.dot_general(
        left, right, (((a,), (b,)), ((), ())), preferred_element_type=f32
    )


SMEM, VMEM, ANY, HBM = pltpu.SMEM, pltpu.VMEM, pl.ANY, pltpu.HBM


class Line:
    def __init__(self):
        self.last = None

    def call(self, body, outs, args, name, flops, limit, places=None, scratch=(), after=()):
        places = places or {}
        args = list(args)
        after = tuple(after) + ((self.last,) if self.last is not None else ())
        if after:
            at = max(i for i in range(len(args)) if places.get(i, VMEM) is VMEM)
            args[at] = tie(args[at], *after)
        specs = [pl.BlockSpec(memory_space=places.get(i, VMEM)) for i in range(len(args))]
        for i, place in places.items():
            if place is HBM:
                args[i] = pltpu.with_memory_space_constraint(args[i], HBM)
        got = pl.pallas_call(
            body,
            out_shape=[jax.ShapeDtypeStruct(s, d) for s, d in outs],
            in_specs=specs,
            out_specs=[pl.BlockSpec(memory_space=VMEM)] * len(outs),
            scratch_shapes=list(scratch),
            compiler_params=pltpu.CompilerParams(vmem_limit_bytes=int(limit * 2**20)),
            cost_estimate=pl.CostEstimate(flops=int(flops), bytes_accessed=1, transcendentals=0),
            name=name,
        )(*args)
        self.last = got[0]
        return got


def tie(value, *others):
    return lax.optimization_barrier((value,) + others)[0]


def where():
    dp = lax.axis_index("dp")
    return lax.axis_index("seq"), dp & 1, (dp >> 1) & 1, dp >> 2


def my_bit(bit):
    return lax.axis_index("seq") if bit == 0 else (lax.axis_index("dp") >> (bit - 1)) & 1


def row_of(ref):
    return ref[...].reshape(1, ref.shape[0]).astype(f32)


def centered(hidden):
    center = hidden - jnp.mean(hidden, axis=-1, keepdims=True)
    spread = jnp.mean(center * center, axis=-1, keepdims=True)
    inverse = lax.rsqrt(spread + EPS)
    return center * inverse, inverse


def norm_pull(grad, unit, inverse, gain):
    scaled = grad * gain
    mean = jnp.mean(scaled, axis=-1, keepdims=True)
    along = jnp.mean(scaled * unit, axis=-1, keepdims=True)
    return inverse * (scaled - mean - unit * along)


def col_sum(values):
    return jnp.sum(values, axis=0, keepdims=True)


def both_halves(seq, own, came):
    low = jnp.where(seq == 0, own, came)
    high = jnp.where(seq == 0, came, own)
    return jnp.concatenate([low, high], axis=1)


def prep_kernel(runs, cot_runs, valid, out, part, mask, sems):
    x, _, _, _ = where()
    items = out.shape[0]
    feat, span = runs.shape[1:]
    theirs = pl.ds((1 - x) * items, items)
    copies = [
        pltpu.make_async_copy(runs.at[theirs], part, sems.at[0]),
        pltpu.make_async_copy(cot_runs.at[theirs], out.at[:, feat : 2 * feat], sems.at[1]),
        pltpu.make_async_copy(valid, mask, sems.at[2]),
    ]
    for copy in copies:
        copy.start()
    for copy in copies:
        copy.wait()
    out[:, :feat] = part[...].astype(f32)
    for i in range(items):
        row = mask[pl.ds((1 - x) * items + i, 1), :].astype(f32)
        out[i, 2 * feat :] = jnp.broadcast_to(row, (out.shape[1] - 2 * feat, span))


def front_kernel(labels, came, runs_in, class_embed, b_patch_in, gain_in, shift_in, pos_in, w_patch_in, w_qkv_in,
                 w_out_in, w_fc1_in, w_fc2_in,
                 hidden0, normed1, qkv, shifted_t, attended, lse, w_qkv, w_out, w_fc1, w_fc2,
                 class_rows, runs, b_patch, gain, shift, pos, w_patch, sems):
    x, _, _, _ = where()
    items = came.shape[0]
    feat = w_patch.shape[0]
    length, width = pos.shape
    copies = []

    def fetch(source, target):
        copies.append(pltpu.make_async_copy(source, target, sems.at[len(copies)]))
        copies[-1].start()

    fetch(runs_in.at[pl.ds(x * items, items)], runs)
    for i in range(items):
        tile = pl.multiple_of(labels[x * items + i] // 16 * 16, 16)
        fetch(class_embed.at[pl.ds(tile, 16)], class_rows.at[i])
    for source, target in ((b_patch_in, b_patch), (gain_in, gain), (shift_in, shift), (w_patch_in, w_patch),
                           (pos_in, pos), (w_qkv_in, w_qkv)):
        fetch(source, target)
    small = len(copies) - 1
    for copy in copies[:small]:
        copy.wait()
    gain_row, shift_row, bias = row_of(gain), row_of(shift), row_of(b_patch)
    at_row = lax.broadcasted_iota(jnp.int32, (16, width), 0)
    for i in range(items):
        rows = slice(i * length, (i + 1) * length)
        whole = both_halves(x, runs[i].astype(f32), came[i, :feat])
        lane = lax.broadcasted_iota(jnp.int32, whole.shape, 1)
        moved = jnp.where(lane == 0, 0.0, pltpu.roll(whole, 1, 1)).astype(bf16)
        shifted_t[:, rows] = moved
        mine = at_row == labels[x * items + i] % 16
        base = bias + col_sum(jnp.where(mine, class_rows[i].astype(f32), 0.0))
        h0 = dot(moved, w_patch[...], 0, 0) + base + pos[...].astype(f32)
        hidden0[rows, :] = h0
        unit, _ = centered(h0)
        normed1[rows, :] = (unit * gain_row + shift_row).astype(bf16)
    copies[small].wait()
    for source, target in ((w_out_in, w_out), (w_fc1_in, w_fc1), (w_fc2_in, w_fc2)):
        fetch(source, target)
    for j in range(3):
        cols = slice(j * width, (j + 1) * width)
        qkv[:, cols] = dot(normed1[...], w_qkv[:, cols]).astype(bf16)
    key_at = lax.broadcasted_iota(jnp.int32, (length, length), 0)
    query_at = lax.broadcasted_iota(jnp.int32, (length, length), 1)
    allowed = key_at <= query_at

    def step(p, carry):
        for i in range(items):
            rows = slice(i * length, (i + 1) * length)
            at = [pl.ds(pl.multiple_of(j * width + p * 128, 128), 128) for j in range(3)]
            q, k, v = (qkv[rows, at[j]] for j in range(3))
            first = lax.broadcasted_iota(jnp.int32, q.shape, 1) < 64
            v_t = v.T
            outs = []
            for h in range(2):
                mine = first if h == 0 else ~first
                qh = jnp.where(mine, q * 0.125, jnp.zeros_like(q))
                s = jnp.where(allowed, dot(k, qh, 1, 1), -1e30)
                top = jnp.max(s, axis=0, keepdims=True)
                e = jnp.exp(s - top)
                total = jnp.sum(e, axis=0, keepdims=True)
                lse[i, pl.ds(p * 2 + h, 1), :] = top + jnp.log(total)
                probs = (e * (1.0 / total)).astype(bf16)
                outs.append(dot(v_t[h * 64 : (h + 1) * 64], probs))
            attended[rows, at[0]] = jnp.concatenate(outs, axis=0).T.astype(bf16)
        return carry

    lax.fori_loop(0, HEADS // 2, step, 0)
    for copy in copies[small + 1 :]:
        copy.wait()


def middle_kernel(det, labels, class_slot, hidden0, attended, w_out, gain2, shift2, w_fc1, b_fc1, w_fc2, b_fc2,
                  gainf, shiftf, w_head_t, b_head, runs, cot_runs, valid_runs, came,
                  hidden1, normed2, act, slope, d_hidden2, part_in, lat_keep, lat_send,
                  short, grad_head_t, facts):
    x, _, _, _ = where()
    items = came.shape[0]
    feat = runs.shape[1]
    width = w_out.shape[0]
    span = came.shape[2]
    length = 2 * span
    hidden1[...] = hidden0[...] + dot(attended[...], w_out[...])
    gain, shift = row_of(gain2), row_of(shift2)
    for i in range(items):
        rows = slice(i * length, (i + 1) * length)
        unit, _ = centered(hidden1[rows, :])
        normed2[rows, :] = (unit * gain + shift).astype(bf16)
    total = None
    for j in range(w_fc1.shape[1] // width):
        cols = slice(j * width, (j + 1) * width)
        up = dot(normed2[...], w_fc1[:, cols]) + b_fc1[cols].reshape(1, width).astype(f32)
        square = up * up
        half = 0.5 * jnp.tanh(up * (GELU_A + GELU_A * GELU_B * square)) + 0.5
        value = up * half
        act[:, cols] = value.astype(bf16)
        slope[:, cols] = (
            half + 2.0 * value * (1.0 - half) * (GELU_A + 3.0 * GELU_A * GELU_B * square)
        ).astype(bf16)
        part = dot(act[:, cols], w_fc2[cols, :])
        total = part if total is None else total + part
    hidden2 = hidden1[...] + total + row_of(b_fc2)
    unit, inverse_dev = centered(hidden2)
    gain = row_of(gainf)
    normed3 = (unit * gain + row_of(shiftf)).astype(bf16)
    bias = jnp.broadcast_to(row_of(b_head), (8, 2 * feat)).T[:, :1]
    head = dot(w_head_t[...], normed3, 1, 1) + bias
    short[...] = jnp.zeros(short.shape, f32)
    d_heads = []
    sums = [jnp.zeros((1, 1), f32), jnp.zeros((1, 1), f32), jnp.full((1, 1), -1e30, f32)]
    for i in range(items):
        cols = slice(i * length, (i + 1) * length)
        source = x * items + i
        given = both_halves(x, runs[source].astype(f32), came[i, :feat])
        cot = both_halves(x, cot_runs[source], came[i, feat : 2 * feat])
        valid = both_halves(
            x, valid_runs[source].astype(f32), came[i, 2 * feat : 2 * feat + 1]
        )
        shift_part = head[:feat, cols]
        log_scale = head[feat:, cols]
        inverse = jnp.exp(-log_scale)
        moved = (given - shift_part) * inverse
        latent = valid * moved + (1.0 - valid) * given
        d_moved = valid * cot
        d_heads.append(
            jnp.concatenate(
                [-d_moved * inverse, -d_moved * moved - valid * det[source]], axis=0
            ).astype(bf16)
        )
        part_in[:, cols] = cot * (1.0 - valid) + d_moved * inverse
        counted = valid * log_scale
        item_sum = jnp.sum(jnp.sum(counted, axis=1, keepdims=True), axis=0, keepdims=True)
        sums[0] = sums[0] + item_sum
        sums[1] = sums[1] + jnp.sum(valid, axis=1, keepdims=True) * feat
        tops = jnp.where(valid > 0, log_scale, -1e30)
        tops = jnp.max(jnp.max(tops, axis=1, keepdims=True), axis=0, keepdims=True)
        sums[2] = jnp.maximum(sums[2], tops)
        low, high = latent[:, :span], latent[:, span:]
        logdet = jnp.broadcast_to(-item_sum, (8, span))
        lat_keep[i, :feat] = jnp.where(x == 0, low, high)
        lat_send[i, :feat] = jnp.where(x == 0, high, low)
        lat_keep[i, feat:] = logdet
        lat_send[i, feat:] = logdet
    lane = lax.broadcasted_iota(jnp.int32, facts.shape, 1)
    row = jnp.zeros(facts.shape, f32)
    for k, value in enumerate(sums):
        for j in range(3):
            piece = value.astype(bf16).astype(f32)
            value = value - piece
            row = jnp.where(lane == 3 * k + j, piece, row)
    for i in range(items):
        slot = class_slot[labels[x * items + i]]
        row = jnp.where(lane == 9 + i, (slot // 32).astype(f32), row)
        row = jnp.where(lane == 9 + items + i, (slot % 32).astype(f32), row)
    facts[...] = row
    d_head = jnp.concatenate(d_heads, axis=1)
    grad_head_t[...] = dot(d_head, normed3)
    short[ROW["bh"] : ROW["bh"] + 1, : 2 * feat] = dot(
        jnp.ones((8, d_head.shape[1]), bf16), d_head, 1, 1
    )[:1]
    d_normed3 = dot(d_head, w_head_t[...], 0, 0)
    short[ROW["fg"] : ROW["fg"] + 1, :] = col_sum(d_normed3 * unit)
    short[ROW["fs"] : ROW["fs"] + 1, :] = col_sum(d_normed3)
    pulled = norm_pull(d_normed3, unit, inverse_dev, gain)
    d_hidden2[...] = pulled
    short[ROW["b2"] : ROW["b2"] + 1, :] = col_sum(pulled.astype(bf16).astype(f32))


def split_by(bit, block, keep, send, half):
    low, high = block[:half], block[half:]
    keep[...] = jnp.where(bit == 0, low, high).astype(keep.dtype)
    send[...] = jnp.where(bit == 0, high, low).astype(send.dtype)


def split_groups(core, block, first, keep, send):
    group = keep.shape[1]
    for k in range(block.shape[0] // (2 * group)):
        rows = block[2 * group * k : 2 * group * (k + 1)]
        split_by(core, rows, keep.at[first + k], send.at[first + k], group)


STEP = 384


def fc2_kernel(half, act, d_hidden2, keep, send):
    _, core, _, _ = where()
    d_mlp = d_hidden2[...].astype(bf16)
    count = act.shape[1] // 2 // STEP
    for j in range(count):
        at = (half * count + j) * STEP
        block = dot(act[:, at : at + STEP], d_mlp, 0, 0)
        split_groups(core, block, j * STEP // (2 * keep.shape[1]), keep, send)


def fc1_kernel(half, d_hidden2, w_fc2, slope, normed2, w_fc1, *refs):
    before, (keep, send, total_out, bias) = refs[:-4], refs[-4:]
    _, core, _, _ = where()
    width = normed2.shape[1]
    d_mlp = d_hidden2[...].astype(bf16)
    total = before[0][...] if before else None
    count = w_fc1.shape[1] // 2 // width
    for j in range(count):
        at = (half * count + j) * width
        cols = slice(at, at + width)
        d_up = (dot(d_mlp, w_fc2[cols, :], 1, 1) * slope[:, cols].astype(f32)).astype(bf16)
        bias[j : j + 1, :] = col_sum(d_up.astype(f32))
        for m in range(width // STEP):
            block = dot(d_up[:, m * STEP : (m + 1) * STEP], normed2[...], 0, 0)
            split_groups(core, block, (j * width + m * STEP) // (2 * keep.shape[1]), keep, send)
        part = dot(d_up, w_fc1[:, cols], 1, 1)
        total = part if total is None else total + part
    total_out[...] = total


def back_kernel(d_hidden2, total_in, hidden1, gain2, attended, w_out, short_in, bias_a, bias_b, grad_head_t,
                d_hidden1, short, out_keep, out_send, d_attended):
    _, core, _, _ = where()
    width = w_out.shape[0]
    short[...] = short_in[...]
    n = bias_a.shape[0]
    short[ROW["b1"] : ROW["b1"] + n, :] = bias_a[...]
    short[ROW["b1"] + n : ROW["b1"] + 2 * n, :] = bias_b[...]
    unit, inverse_dev = centered(hidden1[...])
    total = total_in[...]
    short[ROW["n2g"] : ROW["n2g"] + 1, :] = col_sum(total * unit)
    short[ROW["n2s"] : ROW["n2s"] + 1, :] = col_sum(total)
    h1 = d_hidden2[...] + norm_pull(total, unit, inverse_dev, row_of(gain2))
    d_hidden1[...] = h1
    d_out = h1.astype(bf16)
    d_attended[...] = dot(d_out, w_out[...], 1, 1).astype(bf16)
    grad_out = dot(attended[...], d_out, 0, 0)
    half = out_keep.shape[0]
    rest = 2 * half - grad_out.shape[0] - grad_head_t.shape[0]
    block = jnp.concatenate([grad_out, grad_head_t[...], jnp.zeros((rest, width), f32)], axis=0)
    split_by(core, block, out_keep, out_send, half)


def attention_back_kernel(qkv, lse, d_attended, d_qkv):
    rows_all, width = d_attended.shape
    items = lse.shape[0]
    length = rows_all // items
    key_at = lax.broadcasted_iota(jnp.int32, (length, length), 0)
    query_at = lax.broadcasted_iota(jnp.int32, (length, length), 1)
    allowed = key_at <= query_at

    def step(p, carry):
        for i in range(items):
            rows = slice(i * length, (i + 1) * length)
            at = [pl.ds(pl.multiple_of(j * width + p * 128, 128), 128) for j in range(3)]
            q, k, v = (qkv[rows, at[j]] for j in range(3))
            q = q * 0.125
            d_o = d_attended[rows, at[0]]
            first = lax.broadcasted_iota(jnp.int32, q.shape, 1) < 64
            none = jnp.zeros_like(q)
            total = [None, None, None]
            for h in range(2):
                mine = first if h == 0 else ~first
                qh = jnp.where(mine, q, none)
                kh = jnp.where(mine, k * 0.125, none)
                dh = jnp.where(mine, d_o, none)
                s = jnp.where(allowed, dot(k, qh, 1, 1), -1e30)
                probs = jnp.exp(s - lse[i, pl.ds(p * 2 + h, 1), :])
                d_probs = dot(v, dh, 1, 1)
                delta = jnp.sum(probs * d_probs, axis=0, keepdims=True)
                d_s = (probs * (d_probs - delta)).astype(bf16)
                parts = [dot(d_s, kh, 0, 0), dot(d_s, qh), dot(probs.astype(bf16), dh)]
                total = [b if a is None else a + b for a, b in zip(total, parts)]
            for j in range(3):
                d_qkv[rows, at[j]] = total[j].astype(bf16)
        return carry

    lax.fori_loop(0, HEADS // 2, step, 0)


def qkv_kernel(normed1, d_qkv, keep, send):
    _, core, _, _ = where()
    width = normed1.shape[1]
    half = keep.shape[0]
    for m in range(width // STEP):
        block = dot(normed1[:, m * STEP : (m + 1) * STEP], d_qkv[...], 0, 0)
        for j in range(3):
            part = block[:, j * width : (j + 1) * width]
            at = j * width + m * STEP
            inside = at % half

            @pl.when(core == at // half)
            def _():
                keep[inside : inside + STEP, :] = part

            @pl.when(core != at // half)
            def _():
                send[inside : inside + STEP, :] = part.astype(bf16)


def rest_kernel(d_qkv, w_qkv, hidden0, d_hidden1, gain1, shifted_t, w_patch, part_in, short_in, facts, lat_keep, lat_send,
                keep, send, short, in_keep, in_send, extra):
    x, core, _, _ = where()
    width = hidden0.shape[1]
    items, done, span = lat_keep.shape
    feat = w_patch.shape[0]
    length = 2 * span
    in_keep[:, :done] = lat_keep[...]
    in_send[:, :done] = lat_send[...]
    d_normed1 = dot(d_qkv[...], w_qkv[...], 1, 1)
    unit, inverse_dev = centered(hidden0[...])
    short[...] = short_in[...]
    short[ROW["n1g"] : ROW["n1g"] + 1, :] = col_sum(d_normed1 * unit)
    short[ROW["n1s"] : ROW["n1s"] + 1, :] = col_sum(d_normed1)
    d0 = d_hidden1[...] + norm_pull(d_normed1, unit, inverse_dev, row_of(gain1))
    d_low = d0.astype(bf16)
    extra[...] = jnp.zeros(extra.shape, bf16)
    d_pos, whole = None, None
    for i in range(items):
        mine = d0[i * length : (i + 1) * length]
        d_pos = mine if d_pos is None else d_pos + mine
        item = col_sum(mine)
        whole = item if whole is None else whole + item
        extra[i : i + 1, :] = item.astype(bf16)
    extra[items : items + 1, :] = facts[...].astype(bf16)
    short[ROW["bp"] : ROW["bp"] + 1, :] = whole
    d_patch = dot(shifted_t[...], d_low)
    half = keep.shape[0]
    rest = 2 * half - d_pos.shape[0] - d_patch.shape[0]
    block = jnp.concatenate([d_pos, d_patch, jnp.zeros((rest, width), f32)], axis=0)
    split_by(core, block, keep, send.at[:half], half)
    short[...] = put_short(send, half, short[...])
    d_shift = dot(w_patch[...], d_low, 1, 1)
    for i in range(items):
        cols = slice(i * length, (i + 1) * length)
        moved = d_shift[:, cols]
        lane = lax.broadcasted_iota(jnp.int32, moved.shape, 1)
        back = jnp.where(lane == length - 1, 0.0, pltpu.roll(moved, length - 1, 1))
        grad = part_in[:, cols] + back
        in_keep[i, done:] = jnp.where(x == 0, grad[:, :span], grad[:, span:])
        in_send[i, done:] = jnp.where(x == 0, grad[:, span:], grad[:, :span])


def put_short(send, at, short):
    n = short.shape[0]
    high = short.astype(bf16)
    low = (short - high.astype(f32)).astype(bf16)
    send[at : at + n, :] = high
    send[at + n : at + 2 * n, :] = low
    return high.astype(f32) + low.astype(f32)


def take_short(came, at, n):
    return came[at : at + n, :].astype(f32) + came[at + n : at + 2 * n, :].astype(f32)


def split_sum(bit, pairs, kept, send):
    mine = my_bit(bit)
    n = 0
    for keep, came in pairs:
        for a in range(keep.shape[0]):
            kept[n] = keep[a, mine] + came[a, mine].astype(f32)
            send[n] = (keep[a, 1 - mine] + came[a, 1 - mine].astype(f32)).astype(bf16)
            n += 1


def stage_kernel(bits, counts, *refs):
    n = 2 * sum(counts)
    ins, outs = refs[:n], refs[n:]
    for i, (bit, count) in enumerate(zip(bits, counts)):
        pairs = [(ins[2 * j], ins[2 * j + 1]) for j in range(count)]
        ins = ins[2 * count :]
        split_sum(bit, pairs, outs[2 * i], outs[2 * i + 1])


def stage(line, name, *parts, after=()):
    outs, args = [], []
    for bit, pairs in parts:
        _, _, b, w = pairs[0][0].shape
        total = sum(keep.shape[0] for keep, _ in pairs)
        outs += [((total, b, w), f32), ((total, b, w), bf16)]
        for pair in pairs:
            args += list(pair)
    bits, counts = tuple(p[0] for p in parts), tuple(len(p[1]) for p in parts)
    return line.call(partial(stage_kernel, bits, counts), outs, args, name, 1, 8, after=after)


def add_kernel(keep, came, *outs):
    at = 0
    for out in outs:
        n = out.shape[0]
        out[...] = keep[at : at + n, :] + came[at : at + n, :].astype(f32)
        at += n


def bulk0_kernel(qk, qc, ek, ec, lk, lc, short_in, keep_a, keep_b, send_a, send_b, short):
    x, _, y, _ = where()
    na, nb = keep_a.shape[0], keep_b.shape[0]
    nq, nl = qk.shape[0], lk.shape[0]
    ns = short.shape[0]
    total = short_in[...] + take_short(lc, nl, ns)
    mine, away = pl.ds(pl.multiple_of(x * na, na), na), pl.ds(pl.multiple_of((1 - x) * na, na), na)
    keep_a[...] = qk[mine, :] + qc[mine, :].astype(f32)
    send_a[...] = (qk[away, :] + qc[away, :].astype(f32)).astype(bf16)
    low = 2 * na
    parts = [
        qk[low:nq, :] + qc[low:nq, :].astype(f32),
        ek[...] + ec[...].astype(f32),
        lk[...] + lc[:nl, :].astype(f32),
    ]
    block = jnp.concatenate(parts, axis=0)
    split_by(y, block, keep_b, send_b.at[:nb], nb)
    short[...] = put_short(send_b, nb, total)


def bulk1_kernel(ka, ca, kb, cb, short_in, keep_a, keep_b, send_a, send_b, short):
    x, _, y, _ = where()
    na, nb = keep_a.shape[0], keep_b.shape[0]
    ns = short.shape[0]
    total = short_in[...] + take_short(cb, 2 * nb, ns)
    for bit, n, k, c, keep, send in ((y, na, ka, ca, keep_a, send_a), (x, nb, kb, cb, keep_b, send_b)):
        mine, away = pl.ds(pl.multiple_of(bit * n, n), n), pl.ds(pl.multiple_of((1 - bit) * n, n), n)
        keep[...] = k[mine, :] + c[mine, :].astype(f32)
        send[:n, :] = (k[away, :] + c[away, :].astype(f32)).astype(bf16)
    short[...] = put_short(send_b, nb, total)


def bulk2_kernel(ka, ca, kb, cb, short_in, keep, send1, send2, send3, short):
    _, _, _, z = where()
    na, nb = ka.shape[0] // 4, kb.shape[0] // 4
    ns = short.shape[0]
    total = short_in[...] + take_short(cb, 4 * nb, ns)
    for m, out in enumerate((keep, send1, send2, send3)):
        at = z ^ m
        ra = pl.ds(pl.multiple_of(at * na, na), na)
        rb = pl.ds(pl.multiple_of(at * nb, nb), nb)
        out[:na, :] = (ka[ra, :] + ca[ra, :].astype(f32)).astype(out.dtype)
        out[na : na + nb, :] = (kb[rb, :] + cb[rb, :].astype(f32)).astype(out.dtype)
        if m:
            short[...] = put_short(out, na + nb, total)


def bulk3_kernel(keep, c1, c2, c3, short_in, extra, piece, short):
    n = keep.shape[0]
    ns = short.shape[0]
    total = keep[...]
    for c in (c1, c2, c3):
        total = total + c[:n, :].astype(f32)
    piece[:n, :] = total.astype(bf16)
    piece[n:, :] = extra[...]
    short[...] = (short_in[...] + take_short(c1, n, ns)) + (take_short(c2, n, ns) + take_short(c3, n, ns))


def join0_kernel(own, c1, c2, c3, part_a, part_b):
    _, _, _, z = where()
    na, nb = part_a.shape[0] // 4, part_b.shape[0] // 4
    for m, c in enumerate((own, c1, c2, c3)):
        at = z ^ m
        part_a[pl.ds(pl.multiple_of(at * na, na), na), :] = c[:na, :]
        part_b[pl.ds(pl.multiple_of(at * nb, nb), nb), :] = c[na:, :]


def join1_kernel(own_a, came_a, own_b, came_b, part_a, part_b):
    x, _, y, _ = where()
    n = own_a.shape[0]
    for bit, own, came, part in ((y, own_a, came_a, part_a), (x, own_b, came_b, part_b)):
        part[pl.ds(pl.multiple_of(bit * n, n), n), :] = own[...]
        part[pl.ds(pl.multiple_of((1 - bit) * n, n), n), :] = came[...]


def write_kernel(geo, first, jobs, *refs):
    n_out = 5
    quarters = refs[: len(jobs)]
    refs = refs[len(jobs) :]
    if not first:
        refs = refs[n_out:]
    g_qkv, g_out, g_pos, g_head, g_patch, wide, sems = refs
    x, core, y, _ = where()
    width = g_out.shape[0]
    half_q, half_e, half_l = geo["half_q"], geo["half_e"], geo["half_l"]
    nb, ne = geo["nb"], geo["extra"]
    feat = g_patch.shape[0]
    at, sem = 0, 0
    waits = []

    def copy(rows, target):
        nonlocal sem
        c = pltpu.make_async_copy(wide.at[rows], target, sems.at[sem])
        sem += 1
        return c

    for quarter, (part, other_core, other_half) in zip(quarters, jobs):
        c = 1 - core if other_core else core
        n = quarter.shape[0]
        if part == "a":
            h = 1 - x if other_half else x
            wide[at : at + n, :] = quarter[...].astype(f32)
            for k in range(0, n, 128):
                q = c * half_q + h * n + k
                third, row = q // width, q % width
                target = g_qkv.at[
                    pl.ds(pl.multiple_of(row, 128), 128),
                    pl.ds(pl.multiple_of(third * width, 128), width),
                ]
                waits.append((None, copy(slice(at + k, at + k + 128), target)))
                waits[-1][1].start()
            at += n
        else:
            h = 1 - y if other_half else y
            for k in range(n // (nb + ne)):
                wide[at + k * nb : at + (k + 1) * nb, :] = quarter[
                    k * (nb + ne) : k * (nb + ne) + nb, :
                ].astype(f32)
            left = half_q - 2 * geo["na"]
            rows = n // (nb + ne) * nb
            for case_c in range(2):
                for case_h in range(2):
                    spans = []
                    if case_h == 0:
                        spans.append((0, left, "q", case_c * half_q + 2 * geo["na"]))
                        spans.append((left, rows - left, "e", case_c * half_e))
                    else:
                        spans.append((0, half_e - (rows - left), "e", case_c * half_e + rows - left))
                        spans.append((half_e - (rows - left), half_l, "l", case_c * half_l))
                    moves = []
                    for start, size, kind, place in spans:
                        pieces = {
                            "q": [(case_c * half_q + 2 * geo["na"], left, g_qkv)],
                            "e": [(0, width, g_out), (width, 2 * feat, g_head)],
                            "l": [(0, g_pos.shape[0], g_pos), (g_pos.shape[0], feat, g_patch)],
                        }[kind]
                        for low, long, ref in pieces:
                            a, b = max(place, low), min(place + size, low + long)
                            if a >= b:
                                continue
                            source = slice(at + start + a - place, at + start + b - place)
                            if kind == "q":
                                third, row = a // width, a % width
                                target = g_qkv.at[row : row + b - a, third * width : (third + 1) * width]
                            else:
                                target = ref.at[a - low : b - low]
                            moves.append(copy(source, target))
                    taken = (c == case_c) & (h == case_h)

                    @pl.when(taken)
                    def _(moves=moves):
                        for move in moves:
                            move.start()

                    waits += [(taken, move) for move in moves]
            at += rows
    for taken, move in waits:
        if taken is None:
            move.wait()
        else:
            pl.when(taken)(move.wait)


def class_kernel(geo, q0, q1, q2, q3, class_own, scalars, facts):
    x, core, y, _ = where()
    nb, ne, items = geo["nb"], geo["extra"], geo["items"]
    rows = class_own.shape[0]
    me = lax.axis_index("dp") * 2 + x
    want = (me * rows + lax.broadcasted_iota(jnp.int32, (rows, 1), 0)).astype(f32)
    total = jnp.zeros(class_own.shape, f32)
    for q, c, h in ((q0, core, y), (q1, core, 1 - y), (q2, 1 - core, y), (q3, 1 - core, 1 - y)):
        for k in range(8):
            block = q[k * (nb + ne) + nb : (k + 1) * (nb + ne), :].astype(f32)
            fact = block[items : items + 1]
            facts[pl.ds((c * 2 + h) * 8 + k, 1), :] = fact
            for i in range(items):
                slot = fact[:, 9 + i : 10 + i] * 32 + fact[:, 9 + items + i : 10 + items + i]
                total = total + jnp.where(want == slot, 1.0, 0.0) * block[i : i + 1]
    class_own[...] = total
    every = facts[...]
    summed = col_sum(every)
    scale_sum = summed[:, 0:1] + summed[:, 1:2] + summed[:, 2:3]
    count = summed[:, 3:4] + summed[:, 4:5] + summed[:, 5:6]
    tops = every[:, 6:7] + every[:, 7:8] + every[:, 8:9]
    lane = lax.broadcasted_iota(jnp.int32, scalars.shape, 1)
    scalars[...] = jnp.where(lane == 0, scale_sum / count, jnp.max(tops, axis=0, keepdims=True))


class Cube:
    def __init__(self):
        self.size = lax.axis_size("dp") * lax.axis_size("seq")
        self.nbits = self.size.bit_length() - 1
        self.me = lax.axis_index("dp") * lax.axis_size("seq") + lax.axis_index("seq")
        self.bit = [(self.me >> k) & 1 for k in range(self.nbits)]

    def send(self, block, mask):
        return lax.ppermute(block, AXES, [(i, i ^ mask) for i in range(self.size)])

    def start(self, full, bits):
        rows = full.shape[0] >> len(bits)
        return full.reshape((2,) * len(bits) + (rows, full.shape[1])), list(bits)

    def scatter(self, block, left):
        for bit in list(left):
            axis = left.index(bit)
            mine = lax.dynamic_index_in_dim(block, self.bit[bit], axis, keepdims=False)
            away = lax.dynamic_index_in_dim(block, 1 - self.bit[bit], axis, keepdims=False)
            block = mine + self.send(away.astype(bf16), 1 << bit).astype(f32)
            left = [b for b in left if b != bit]
        return block

    def add_up(self, block, bits):
        for k in bits:
            block = block + self.send(block, 1 << k)
        return block

    def gather(self, block, bits):
        for k in reversed(bits):
            came = self.send(block, 1 << k)
            block = jnp.where(self.bit[k] == 0, jnp.stack([block, came]), jnp.stack([came, block]))
        return block


def local(
    patches, labels, valid_mask, class_slot, w_patch, b_patch, pos_embed, class_embed,
    norm1_gain, norm1_shift, w_qkv, w_out, norm2_gain, norm2_shift, w_fc1, b_fc1, w_fc2, b_fc2,
    final_gain, final_shift, w_head, b_head, cot_latent, cot_logdet,
):
    cube = Cube()
    line = Line()
    seq_n = lax.axis_size("seq")
    assert seq_n == 2
    seq = lax.axis_index("seq")
    held, span, feat = patches.shape
    items = held // seq_n
    length = span * seq_n
    width = w_out.shape[0]
    ff = w_fc1.shape[1]
    rows = items * length
    classes = class_embed.shape[0]
    chunk = ff // cube.size
    group = 2 * chunk
    fast = cube.size == 32

    runs = patches.transpose(0, 2, 1)
    cot_runs = cot_latent.transpose(0, 2, 1)
    valid_runs = valid_mask[:, None, :]
    w_head_t = w_head.T
    (packed,) = line.call(
        prep_kernel, [((items, 2 * feat + 8, span), f32)], [runs, cot_runs, valid_mask], "prep", 1, 1,
        places={0: HBM, 1: HBM, 2: HBM},
        scratch=[pltpu.VMEM((items, feat, span), bf16), pltpu.VMEM((held, span), jnp.int32),
                 pltpu.SemaphoreType.DMA((3,))],
    )
    came = cube.send(packed, 1)
    big = 2.0 * rows * width * ff
    vector = pltpu.VMEM((width,), bf16)
    hidden0, normed1, qkv, shifted_t, attended, lse, w_qkv, w_out, w_fc1, w_fc2 = line.call(
        front_kernel,
        [((rows, width), f32), ((rows, width), bf16), ((rows, 3 * width), bf16), ((feat, rows), bf16),
         ((rows, width), bf16), ((items, HEADS, length), f32)]
        + [(w.shape, bf16) for w in (w_qkv, w_out, w_fc1, w_fc2)],
        [labels, came, runs, class_embed, b_patch, norm1_gain, norm1_shift, pos_embed, w_patch, w_qkv, w_out,
         w_fc1, w_fc2],
        "front", 1, 6, places={0: SMEM} | {i: HBM for i in range(2, 13)},
        scratch=[pltpu.VMEM((items, 16, width), bf16), pltpu.VMEM((items, feat, span), bf16), vector, vector,
                 vector, pltpu.VMEM((length, width), bf16), pltpu.VMEM((feat, width), bf16),
                 pltpu.SemaphoreType.DMA((items + 10,))],
    )
    n_short = 16
    (hidden1, normed2, act, slope, d_hidden2, part_in, lat_keep, lat_send, short, grad_head_t, facts) = line.call(
        middle_kernel,
        [((rows, width), f32), ((rows, width), bf16), ((rows, ff), bf16), ((rows, ff), bf16),
         ((rows, width), f32), ((feat, rows), f32), ((items, feat + 8, span), f32),
         ((items, feat + 8, span), f32), ((n_short, width), f32), ((2 * feat, width), f32),
         ((1, width), f32)],
        [cot_logdet, labels, class_slot, hidden0, attended, w_out, norm2_gain, norm2_shift, w_fc1, b_fc1,
         w_fc2, b_fc2, final_gain, final_shift, w_head_t, b_head, runs, cot_runs, valid_runs, came],
        "middle", 1, 8, places={0: SMEM, 1: SMEM, 2: SMEM},
    )
    groups = ff // (4 * group)
    pieces = [((groups, group, width), f32), ((groups, group, width), bf16)]

    def fc2_half(h):
        return line.call(partial(fc2_kernel, h), pieces, [act, d_hidden2], "fc2", 1, 4)

    def fc1_half(h, before):
        return line.call(
            partial(fc1_kernel, h),
            pieces + [((rows, width), f32), ((ff // width // 2, width), f32)],
            [d_hidden2, w_fc2, slope, normed2, w_fc1] + before, "fc1", 1, 6,
        )

    def four(block):
        return block.reshape(groups, 2, chunk, width)

    half_e, half_l, half_q = 448, 192, 3 * width // 2
    keep20, send20 = fc2_half(0)
    came20 = cube.send(send20, 2)
    keep21, send21 = fc2_half(1)
    came21 = cube.send(send21, 2)
    keep10, send10, total, bias0 = fc1_half(0, [])
    came10 = cube.send(send10, 2)
    if fast:
        k20, s20 = stage(line, "fc2_core", (0, [(four(keep20), four(came20))]))
        c20 = cube.send(s20, 1)
    keep11, send11, total, bias1 = fc1_half(1, [total])
    came11 = cube.send(send11, 2)
    if fast:
        k21, s21 = stage(line, "fc2_core", (0, [(four(keep21), four(came21))]))
    d_hidden1, short, ekeep, esend, d_attended = line.call(
        back_kernel,
        [((rows, width), f32), ((n_short, width), f32), ((half_e, width), f32), ((half_e, width), bf16),
         ((rows, width), bf16)],
        [d_hidden2, total, hidden1, norm2_gain, attended, w_out, short, bias0, bias1, grad_head_t],
        "back", 1, 6,
    )
    ecame = cube.send(esend, 2)

    def by_y(block):
        return block.reshape(2, 2, group, width)

    if fast:
        k10, s10 = stage(line, "fc1_core", (2, [(by_y(keep10), by_y(came10))]))
        c10 = cube.send(s10, 4)
        k11, s11 = stage(line, "fc1_core", (2, [(by_y(keep11), by_y(came11))]))
    (d_qkv,) = line.call(
        attention_back_kernel, [((rows, 3 * width), bf16)], [qkv, lse, d_attended],
        "attention_back", 1, 4,
    )
    qkeep, qsend = line.call(
        qkv_kernel, [((half_q, width), f32), ((half_q, width), bf16)], [normed1, d_qkv],
        "qkv_grad", 1, 6, after=[c20] if fast else [],
    )
    qcame = cube.send(qsend, 2)
    lkeep, lsend, short, back_keep, back_send, extra = line.call(
        rest_kernel,
        [((half_l, width), f32), ((half_l + 2 * n_short, width), bf16), ((n_short, width), f32),
         ((items, 2 * feat + 8, span), f32), ((items, 2 * feat + 8, span), f32), ((16, width), bf16)],
        [d_qkv, w_qkv, hidden0, d_hidden1, norm1_gain, shifted_t, w_patch, part_in, short, facts,
         lat_keep, lat_send],
        "rest", 3e10, 6, after=[c10] if fast else [],
    )
    lcame = cube.send(lsend, 2)

    if fast:
        ns2 = 2 * n_short

        def two(na, nb):
            return [((na, width), f32), ((nb, width), f32), ((na, width), bf16), ((nb + ns2, width), bf16),
                    ((n_short, width), f32)]

        ka, kb, sa, sb, short = line.call(
            bulk0_kernel, two(512, 384), [qkeep, qcame, ekeep, ecame, lkeep, lcame, short], "bulk0", 1, 10,
        )
        ca, cb = cube.send(sa, 1), cube.send(sb, 4)
        back_came = cube.send(back_send, 1)
        ka, kb, sa, sb, short = line.call(
            bulk1_kernel, two(256, 192), [ka, ca, kb, cb, short], "bulk1", 1, 6, after=[back_came]
        )
        ca, cb = cube.send(sa, 4), cube.send(sb, 1)
        na, nb, ne = 64, 48, 16
        n = na + nb
        keep, z1, z2, z3, short = line.call(
            bulk2_kernel,
            [((n, width), f32)] + [((n + ns2, width), bf16)] * 3 + [((n_short, width), f32)],
            [ka, ca, kb, cb, short], "bulk2", 1, 4,
        )
        z1, z2, z3 = cube.send(z1, 8), cube.send(z2, 16), cube.send(z3, 24)
        c21, c11 = cube.send(tie(s21, keep), 1), cube.send(tie(s11, keep), 4)
        piece, short = line.call(
            bulk3_kernel, [((n + ne, width), bf16), ((n_short, width), f32)],
            [keep, z1, z2, z3, short, extra], "bulk3", 1, 4, after=[c21, c11],
        )
        g1, g2, g3 = cube.send(piece, 8), cube.send(piece, 16), cube.send(piece, 24)
        def next_y(block):
            return block.reshape(2, 2, chunk, width)

        k2, s2, k1, s1 = stage(
            line, "fc_second",
            (2, [(next_y(k20), next_y(c20)), (next_y(k21), next_y(c21))]),
            (0, [(next_y(k10), next_y(c10)), (next_y(k11), next_y(c11))]),
        )
        c2, c1 = cube.send(s2, 4), cube.send(s1, 1)
        kf, sf = stage(
            line, "fc_third", (3, [(next_y(k2), next_y(c2)), (next_y(k1), next_y(c1))])
        )

        part_a, part_b = line.call(
            join0_kernel, [((4 * na, width), bf16), ((4 * (nb + ne), width), bf16)],
            [piece, g1, g2, g3], "join0", 1, 4,
        )
        ca, cb = cube.send(part_a, 4), cube.send(part_b, 1)
        cf = cube.send(tie(sf, g1, g2, g3), 8)
        part_a, part_b = line.call(
            join1_kernel, [((8 * na, width), bf16), ((8 * (nb + ne), width), bf16)],
            [part_a, ca, part_b, cb], "join1", 1, 5,
        )
        ca, cb = cube.send(part_a, 1), cube.send(part_b, 4)
        xa, xb = cube.send(part_a, 2), cube.send(part_b, 2)
        geo = dict(na=8 * na, nb=nb, extra=ne, half_q=half_q, half_e=half_e, half_l=half_l, items=items)
        grads = write(line, geo, [("a", 0, 0), ("b", 0, 0)], [part_a, part_b], None, width, length, feat)

        kf, sf = stage(line, "fc_fourth", (4, [(next_y(kf), next_y(cf))]))
        cf = cube.send(sf, 16)
        ya, yb = cube.send(ca, 2), cube.send(cb, 2)
        grads = write(
            line, geo, [("a", 1, 0), ("b", 1, 0), ("a", 0, 1), ("b", 0, 1)], [xa, xb, ca, cb], grads,
            width, length, feat,
        )
        own_fc2, own_fc1 = line.call(
            add_kernel, [((chunk, width), f32)] * 2,
            [kf.reshape(2 * chunk, width), cf.reshape(2 * chunk, width)], "fc_last", 1, 3,
        )
        grads = write(line, geo, [("a", 1, 1), ("b", 1, 1)], [ya, yb], grads, width, length, feat)
        g_qkv, g_out, g_pos, g_head_t, g_patch = grads
        class_own, scalars = line.call(
            partial(class_kernel, geo), [((classes // cube.size, width), f32), ((1, 128), f32)],
            [part_b, cb, xb, yb], "classes", 1, 5, scratch=[pltpu.VMEM((cube.size, width), f32)],
        )
        mean, top = scalars[0, 0], scalars[0, 1]
    else:
        rest = [0] + list(range(2, cube.nbits))
        upper = list(range(cube.nbits - 1, 1, -1)) + [0]
        back_came = cube.send(back_send, 1)

        def owned(*parts):
            total = jnp.concatenate([k + c.astype(f32) for k, c in parts]).reshape(-1, width)
            return cube.scatter(*cube.start(total, upper))

        own_fc2 = owned((keep20, came20), (keep21, came21))
        own_fc1 = owned((keep10, came10), (keep11, came11))
        full = jnp.concatenate(
            [qkeep + qcame.astype(f32), ekeep + ecame.astype(f32), lkeep + lcame[:half_l].astype(f32)]
        )
        n_full = full.shape[0]
        full = jnp.pad(full, ((0, -n_full % (cube.size * 8)), (0, 0)))
        own = cube.scatter(*cube.start(full, upper))
        n_own = own.shape[0]
        got = cube.gather(jnp.concatenate([own.astype(bf16), extra]), [1] + upper)
        halves = got[..., :n_own, :].reshape(2, -1, width)[:, :n_full].astype(f32)
        short = cube.add_up(short, [1] + rest)
        q = halves[:, :half_q].reshape(3, width, width)
        g_qkv = jnp.concatenate([q[0], q[1], q[2]], axis=1)
        e = halves[:, half_q : half_q + half_e].reshape(-1, width)
        g_out, g_head_t = e[:width], e[width : width + 2 * feat]
        later = halves[:, half_q + half_e :].reshape(-1, width)
        g_pos, g_patch = later[:length], later[length : length + feat]
        extras = got[..., n_own : n_own + items + 1, :].reshape(cube.size, items + 1, width).astype(f32)
        sums = extras[:, :items].reshape(-1, width)
        facts = extras[:, items]
        mean = jnp.sum(facts[:, :3]) / jnp.sum(facts[:, 3:6])
        top = jnp.max(facts[:, 6] + facts[:, 7] + facts[:, 8])
        all_slots = (facts[:, 9 : 9 + items] * 32 + facts[:, 9 + items : 9 + 2 * items]).reshape(-1)
        own_rows = classes // cube.size
        wanted = (cube.me * own_rows + jnp.arange(own_rows)).astype(f32)
        hot = (wanted[:, None] == all_slots[None, :]).astype(bf16)
        class_own = dot(hot, sums.astype(bf16))

    out = jnp.where(
        seq == 0, jnp.concatenate([back_keep, back_came]), jnp.concatenate([back_came, back_keep])
    )
    latent_out = out[:, :feat].transpose(0, 2, 1)
    logdet_out = out[:, feat, 0]
    grad_in_out = out[:, feat + 8 :].transpose(0, 2, 1)
    b1_all = short[ROW["b1"] : ROW["b1"] + ff // width].reshape(-1)
    b1_own = lax.dynamic_slice_in_dim(b1_all, cube.me * chunk, chunk, 0)
    vec = {name: short[at] for name, at in ROW.items()}
    return (
        latent_out, logdet_out, grad_in_out, g_patch, vec["bp"], g_pos, class_own,
        vec["n1g"], vec["n1s"], g_qkv, g_out, vec["n2g"], vec["n2s"], own_fc1.T, b1_own, own_fc2,
        vec["b2"], vec["fg"], vec["fs"], g_head_t.T, vec["bh"][: 2 * feat], mean, top,
    )


def write(line, geo, jobs, quarters, grads, width, length, feat):
    shapes = [(width, 3 * width), (width, width), (length, width), (2 * feat, width), (feat, width)]
    n = len(quarters)
    args = list(quarters)
    args[0] = tie(args[0], line.last)
    aliases = {}
    if grads is not None:
        aliases = {n + i: i for i in range(len(shapes))}
        args += list(grads)
    grads = pl.pallas_call(
        partial(write_kernel, geo, grads is None, jobs),
        out_shape=[jax.ShapeDtypeStruct(s, f32) for s in shapes],
        in_specs=[pl.BlockSpec(memory_space=VMEM)] * n + [pl.BlockSpec(memory_space=ANY)] * len(aliases),
        out_specs=[pl.BlockSpec(memory_space=ANY)] * len(shapes),
        scratch_shapes=[pltpu.VMEM((512 * n, width), f32), pltpu.SemaphoreType.DMA((16 * n,))],
        input_output_aliases=aliases,
        compiler_params=pltpu.CompilerParams(vmem_limit_bytes=(2 * n + 4) * 2**20),
        cost_estimate=pl.CostEstimate(flops=10**10, bytes_accessed=1, transcendentals=0),
        name="write",
    )(*args)
    line.last = grads[-1]
    return grads


def solution(mesh):
    run, item, whole = P("dp", "seq", None), P("dp"), P()
    placed = (run, item, P("dp", "seq")) + (whole,) * 19 + (run, item)
    owned = P(AXES)
    return jax.shard_map(
        local,
        mesh=mesh,
        in_specs=placed,
        out_specs=(run, item, run, whole, whole, whole, P(AXES, None), whole, whole, whole, whole,
                   whole, whole, P(None, AXES), owned, P(AXES, None)) + (whole,) * 7,
        check_vma=False,
    )
```

```python
import math
from functools import partial

import jax
import jax.numpy as jnp
from jax import lax
from jax.experimental import pallas as pl
from jax.experimental.pallas import tpu as pltpu
from jax.sharding import PartitionSpec as P

HEADS = 12
EPS = 1e-05
GELU_A = math.sqrt(2.0 / math.pi)
GELU_B = 0.044715
bf16 = jnp.bfloat16
f32 = jnp.float32
AXES = ("dp", "seq")
ROW = dict(bp=0, n1g=1, n1s=2, n2g=3, n2s=4, b2=5, fg=6, fs=7, bh=8, b1=9)


def dot(left, right, a=1, b=0):
    return lax.dot_general(
        left, right, (((a,), (b,)), ((), ())), preferred_element_type=f32
    )


SMEM, VMEM, ANY, HBM = pltpu.SMEM, pltpu.VMEM, pl.ANY, pltpu.HBM


class Line:
    def __init__(self):
        self.last = None

    def call(self, body, outs, args, name, flops, limit, places=None, scratch=(), after=(), tied=True, pinned=True):
        places = places or {}
        args = list(args)
        after = tuple(after) + ((self.last,) if self.last is not None else ())
        if after and tied:
            at = max(i for i in range(len(args)) if places.get(i, VMEM) is VMEM)
            args[at] = tie(args[at], *after)
        specs = [pl.BlockSpec(memory_space=places.get(i, VMEM)) for i in range(len(args))]
        for i, place in places.items():
            if place is HBM:
                args[i] = pltpu.with_memory_space_constraint(args[i], HBM)
        got = pl.pallas_call(
            body,
            out_shape=[pltpu.VMEM(s, d) if pinned else jax.ShapeDtypeStruct(s, d) for s, d in outs],
            in_specs=specs,
            out_specs=[pl.BlockSpec(memory_space=VMEM)] * len(outs),
            scratch_shapes=list(scratch),
            compiler_params=pltpu.CompilerParams(vmem_limit_bytes=int(limit * 2**20)),
            cost_estimate=pl.CostEstimate(flops=int(flops), bytes_accessed=1, transcendentals=0),
            name=name,
        )(*args)
        self.last = got[0]
        return got


def tie(value, *others):
    return lax.optimization_barrier((value,) + others)[0]


def where():
    dp = lax.axis_index("dp")
    return lax.axis_index("seq"), dp & 1, (dp >> 1) & 1, dp >> 2


def my_bit(bit):
    return lax.axis_index("seq") if bit == 0 else (lax.axis_index("dp") >> (bit - 1)) & 1


def row_of(ref):
    return ref[...].reshape(1, ref.shape[0]).astype(f32)


def centered(hidden):
    center = hidden - jnp.mean(hidden, axis=-1, keepdims=True)
    spread = jnp.mean(center * center, axis=-1, keepdims=True)
    inverse = lax.rsqrt(spread + EPS)
    return center * inverse, inverse


def norm_pull(grad, unit, inverse, gain):
    scaled = grad * gain
    mean = jnp.mean(scaled, axis=-1, keepdims=True)
    along = jnp.mean(scaled * unit, axis=-1, keepdims=True)
    return inverse * (scaled - mean - unit * along)


def col_sum(values):
    return jnp.sum(values, axis=0, keepdims=True)


def both_halves(seq, own, came):
    low = jnp.where(seq == 0, own, came)
    high = jnp.where(seq == 0, came, own)
    return jnp.concatenate([low, high], axis=1)


def prep_kernel(runs, cot_runs, valid, out, part, mask, sems):
    x, _, _, _ = where()
    items = out.shape[0]
    feat, span = runs.shape[1:]
    theirs = pl.ds((1 - x) * items, items)
    copies = [
        pltpu.make_async_copy(runs.at[theirs], part, sems.at[0]),
        pltpu.make_async_copy(cot_runs.at[theirs], out.at[:, feat : 2 * feat], sems.at[1]),
        pltpu.make_async_copy(valid, mask, sems.at[2]),
    ]
    for copy in copies:
        copy.start()
    for copy in copies:
        copy.wait()
    out[:, :feat] = part[...].astype(f32)
    for i in range(items):
        row = mask[pl.ds((1 - x) * items + i, 1), :].astype(f32)
        out[i, 2 * feat :] = jnp.broadcast_to(row, (out.shape[1] - 2 * feat, span))


def fetch_kernel(labels, sent, runs_in, class_embed, b_patch_in, gain_in, shift_in, pos_in, w_patch_in, w_qkv_in,
                 runs, class_rows, b_patch, gain, shift, pos, w_patch, w_qkv, sems):
    x, _, _, _ = where()
    items = runs.shape[0]
    pairs = [(w_qkv_in, w_qkv), (runs_in.at[pl.ds(x * items, items)], runs)]
    for i in range(items):
        tile = pl.multiple_of(labels[x * items + i] // 16 * 16, 16)
        pairs.append((class_embed.at[pl.ds(tile, 16)], class_rows.at[i]))
    pairs += [(b_patch_in, b_patch), (gain_in, gain), (shift_in, shift), (w_patch_in, w_patch), (pos_in, pos)]
    copies = [pltpu.make_async_copy(*pair, sems.at[n]) for n, pair in enumerate(pairs)]
    for copy in copies:
        copy.start()
    for copy in copies:
        copy.wait()


def front_kernel(labels, came, runs, class_rows, b_patch, gain, shift, pos, w_patch, w_qkv,
                 w_out_in, w_fc1_in, w_fc2_in,
                 hidden0, normed1, qkv, shifted_t, attended, lse, w_out, w_fc1, w_fc2, sems):
    x, _, _, _ = where()
    items = came.shape[0]
    feat = w_patch.shape[0]
    length, width = pos.shape
    copies = []
    for source, target in ((w_out_in, w_out), (w_fc1_in, w_fc1), (w_fc2_in, w_fc2)):
        copies.append(pltpu.make_async_copy(source, target, sems.at[len(copies)]))
        copies[-1].start()
    gain_row, shift_row, bias = row_of(gain), row_of(shift), row_of(b_patch)
    at_row = lax.broadcasted_iota(jnp.int32, (16, width), 0)
    for i in range(items):
        rows = slice(i * length, (i + 1) * length)
        whole = both_halves(x, runs[i].astype(f32), came[i, :feat])
        lane = lax.broadcasted_iota(jnp.int32, whole.shape, 1)
        moved = jnp.where(lane == 0, 0.0, pltpu.roll(whole, 1, 1)).astype(bf16)
        shifted_t[:, rows] = moved
        mine = at_row == labels[x * items + i] % 16
        base = bias + col_sum(jnp.where(mine, class_rows[i].astype(f32), 0.0))
        h0 = dot(moved, w_patch[...], 0, 0) + base + pos[...].astype(f32)
        hidden0[rows, :] = h0
        unit, _ = centered(h0)
        normed1[rows, :] = (unit * gain_row + shift_row).astype(bf16)
    for j in range(3):
        cols = slice(j * width, (j + 1) * width)
        qkv[:, cols] = dot(normed1[...], w_qkv[:, cols]).astype(bf16)
    mid = length // 2
    allowed = lower_keys(mid)

    def step(p, carry):
        for i in range(items):
            rows = slice(i * length, (i + 1) * length)
            at = [pl.ds(pl.multiple_of(j * width + p * 128, 128), 128) for j in range(3)]
            q, k, v = (qkv[rows, at[j]] for j in range(3))
            first = lax.broadcasted_iota(jnp.int32, q.shape, 1) < 64
            v_t = v.T
            outs = []
            for h in range(2):
                mine = first if h == 0 else ~first
                qh = jnp.where(mine, q * 0.125, jnp.zeros_like(q))
                v_h = v_t[h * 64 : (h + 1) * 64]
                s = dot(k[:mid], qh, 1, 1)
                s_a, s_b = jnp.where(allowed, s[:, :mid], -1e30), s[:, mid:]
                s_c = jnp.where(allowed, dot(k[mid:], qh[mid:], 1, 1), -1e30)
                top_a = jnp.max(s_a, axis=0, keepdims=True)
                top_b = jnp.max(jnp.maximum(s_b, s_c), axis=0, keepdims=True)
                e_a, e_b, e_c = jnp.exp(s_a - top_a), jnp.exp(s_b - top_b), jnp.exp(s_c - top_b)
                total_a = jnp.sum(e_a, axis=0, keepdims=True)
                total_b = jnp.sum(e_b + e_c, axis=0, keepdims=True)
                lse[i, pl.ds(p * 2 + h, 1), :] = jnp.concatenate(
                    [top_a + jnp.log(total_a), top_b + jnp.log(total_b)], axis=1
                )
                part_a, part_b = 1.0 / total_a, 1.0 / total_b
                p_ab = jnp.concatenate([(e_a * part_a).astype(bf16), (e_b * part_b).astype(bf16)], axis=1)
                out = dot(v_h[:, :mid], p_ab)
                late = out[:, mid:] + dot(v_h[:, mid:], (e_c * part_b).astype(bf16))
                outs.append(jnp.concatenate([out[:, :mid], late], axis=1))
            attended[rows, at[0]] = jnp.concatenate(outs, axis=0).T.astype(bf16)
        return carry

    lax.fori_loop(0, HEADS // 2, step, 0, unroll=3)
    for copy in copies:
        copy.wait()


def middle_kernel(det, labels, class_slot, hidden0, attended, w_out, gain2, shift2, w_fc1, b_fc1, w_fc2, b_fc2,
                  gainf, shiftf, w_head_t, b_head, runs, cot_runs, valid_runs, came,
                  hidden1, normed2, act, slope, d_hidden2, part_in, lat_keep, lat_send,
                  short, grad_head_t, facts):
    x, _, _, _ = where()
    items = came.shape[0]
    feat = runs.shape[1]
    width = w_out.shape[0]
    span = came.shape[2]
    length = 2 * span
    hidden1[...] = hidden0[...] + dot(attended[...], w_out[...])
    gain, shift = row_of(gain2), row_of(shift2)
    for i in range(items):
        rows = slice(i * length, (i + 1) * length)
        unit, _ = centered(hidden1[rows, :])
        normed2[rows, :] = (unit * gain + shift).astype(bf16)
    total = None
    for j in range(w_fc1.shape[1] // width):
        cols = slice(j * width, (j + 1) * width)
        up = dot(normed2[...], w_fc1[:, cols]) + b_fc1[cols].reshape(1, width).astype(f32)
        square = up * up
        half = 0.5 * jnp.tanh(up * (GELU_A + GELU_A * GELU_B * square)) + 0.5
        value = up * half
        act[:, cols] = value.astype(bf16)
        slope[:, cols] = (
            half + 2.0 * value * (1.0 - half) * (GELU_A + 3.0 * GELU_A * GELU_B * square)
        ).astype(bf16)
        part = dot(act[:, cols], w_fc2[cols, :])
        total = part if total is None else total + part
    hidden2 = hidden1[...] + total + row_of(b_fc2)
    unit, inverse_dev = centered(hidden2)
    gain = row_of(gainf)
    normed3 = (unit * gain + row_of(shiftf)).astype(bf16)
    bias = jnp.broadcast_to(row_of(b_head), (8, 2 * feat)).T[:, :1]
    head = dot(w_head_t[...], normed3, 1, 1) + bias
    short[...] = jnp.zeros(short.shape, f32)
    d_heads = []
    sums = [jnp.zeros((1, 1), f32), jnp.zeros((1, 1), f32), jnp.full((1, 1), -1e30, f32)]
    for i in range(items):
        cols = slice(i * length, (i + 1) * length)
        source = x * items + i
        given = both_halves(x, runs[source].astype(f32), came[i, :feat])
        cot = both_halves(x, cot_runs[source], came[i, feat : 2 * feat])
        valid = both_halves(
            x, valid_runs[source].astype(f32), came[i, 2 * feat : 2 * feat + 1]
        )
        shift_part = head[:feat, cols]
        log_scale = head[feat:, cols]
        inverse = jnp.exp(-log_scale)
        moved = (given - shift_part) * inverse
        latent = valid * moved + (1.0 - valid) * given
        d_moved = valid * cot
        d_heads.append(
            jnp.concatenate(
                [-d_moved * inverse, -d_moved * moved - valid * det[source]], axis=0
            ).astype(bf16)
        )
        part_in[:, cols] = cot * (1.0 - valid) + d_moved * inverse
        counted = valid * log_scale
        item_sum = jnp.sum(jnp.sum(counted, axis=1, keepdims=True), axis=0, keepdims=True)
        sums[0] = sums[0] + item_sum
        sums[1] = sums[1] + jnp.sum(valid, axis=1, keepdims=True) * feat
        tops = jnp.where(valid > 0, log_scale, -1e30)
        tops = jnp.max(jnp.max(tops, axis=1, keepdims=True), axis=0, keepdims=True)
        sums[2] = jnp.maximum(sums[2], tops)
        low, high = latent[:, :span], latent[:, span:]
        logdet = jnp.broadcast_to(-item_sum, (8, span))
        lat_keep[i, :feat] = jnp.where(x == 0, low, high)
        lat_send[i, :feat] = jnp.where(x == 0, high, low)
        lat_keep[i, feat:] = logdet
        lat_send[i, feat:] = logdet
    lane = lax.broadcasted_iota(jnp.int32, facts.shape, 1)
    row = jnp.zeros(facts.shape, f32)
    for k, value in enumerate(sums):
        for j in range(3):
            piece = value.astype(bf16).astype(f32)
            value = value - piece
            row = jnp.where(lane == 3 * k + j, piece, row)
    for i in range(items):
        slot = class_slot[labels[x * items + i]]
        row = jnp.where(lane == 9 + i, (slot // 32).astype(f32), row)
        row = jnp.where(lane == 9 + items + i, (slot % 32).astype(f32), row)
    facts[...] = row
    d_head = jnp.concatenate(d_heads, axis=1)
    grad_head_t[...] = dot(d_head, normed3)
    short[ROW["bh"] : ROW["bh"] + 1, : 2 * feat] = dot(
        jnp.ones((8, d_head.shape[1]), bf16), d_head, 1, 1
    )[:1]
    d_normed3 = dot(d_head, w_head_t[...], 0, 0)
    short[ROW["fg"] : ROW["fg"] + 1, :] = col_sum(d_normed3 * unit)
    short[ROW["fs"] : ROW["fs"] + 1, :] = col_sum(d_normed3)
    pulled = norm_pull(d_normed3, unit, inverse_dev, gain)
    d_hidden2[...] = pulled
    short[ROW["b2"] : ROW["b2"] + 1, :] = col_sum(pulled.astype(bf16).astype(f32))


def split_by(bit, block, keep, send, half):
    low, high = block[:half], block[half:]
    keep[...] = jnp.where(bit == 0, low, high).astype(keep.dtype)
    send[...] = jnp.where(bit == 0, high, low).astype(send.dtype)


def split_groups(core, block, first, keep, send):
    group = keep.shape[1]
    for k in range(block.shape[0] // (2 * group)):
        rows = block[2 * group * k : 2 * group * (k + 1)]
        split_by(core, rows, keep.at[first + k], send.at[first + k], group)


STEP = 384


def fc2_kernel(half, act, d_hidden2, keep, send):
    _, core, _, _ = where()
    d_mlp = d_hidden2[...].astype(bf16)
    count = act.shape[1] // 2 // STEP
    for j in range(count):
        at = (half * count + j) * STEP
        block = dot(act[:, at : at + STEP], d_mlp, 0, 0)
        split_groups(core, block, j * STEP // (2 * keep.shape[1]), keep, send)


def fc1_kernel(half, d_hidden2, w_fc2, slope, normed2, w_fc1, *refs):
    before, (keep, send, total_out, bias) = refs[:-4], refs[-4:]
    _, core, _, _ = where()
    width = normed2.shape[1]
    d_mlp = d_hidden2[...].astype(bf16)
    total = before[0][...] if before else None
    count = w_fc1.shape[1] // 2 // width
    for j in range(count):
        at = (half * count + j) * width
        cols = slice(at, at + width)
        d_up = (dot(d_mlp, w_fc2[cols, :], 1, 1) * slope[:, cols].astype(f32)).astype(bf16)
        bias[j : j + 1, :] = col_sum(d_up.astype(f32))
        for m in range(width // STEP):
            block = dot(d_up[:, m * STEP : (m + 1) * STEP], normed2[...], 0, 0)
            split_groups(core, block, (j * width + m * STEP) // (2 * keep.shape[1]), keep, send)
        part = dot(d_up, w_fc1[:, cols], 1, 1)
        total = part if total is None else total + part
    total_out[...] = total


def back_kernel(d_hidden2, total_in, hidden1, gain2, attended, w_out, short_in, bias_a, bias_b, grad_head_t,
                d_hidden1, short, out_keep, out_send, d_attended):
    _, core, _, _ = where()
    width = w_out.shape[0]
    short[...] = short_in[...]
    n = bias_a.shape[0]
    short[ROW["b1"] : ROW["b1"] + n, :] = bias_a[...]
    short[ROW["b1"] + n : ROW["b1"] + 2 * n, :] = bias_b[...]
    unit, inverse_dev = centered(hidden1[...])
    total = total_in[...]
    short[ROW["n2g"] : ROW["n2g"] + 1, :] = col_sum(total * unit)
    short[ROW["n2s"] : ROW["n2s"] + 1, :] = col_sum(total)
    h1 = d_hidden2[...] + norm_pull(total, unit, inverse_dev, row_of(gain2))
    d_hidden1[...] = h1
    d_out = h1.astype(bf16)
    d_attended[...] = dot(d_out, w_out[...], 1, 1).astype(bf16)
    grad_out = dot(attended[...], d_out, 0, 0)
    half = out_keep.shape[0]
    rest = 2 * half - grad_out.shape[0] - grad_head_t.shape[0]
    block = jnp.concatenate([grad_out, grad_head_t[...], jnp.zeros((rest, width), f32)], axis=0)
    split_by(core, block, out_keep, out_send, half)


def lower_keys(n):
    key_at = lax.broadcasted_iota(jnp.int32, (n, n), 0)
    return key_at <= lax.broadcasted_iota(jnp.int32, (n, n), 1)


def attention_back_kernel(qkv, lse, d_attended, d_qkv):
    rows_all, width = d_attended.shape
    items = lse.shape[0]
    length = rows_all // items
    mid = length // 2
    allowed = lower_keys(mid)

    def step(p, carry):
        for i in range(items):
            rows = slice(i * length, (i + 1) * length)
            at = [pl.ds(pl.multiple_of(j * width + p * 128, 128), 128) for j in range(3)]
            q, k, v = (qkv[rows, at[j]] for j in range(3))
            q = q * 0.125
            d_o = d_attended[rows, at[0]]
            first = lax.broadcasted_iota(jnp.int32, q.shape, 1) < 64
            none = jnp.zeros_like(q)
            total = [None] * 6
            for h in range(2):
                mine = first if h == 0 else ~first
                qh = jnp.where(mine, q, none)
                kh = jnp.where(mine, k * 0.125, none)
                dh = jnp.where(mine, d_o, none)
                log_sum = lse[i, pl.ds(p * 2 + h, 1), :]
                log_a, log_b = log_sum[:, :mid], log_sum[:, mid:]
                s = dot(k[:mid], qh, 1, 1)
                s_c = dot(k[mid:], qh[mid:], 1, 1)
                p_a = jnp.exp(jnp.where(allowed, s[:, :mid], -1e30) - log_a)
                p_b = jnp.exp(s[:, mid:] - log_b)
                p_c = jnp.exp(jnp.where(allowed, s_c, -1e30) - log_b)
                d_p = dot(v[:mid], dh, 1, 1)
                d_a, d_b = d_p[:, :mid], d_p[:, mid:]
                d_c = dot(v[mid:], dh[mid:], 1, 1)
                delta_a = jnp.sum(p_a * d_a, axis=0, keepdims=True)
                delta_b = jnp.sum(p_b * d_b + p_c * d_c, axis=0, keepdims=True)
                s_a = (p_a * (d_a - delta_a)).astype(bf16)
                s_b = (p_b * (d_b - delta_b)).astype(bf16)
                s_c = (p_c * (d_c - delta_b)).astype(bf16)
                s_ab = jnp.concatenate([s_a, s_b], axis=1)
                p_ab = jnp.concatenate([p_a.astype(bf16), p_b.astype(bf16)], axis=1)
                parts = [
                    dot(s_a, kh[:mid], 0, 0),
                    dot(jnp.concatenate([s_b, s_c], axis=0), kh, 0, 0),
                    dot(s_ab, qh),
                    dot(s_c, qh[mid:]),
                    dot(p_ab, dh),
                    dot(p_c.astype(bf16), dh[mid:]),
                ]
                total = [b if a is None else a + b for a, b in zip(total, parts)]
            low, high = slice(i * length, i * length + mid), slice(i * length + mid, (i + 1) * length)
            for j in range(3):
                d_qkv[low, at[j]] = total[2 * j].astype(bf16)
                d_qkv[high, at[j]] = total[2 * j + 1].astype(bf16)
        return carry

    lax.fori_loop(0, HEADS // 2, step, 0, unroll=6)


def qkv_kernel(normed1, d_qkv, keep, send):
    _, core, _, _ = where()
    width = normed1.shape[1]
    half = keep.shape[0]
    for m in range(width // STEP):
        block = dot(normed1[:, m * STEP : (m + 1) * STEP], d_qkv[...], 0, 0)
        for j in range(3):
            part = block[:, j * width : (j + 1) * width]
            at = j * width + m * STEP
            inside = at % half

            @pl.when(core == at // half)
            def _():
                keep[inside : inside + STEP, :] = part

            @pl.when(core != at // half)
            def _():
                send[inside : inside + STEP, :] = part.astype(bf16)


def rest_kernel(d_qkv, w_qkv, hidden0, d_hidden1, gain1, shifted_t, w_patch, part_in, short_in, facts, lat_keep, lat_send,
                keep, send, short, in_keep, in_send, extra):
    x, core, _, _ = where()
    width = hidden0.shape[1]
    items, done, span = lat_keep.shape
    feat = w_patch.shape[0]
    length = 2 * span
    in_keep[:, :done] = lat_keep[...]
    in_send[:, :done] = lat_send[...]
    d_normed1 = dot(d_qkv[...], w_qkv[...], 1, 1)
    unit, inverse_dev = centered(hidden0[...])
    short[...] = short_in[...]
    short[ROW["n1g"] : ROW["n1g"] + 1, :] = col_sum(d_normed1 * unit)
    short[ROW["n1s"] : ROW["n1s"] + 1, :] = col_sum(d_normed1)
    d0 = d_hidden1[...] + norm_pull(d_normed1, unit, inverse_dev, row_of(gain1))
    d_low = d0.astype(bf16)
    extra[...] = jnp.zeros(extra.shape, bf16)
    d_pos, whole = None, None
    for i in range(items):
        mine = d0[i * length : (i + 1) * length]
        d_pos = mine if d_pos is None else d_pos + mine
        item = col_sum(mine)
        whole = item if whole is None else whole + item
        extra[i : i + 1, :] = item.astype(bf16)
    extra[items : items + 1, :] = facts[...].astype(bf16)
    short[ROW["bp"] : ROW["bp"] + 1, :] = whole
    d_patch = dot(shifted_t[...], d_low)
    half = keep.shape[0]
    rest = 2 * half - d_pos.shape[0] - d_patch.shape[0]
    block = jnp.concatenate([d_pos, d_patch, jnp.zeros((rest, width), f32)], axis=0)
    split_by(core, block, keep, send.at[:half], half)
    short[...] = put_short(send, half, short[...])
    d_shift = dot(w_patch[...], d_low, 1, 1)
    for i in range(items):
        cols = slice(i * length, (i + 1) * length)
        moved = d_shift[:, cols]
        lane = lax.broadcasted_iota(jnp.int32, moved.shape, 1)
        back = jnp.where(lane == length - 1, 0.0, pltpu.roll(moved, length - 1, 1))
        grad = part_in[:, cols] + back
        in_keep[i, done:] = jnp.where(x == 0, grad[:, :span], grad[:, span:])
        in_send[i, done:] = jnp.where(x == 0, grad[:, span:], grad[:, :span])


def put_short(send, at, short):
    n = short.shape[0]
    high = short.astype(bf16)
    low = (short - high.astype(f32)).astype(bf16)
    send[at : at + n, :] = high
    send[at + n : at + 2 * n, :] = low
    return high.astype(f32) + low.astype(f32)


def take_short(came, at, n):
    return came[at : at + n, :].astype(f32) + came[at + n : at + 2 * n, :].astype(f32)


def split_sum(bit, pairs, kept, send):
    mine = my_bit(bit)
    n = 0
    for keep, came in pairs:
        for a in range(keep.shape[0]):
            kept[n] = keep[a, mine] + came[a, mine].astype(f32)
            send[n] = (keep[a, 1 - mine] + came[a, 1 - mine].astype(f32)).astype(bf16)
            n += 1


def stage_kernel(bits, counts, *refs):
    n = 2 * sum(counts)
    ins, outs = refs[:n], refs[n:]
    for i, (bit, count) in enumerate(zip(bits, counts)):
        pairs = [(ins[2 * j], ins[2 * j + 1]) for j in range(count)]
        ins = ins[2 * count :]
        split_sum(bit, pairs, outs[2 * i], outs[2 * i + 1])


def stage(line, name, *parts, after=(), cost=1):
    outs, args = [], []
    for bit, pairs in parts:
        _, _, b, w = pairs[0][0].shape
        total = sum(keep.shape[0] for keep, _ in pairs)
        outs += [((total, b, w), f32), ((total, b, w), bf16)]
        for pair in pairs:
            args += list(pair)
    bits, counts = tuple(p[0] for p in parts), tuple(len(p[1]) for p in parts)
    return line.call(partial(stage_kernel, bits, counts), outs, args, name, cost, 8, after=after, pinned=True)


def add_kernel(keep, came, *outs):
    at = 0
    for out in outs:
        n = out.shape[0]
        out[...] = keep[at : at + n, :] + came[at : at + n, :].astype(f32)
        at += n


def bulk0a_kernel(qk, qc, keep_a, send_a):
    x, _, _, _ = where()
    na = keep_a.shape[0]
    mine, away = pl.ds(pl.multiple_of(x * na, na), na), pl.ds(pl.multiple_of((1 - x) * na, na), na)
    keep_a[...] = qk[mine, :] + qc[mine, :].astype(f32)
    send_a[...] = (qk[away, :] + qc[away, :].astype(f32)).astype(bf16)


def bulk0b_kernel(low, qk, qc, ek, ec, lk, lc, short_in, keep_b, send_b, short):
    _, _, y, _ = where()
    nb = keep_b.shape[0]
    nq, nl = qk.shape[0], lk.shape[0]
    total = short_in[...] + take_short(lc, nl, short.shape[0])
    parts = [
        qk[low:nq, :] + qc[low:nq, :].astype(f32),
        ek[...] + ec[...].astype(f32),
        lk[...] + lc[:nl, :].astype(f32),
    ]
    block = jnp.concatenate(parts, axis=0)
    split_by(y, block, keep_b, send_b.at[:nb], nb)
    short[...] = put_short(send_b, nb, total)


def bulk1_kernel(ka, ca, kb, cb, short_in, keep_a, keep_b, send_a, send_b, short):
    x, _, y, _ = where()
    na, nb = keep_a.shape[0], keep_b.shape[0]
    ns = short.shape[0]
    total = short_in[...] + take_short(cb, 2 * nb, ns)
    for bit, n, k, c, keep, send in ((y, na, ka, ca, keep_a, send_a), (x, nb, kb, cb, keep_b, send_b)):
        mine, away = pl.ds(pl.multiple_of(bit * n, n), n), pl.ds(pl.multiple_of((1 - bit) * n, n), n)
        keep[...] = k[mine, :] + c[mine, :].astype(f32)
        send[:n, :] = (k[away, :] + c[away, :].astype(f32)).astype(bf16)
    short[...] = put_short(send_b, nb, total)


def quarter_of(block, at):
    out = block[0:4]
    for j in range(1, 4):
        out = jnp.where(at == j, block[4 * j : 4 * j + 4], out)
    return out


def high_low(rows):
    high = rows.astype(bf16).astype(f32)
    return jnp.concatenate([high, rows - high], axis=0).astype(bf16)


def bulk2_kernel(ka, ca, kb, cb, short_in, keep, send1, send2, send3, short):
    _, _, _, z = where()
    na, nb = ka.shape[0] // 4, kb.shape[0] // 4
    n = na + nb
    total = short_in[...] + take_short(cb, 4 * nb, short_in.shape[0])
    for m, out in enumerate((keep, send1, send2, send3)):
        at = z ^ m
        ra = pl.ds(pl.multiple_of(at * na, na), na)
        rb = pl.ds(pl.multiple_of(at * nb, nb), nb)
        out[:na, :] = (ka[ra, :] + ca[ra, :].astype(f32)).astype(out.dtype)
        out[na:n, :] = (kb[rb, :] + cb[rb, :].astype(f32)).astype(out.dtype)
        quarter = quarter_of(total, at)
        if m == 0:
            short[...] = jnp.concatenate([quarter, quarter], axis=0)
        else:
            both = high_low(quarter)
            out[n : n + 16, :] = jnp.concatenate([both, both], axis=0)


def bulk3_kernel(keep, c1, c2, c3, short_in, extra, piece):
    n = keep.shape[0]
    total = keep[...]
    quarter = short_in[0:4, :]
    for c in (c1, c2, c3):
        total = total + c[:n, :].astype(f32)
        both = c[n : n + 16, :].astype(f32)
        quarter = quarter + (both[0:4] + both[4:8])
    piece[:n, :] = total.astype(bf16)
    piece[n:, :] = jnp.concatenate([extra[...][0:8], high_low(quarter)], axis=0)


def join0_kernel(own, c1, c2, c3, part_a, part_b, short):
    _, _, _, z = where()
    na, nb = part_a.shape[0] // 4, part_b.shape[0] // 4
    quarters = []
    for m, c in enumerate((own, c1, c2, c3)):
        at = z ^ m
        part_a[pl.ds(pl.multiple_of(at * na, na), na), :] = c[:na, :]
        part_b[pl.ds(pl.multiple_of(at * nb, nb), nb), :] = c[na:, :]
        both = c[na + nb - 16 :, :].astype(f32)
        quarters.append((at, both[8:12] + both[12:16]))
    rows = []
    for j in range(4):
        row = quarters[0][1]
        for at, quarter in quarters[1:]:
            row = jnp.where(at == j, quarter, row)
        rows.append(row)
    short[...] = jnp.concatenate(rows, axis=0)


def join1_kernel(own_a, came_a, own_b, came_b, part_a, part_b):
    x, _, y, _ = where()
    n = own_a.shape[0]
    for bit, own, came, part in ((y, own_a, came_a, part_a), (x, own_b, came_b, part_b)):
        part[pl.ds(pl.multiple_of(bit * n, n), n), :] = own[...]
        part[pl.ds(pl.multiple_of((1 - bit) * n, n), n), :] = came[...]


def write_kernel(geo, first, jobs, *refs):
    n_out = 5
    quarters = refs[: len(jobs)]
    refs = refs[len(jobs) :]
    if not first:
        refs = refs[n_out:]
    write_end(write_start(geo, jobs, quarters, *refs))


def finish_kernel(geo, jobs, *refs):
    quarters = refs[: len(jobs)]
    own_b, came_b, core_b, fc_keep, fc_came = refs[len(jobs) : len(jobs) + 5]
    refs = refs[len(jobs) + 10 :]
    outs, (own_fc2, own_fc1, class_own, scalars, wide, facts, sems) = refs[:5], refs[5:]
    waits = write_start(geo, jobs, quarters, *outs, wide, sems)
    class_kernel(geo, own_b, came_b, core_b, quarters[1], class_own, scalars, facts)
    add_kernel(fc_keep, fc_came, own_fc2, own_fc1)
    write_end(waits)


def write_end(waits):
    for taken, move in waits:
        if taken is None:
            move.wait()
        else:
            pl.when(taken)(move.wait)


def write_start(geo, jobs, quarters, g_qkv, g_out, g_pos, g_head, g_patch, wide, sems):
    x, core, y, _ = where()
    width = g_out.shape[0]
    half_q, half_e, half_l = geo["half_q"], geo["half_e"], geo["half_l"]
    nb, ne = geo["nb"], geo["extra"]
    feat = g_patch.shape[0]
    at, sem = 0, 0
    waits = []

    def copy(rows, target):
        nonlocal sem
        c = pltpu.make_async_copy(wide.at[rows], target, sems.at[sem])
        sem += 1
        return c

    for quarter, (part, other_core, other_half) in zip(quarters, jobs):
        c = 1 - core if other_core else core
        n = quarter.shape[0]
        if part == "a":
            h = 1 - x if other_half else x
            wide[at : at + n, :] = quarter[...].astype(f32)
            for k in range(0, n, 128):
                q = c * half_q + h * n + k
                third, row = q // width, q % width
                target = g_qkv.at[
                    pl.ds(pl.multiple_of(row, 128), 128),
                    pl.ds(pl.multiple_of(third * width, 128), width),
                ]
                waits.append((None, copy(slice(at + k, at + k + 128), target)))
                waits[-1][1].start()
            at += n
        else:
            h = 1 - y if other_half else y
            for k in range(n // (nb + ne)):
                wide[at + k * nb : at + (k + 1) * nb, :] = quarter[
                    k * (nb + ne) : k * (nb + ne) + nb, :
                ].astype(f32)
            left = half_q - 2 * geo["na"]
            rows = n // (nb + ne) * nb
            for case_c in range(2):
                for case_h in range(2):
                    spans = []
                    if case_h == 0:
                        spans.append((0, left, "q", case_c * half_q + 2 * geo["na"]))
                        spans.append((left, rows - left, "e", case_c * half_e))
                    else:
                        spans.append((0, half_e - (rows - left), "e", case_c * half_e + rows - left))
                        spans.append((half_e - (rows - left), half_l, "l", case_c * half_l))
                    moves = []
                    for start, size, kind, place in spans:
                        pieces = {
                            "q": [(case_c * half_q + 2 * geo["na"], left, g_qkv)],
                            "e": [(0, width, g_out), (width, 2 * feat, g_head)],
                            "l": [(0, g_pos.shape[0], g_pos), (g_pos.shape[0], feat, g_patch)],
                        }[kind]
                        for low, long, ref in pieces:
                            a, b = max(place, low), min(place + size, low + long)
                            if a >= b:
                                continue
                            source = slice(at + start + a - place, at + start + b - place)
                            if kind == "q":
                                third, row = a // width, a % width
                                target = g_qkv.at[row : row + b - a, third * width : (third + 1) * width]
                            else:
                                target = ref.at[a - low : b - low]
                            moves.append(copy(source, target))
                    taken = (c == case_c) & (h == case_h)

                    @pl.when(taken)
                    def _(moves=moves):
                        for move in moves:
                            move.start()

                    waits += [(taken, move) for move in moves]
            at += rows
    return waits


def class_kernel(geo, q0, q1, q2, q3, class_own, scalars, facts):
    x, core, y, _ = where()
    nb, ne, items = geo["nb"], geo["extra"], geo["items"]
    rows = class_own.shape[0]
    me = lax.axis_index("dp") * 2 + x
    want = (me * rows + lax.broadcasted_iota(jnp.int32, (rows, 1), 0)).astype(f32)
    total = jnp.zeros(class_own.shape, f32)
    for q, c, h in ((q0, core, y), (q1, core, 1 - y), (q2, 1 - core, y), (q3, 1 - core, 1 - y)):
        for k in range(8):
            block = q[k * (nb + ne) + nb : (k + 1) * (nb + ne), :].astype(f32)
            fact = block[items : items + 1]
            facts[pl.ds((c * 2 + h) * 8 + k, 1), :] = fact
            for i in range(items):
                slot = fact[:, 9 + i : 10 + i] * 32 + fact[:, 9 + items + i : 10 + items + i]
                total = total + jnp.where(want == slot, 1.0, 0.0) * block[i : i + 1]
    class_own[...] = total
    every = facts[...]
    summed = col_sum(every)
    scale_sum = summed[:, 0:1] + summed[:, 1:2] + summed[:, 2:3]
    count = summed[:, 3:4] + summed[:, 4:5] + summed[:, 5:6]
    tops = every[:, 6:7] + every[:, 7:8] + every[:, 8:9]
    lane = lax.broadcasted_iota(jnp.int32, scalars.shape, 1)
    scalars[...] = jnp.where(lane == 0, scale_sum / count, jnp.max(tops, axis=0, keepdims=True))


class Cube:
    def __init__(self):
        self.size = lax.axis_size("dp") * lax.axis_size("seq")
        self.nbits = self.size.bit_length() - 1
        self.me = lax.axis_index("dp") * lax.axis_size("seq") + lax.axis_index("seq")
        self.bit = [(self.me >> k) & 1 for k in range(self.nbits)]

    def send(self, block, mask):
        return lax.ppermute(block, AXES, [(i, i ^ mask) for i in range(self.size)])

    def start(self, full, bits):
        rows = full.shape[0] >> len(bits)
        return full.reshape((2,) * len(bits) + (rows, full.shape[1])), list(bits)

    def scatter(self, block, left):
        for bit in list(left):
            axis = left.index(bit)
            mine = lax.dynamic_index_in_dim(block, self.bit[bit], axis, keepdims=False)
            away = lax.dynamic_index_in_dim(block, 1 - self.bit[bit], axis, keepdims=False)
            block = mine + self.send(away.astype(bf16), 1 << bit).astype(f32)
            left = [b for b in left if b != bit]
        return block

    def add_up(self, block, bits):
        for k in bits:
            block = block + self.send(block, 1 << k)
        return block

    def gather(self, block, bits):
        for k in reversed(bits):
            came = self.send(block, 1 << k)
            block = jnp.where(self.bit[k] == 0, jnp.stack([block, came]), jnp.stack([came, block]))
        return block


def local(
    patches, labels, valid_mask, class_slot, w_patch, b_patch, pos_embed, class_embed,
    norm1_gain, norm1_shift, w_qkv, w_out, norm2_gain, norm2_shift, w_fc1, b_fc1, w_fc2, b_fc2,
    final_gain, final_shift, w_head, b_head, cot_latent, cot_logdet,
):
    cube = Cube()
    line = Line()
    seq_n = lax.axis_size("seq")
    assert seq_n == 2
    seq = lax.axis_index("seq")
    held, span, feat = patches.shape
    items = held // seq_n
    length = span * seq_n
    width = w_out.shape[0]
    ff = w_fc1.shape[1]
    rows = items * length
    classes = class_embed.shape[0]
    chunk = ff // cube.size
    group = 2 * chunk
    fast = cube.size == 32

    runs = patches.transpose(0, 2, 1)
    cot_runs = cot_latent.transpose(0, 2, 1)
    valid_runs = valid_mask[:, None, :]
    w_head_t = w_head.T
    (packed,) = line.call(
        prep_kernel, [((items, 2 * feat + 8, span), f32)], [runs, cot_runs, valid_mask], "prep", 1, 1,
        places={0: HBM, 1: HBM, 2: HBM},
        scratch=[pltpu.VMEM((items, feat, span), bf16), pltpu.VMEM((held, span), jnp.int32),
                 pltpu.SemaphoreType.DMA((3,))],
    )
    came = cube.send(packed, 1)
    big = 2.0 * rows * width * ff
    firsts = line.call(
        fetch_kernel,
        [((items, feat, span), bf16), ((items, 16, width), bf16), ((width,), bf16), ((width,), bf16),
         ((width,), bf16), ((length, width), bf16), ((feat, width), bf16), (w_qkv.shape, bf16)],
        [labels, packed, runs, class_embed, b_patch, norm1_gain, norm1_shift, pos_embed, w_patch, w_qkv],
        "fetch", 1, 2, places={0: SMEM, 1: ANY} | {i: HBM for i in range(2, 10)},
        scratch=[pltpu.SemaphoreType.DMA((items + 7,))], tied=False,
    )
    w_qkv = firsts[-1]
    hidden0, normed1, qkv, shifted_t, attended, lse, w_out, w_fc1, w_fc2 = line.call(
        front_kernel,
        [((rows, width), f32), ((rows, width), bf16), ((rows, 3 * width), bf16), ((feat, rows), bf16),
         ((rows, width), bf16), ((items, HEADS, length), f32)]
        + [(w.shape, bf16) for w in (w_out, w_fc1, w_fc2)],
        [labels, came] + list(firsts) + [w_out, w_fc1, w_fc2],
        "front", 1, 6, places={0: SMEM} | {i: HBM for i in range(10, 13)},
        scratch=[pltpu.SemaphoreType.DMA((3,))],
    )
    n_short = 16
    (hidden1, normed2, act, slope, d_hidden2, part_in, lat_keep, lat_send, short, grad_head_t, facts) = line.call(
        middle_kernel,
        [((rows, width), f32), ((rows, width), bf16), ((rows, ff), bf16), ((rows, ff), bf16),
         ((rows, width), f32), ((feat, rows), f32), ((items, feat + 8, span), f32),
         ((items, feat + 8, span), f32), ((n_short, width), f32), ((2 * feat, width), f32),
         ((1, width), f32)],
        [cot_logdet, labels, class_slot, hidden0, attended, w_out, norm2_gain, norm2_shift, w_fc1, b_fc1,
         w_fc2, b_fc2, final_gain, final_shift, w_head_t, b_head, runs, cot_runs, valid_runs, came],
        "middle", 1, 8, places={0: SMEM, 1: SMEM, 2: SMEM},
    )
    groups = ff // (4 * group)
    pieces = [((groups, group, width), f32), ((groups, group, width), bf16)]

    def fc2_half(h):
        return line.call(partial(fc2_kernel, h), pieces, [act, d_hidden2], "fc2", 1, 4)

    def fc1_half(h, before):
        return line.call(
            partial(fc1_kernel, h),
            pieces + [((rows, width), f32), ((ff // width // 2, width), f32)],
            [d_hidden2, w_fc2, slope, normed2, w_fc1] + before, "fc1", 1, 6,
        )

    def four(block):
        return block.reshape(groups, 2, chunk, width)

    half_e, half_l, half_q = 448, 192, 3 * width // 2
    keep20, send20 = fc2_half(0)
    came20 = cube.send(send20, 2)
    keep21, send21 = fc2_half(1)
    came21 = cube.send(send21, 2)
    keep10, send10, total, bias0 = fc1_half(0, [])
    came10 = cube.send(send10, 2)
    if fast:
        k20, s20 = stage(line, "fc2_core", (0, [(four(keep20), four(came20))]))
        c20 = cube.send(s20, 1)
    keep11, send11, total, bias1 = fc1_half(1, [total])
    came11 = cube.send(send11, 2)
    if fast:
        k21, s21 = stage(line, "fc2_core", (0, [(four(keep21), four(came21))]))
    d_hidden1, short, ekeep, esend, d_attended = line.call(
        back_kernel,
        [((rows, width), f32), ((n_short, width), f32), ((half_e, width), f32), ((half_e, width), bf16),
         ((rows, width), bf16)],
        [d_hidden2, total, hidden1, norm2_gain, attended, w_out, short, bias0, bias1, grad_head_t],
        "back", 1, 6,
    )
    ecame = cube.send(esend, 2)

    def by_y(block):
        return block.reshape(2, 2, group, width)

    if fast:
        k10, s10 = stage(line, "fc1_core", (2, [(by_y(keep10), by_y(came10))]))
        c10 = cube.send(s10, 4)
        k11, s11 = stage(line, "fc1_core", (2, [(by_y(keep11), by_y(came11))]))
    (d_qkv,) = line.call(
        attention_back_kernel, [((rows, 3 * width), bf16)], [qkv, lse, d_attended],
        "attention_back", 1, 4,
    )
    qkeep, qsend = line.call(
        qkv_kernel, [((half_q, width), f32), ((half_q, width), bf16)], [normed1, d_qkv],
        "qkv_grad", 1, 6, after=[c20] if fast else [],
    )
    qcame = cube.send(qsend, 2)
    lkeep, lsend, short, back_keep, back_send, extra = line.call(
        rest_kernel,
        [((half_l, width), f32), ((half_l + 2 * n_short, width), bf16), ((n_short, width), f32),
         ((items, 2 * feat + 8, span), f32), ((items, 2 * feat + 8, span), f32), ((16, width), bf16)],
        [d_qkv, w_qkv, hidden0, d_hidden1, norm1_gain, shifted_t, w_patch, part_in, short, facts,
         lat_keep, lat_send],
        "rest", 3e10, 6, after=[c10] if fast else [],
    )
    lcame = cube.send(lsend, 2)

    if fast:
        ns2 = 2 * n_short

        def two(na, nb):
            return [((na, width), f32), ((nb, width), f32), ((na, width), bf16), ((nb + ns2, width), bf16),
                    ((n_short, width), f32)]

        na, nb = 512, 384
        ka, sa = line.call(
            bulk0a_kernel, [((na, width), f32), ((na, width), bf16)], [qkeep, qcame], "bulk0a", 1, 10
        )
        ca = cube.send(sa, 1)
        kb, sb, short = line.call(
            partial(bulk0b_kernel, 2 * na),
            [((nb, width), f32), ((nb + ns2, width), bf16), ((n_short, width), f32)],
            [qkeep, qcame, ekeep, ecame, lkeep, lcame, short], "bulk0b", 1, 10,
        )
        cb = cube.send(sb, 4)
        ka, kb, sa, sb, short = line.call(
            bulk1_kernel, two(256, 192), [ka, ca, kb, cb, short], "bulk1", 1, 6
        )
        ca, cb = cube.send(sa, 4), cube.send(sb, 1)
        na, nb, ne = 64, 48, 16
        n = na + nb
        keep, z1, z2, z3, quarter = line.call(
            bulk2_kernel,
            [((n, width), f32)] + [((n + ne, width), bf16)] * 3 + [((8, width), f32)],
            [ka, ca, kb, cb, short], "bulk2", 1, 4,
        )
        z1, z2, z3 = cube.send(z1, 8), cube.send(z2, 16), cube.send(z3, 24)
        c21, c11 = cube.send(tie(s21, keep), 1), cube.send(tie(s11, keep), 4)
        def next_y(block):
            return block.reshape(2, 2, chunk, width)

        k2, s2, k1, s1 = stage(
            line, "fc_second",
            (2, [(next_y(k20), next_y(c20)), (next_y(k21), next_y(c21))]),
            (0, [(next_y(k10), next_y(c10)), (next_y(k11), next_y(c11))]), cost=3e10,
        )
        c2, c1 = cube.send(s2, 4), cube.send(s1, 1)
        piece, = line.call(
            bulk3_kernel, [((n + ne, width), bf16)], [keep, z1, z2, z3, quarter, extra], "bulk3", 3e10, 4
        )
        g1, g2, g3 = cube.send(piece, 8), cube.send(piece, 16), cube.send(piece, 24)
        kf, sf = stage(
            line, "fc_third", (3, [(next_y(k2), next_y(c2)), (next_y(k1), next_y(c1))])
        )

        back_came = cube.send(tie(back_send, c2, c1), 1)
        part_a, part_b, short = line.call(
            join0_kernel, [((4 * na, width), bf16), ((4 * (nb + ne), width), bf16), ((n_short, width), f32)],
            [piece, g1, g2, g3], "join0", 1, 4, after=[back_came],
        )
        ca, cb = cube.send(part_a, 4), cube.send(part_b, 1)
        cf = cube.send(tie(sf, g1, g2, g3), 8)
        part_a, part_b = line.call(
            join1_kernel, [((8 * na, width), bf16), ((8 * (nb + ne), width), bf16)],
            [part_a, ca, part_b, cb], "join1", 1, 5,
        )
        ca, cb = cube.send(part_a, 1), cube.send(part_b, 4)
        xa, xb = cube.send(part_a, 2), cube.send(part_b, 2)
        geo = dict(na=8 * na, nb=nb, extra=ne, half_q=half_q, half_e=half_e, half_l=half_l, items=items)
        grads = write(
            line, geo, [("a", 0, 0), ("b", 0, 0)], [part_a, part_b], None, width, length, feat,
        )

        kf, sf = stage(line, "fc_fourth", (4, [(next_y(kf), next_y(cf))]))
        cf = cube.send(sf, 16)
        ya, yb = cube.send(ca, 2), cube.send(cb, 2)
        grads = write(
            line, geo, [("a", 1, 0), ("b", 1, 0), ("a", 0, 1), ("b", 0, 1)], [xa, xb, ca, cb], grads,
            width, length, feat,
        )
        g_qkv, g_out, g_pos, g_head_t, g_patch, own_fc2, own_fc1, class_own, scalars = finish(
            line, geo, [("a", 1, 1), ("b", 1, 1)], [ya, yb],
            [part_b, cb, xb, kf.reshape(2 * chunk, width), cf.reshape(2 * chunk, width)], grads,
            [(chunk, width), (chunk, width), (classes // cube.size, width), (1, 128)], cube.size,
        )
        mean, top = scalars[0, 0], scalars[0, 1]
    else:
        rest = [0] + list(range(2, cube.nbits))
        upper = list(range(cube.nbits - 1, 1, -1)) + [0]
        back_came = cube.send(back_send, 1)

        def owned(*parts):
            total = jnp.concatenate([k + c.astype(f32) for k, c in parts]).reshape(-1, width)
            return cube.scatter(*cube.start(total, upper))

        own_fc2 = owned((keep20, came20), (keep21, came21))
        own_fc1 = owned((keep10, came10), (keep11, came11))
        full = jnp.concatenate(
            [qkeep + qcame.astype(f32), ekeep + ecame.astype(f32), lkeep + lcame[:half_l].astype(f32)]
        )
        n_full = full.shape[0]
        full = jnp.pad(full, ((0, -n_full % (cube.size * 8)), (0, 0)))
        own = cube.scatter(*cube.start(full, upper))
        n_own = own.shape[0]
        got = cube.gather(jnp.concatenate([own.astype(bf16), extra]), [1] + upper)
        halves = got[..., :n_own, :].reshape(2, -1, width)[:, :n_full].astype(f32)
        short = cube.add_up(short, [1] + rest)
        q = halves[:, :half_q].reshape(3, width, width)
        g_qkv = jnp.concatenate([q[0], q[1], q[2]], axis=1)
        e = halves[:, half_q : half_q + half_e].reshape(-1, width)
        g_out, g_head_t = e[:width], e[width : width + 2 * feat]
        later = halves[:, half_q + half_e :].reshape(-1, width)
        g_pos, g_patch = later[:length], later[length : length + feat]
        extras = got[..., n_own : n_own + items + 1, :].reshape(cube.size, items + 1, width).astype(f32)
        sums = extras[:, :items].reshape(-1, width)
        facts = extras[:, items]
        mean = jnp.sum(facts[:, :3]) / jnp.sum(facts[:, 3:6])
        top = jnp.max(facts[:, 6] + facts[:, 7] + facts[:, 8])
        all_slots = (facts[:, 9 : 9 + items] * 32 + facts[:, 9 + items : 9 + 2 * items]).reshape(-1)
        own_rows = classes // cube.size
        wanted = (cube.me * own_rows + jnp.arange(own_rows)).astype(f32)
        hot = (wanted[:, None] == all_slots[None, :]).astype(bf16)
        class_own = dot(hot, sums.astype(bf16))

    out = jnp.where(
        seq == 0, jnp.concatenate([back_keep, back_came]), jnp.concatenate([back_came, back_keep])
    )
    latent_out = out[:, :feat].transpose(0, 2, 1)
    logdet_out = out[:, feat, 0]
    grad_in_out = out[:, feat + 8 :].transpose(0, 2, 1)
    b1_all = short[ROW["b1"] : ROW["b1"] + ff // width].reshape(-1)
    b1_own = lax.dynamic_slice_in_dim(b1_all, cube.me * chunk, chunk, 0)
    vec = {name: short[at] for name, at in ROW.items()}
    return (
        latent_out, logdet_out, grad_in_out, g_patch, vec["bp"], g_pos, class_own,
        vec["n1g"], vec["n1s"], g_qkv, g_out, vec["n2g"], vec["n2s"], own_fc1.T, b1_own, own_fc2,
        vec["b2"], vec["fg"], vec["fs"], g_head_t.T, vec["bh"][: 2 * feat], mean, top,
    )


def finish(line, geo, jobs, quarters, others, grads, shapes, devices):
    n = len(quarters)
    args = list(quarters) + list(others)
    args[0] = tie(args[0], line.last)
    vmem, hbm = pl.BlockSpec(memory_space=VMEM), pl.BlockSpec(memory_space=ANY)
    width = grads[1].shape[0]
    return pl.pallas_call(
        partial(finish_kernel, geo, jobs),
        out_shape=[jax.ShapeDtypeStruct(g.shape, f32) for g in grads]
        + [jax.ShapeDtypeStruct(shape, f32) for shape in shapes],
        in_specs=[vmem] * len(args) + [hbm] * len(grads),
        out_specs=[hbm] * len(grads) + [vmem] * len(shapes),
        scratch_shapes=[pltpu.VMEM((512 * n, width), f32), pltpu.VMEM((devices, width), f32),
                        pltpu.SemaphoreType.DMA((16 * n,))],
        input_output_aliases={len(args) + i: i for i in range(len(grads))},
        compiler_params=pltpu.CompilerParams(vmem_limit_bytes=14 * 2**20),
        cost_estimate=pl.CostEstimate(flops=1, bytes_accessed=1, transcendentals=0),
        name="finish",
    )(*args, *grads)


def write(line, geo, jobs, quarters, grads, width, length, feat, after=()):
    shapes = [(width, 3 * width), (width, width), (length, width), (2 * feat, width), (feat, width)]
    n = len(quarters)
    args = list(quarters)
    args[0] = tie(args[0], line.last, *after)
    aliases = {}
    if grads is not None:
        aliases = {n + i: i for i in range(len(shapes))}
        args += list(grads)
    grads = pl.pallas_call(
        partial(write_kernel, geo, grads is None, jobs),
        out_shape=[jax.ShapeDtypeStruct(s, f32) for s in shapes],
        in_specs=[pl.BlockSpec(memory_space=VMEM)] * n + [pl.BlockSpec(memory_space=ANY)] * len(aliases),
        out_specs=[pl.BlockSpec(memory_space=ANY)] * len(shapes),
        scratch_shapes=[pltpu.VMEM((512 * n, width), f32), pltpu.SemaphoreType.DMA((16 * n,))],
        input_output_aliases=aliases,
        compiler_params=pltpu.CompilerParams(vmem_limit_bytes=(2 * n + 4) * 2**20),
        cost_estimate=pl.CostEstimate(flops=10**10, bytes_accessed=1, transcendentals=0),
        name="write",
    )(*args)
    line.last = grads[-1]
    return grads


def solution(mesh):
    run, item, whole = P("dp", "seq", None), P("dp"), P()
    placed = (run, item, P("dp", "seq")) + (whole,) * 19 + (run, item)
    owned = P(AXES)
    return jax.shard_map(
        local,
        mesh=mesh,
        in_specs=placed,
        out_specs=(run, item, run, whole, whole, whole, P(AXES, None), whole, whole, whole, whole,
                   whole, whole, P(None, AXES), owned, P(AXES, None)) + (whole,) * 7,
        check_vma=False,
    )
```

```python
import math
from functools import partial

import jax
import jax.numpy as jnp
from jax import lax
from jax.experimental import pallas as pl
from jax.experimental.pallas import tpu as pltpu
from jax.sharding import PartitionSpec as P

HEADS = 12
EPS = 1e-05
GELU_A = math.sqrt(2.0 / math.pi)
GELU_B = 0.044715
bf16 = jnp.bfloat16
f32 = jnp.float32
AXES = ("dp", "seq")
ROW = dict(bp=0, n1g=1, n1s=2, n2g=3, n2s=4, b2=5, fg=6, fs=7, bh=8, b1=9)


def dot(left, right, a=1, b=0):
    return lax.dot_general(
        left, right, (((a,), (b,)), ((), ())), preferred_element_type=f32
    )


SMEM, VMEM, ANY, HBM = pltpu.SMEM, pltpu.VMEM, pl.ANY, pltpu.HBM


class Line:
    def __init__(self):
        self.last = None

    def call(self, body, outs, args, name, flops, limit, places=None, scratch=(), after=(), tied=True, pinned=True):
        places = places or {}
        args = list(args)
        after = tuple(after) + ((self.last,) if self.last is not None else ())
        if after and tied:
            at = max(i for i in range(len(args)) if places.get(i, VMEM) is VMEM)
            args[at] = tie(args[at], *after)
        specs = [pl.BlockSpec(memory_space=places.get(i, VMEM)) for i in range(len(args))]
        for i, place in places.items():
            if place is HBM:
                args[i] = pltpu.with_memory_space_constraint(args[i], HBM)
        got = pl.pallas_call(
            body,
            out_shape=[pltpu.VMEM(s, d) if pinned else jax.ShapeDtypeStruct(s, d) for s, d in outs],
            in_specs=specs,
            out_specs=[pl.BlockSpec(memory_space=VMEM)] * len(outs),
            scratch_shapes=list(scratch),
            compiler_params=pltpu.CompilerParams(vmem_limit_bytes=int(limit * 2**20)),
            cost_estimate=pl.CostEstimate(flops=int(flops), bytes_accessed=1, transcendentals=0),
            name=name,
        )(*args)
        self.last = got[0]
        return got


def tie(value, *others):
    return lax.optimization_barrier((value,) + others)[0]


def where():
    dp = lax.axis_index("dp")
    return lax.axis_index("seq"), dp & 1, (dp >> 1) & 1, dp >> 2


def my_bit(bit):
    return lax.axis_index("seq") if bit == 0 else (lax.axis_index("dp") >> (bit - 1)) & 1


def row_of(ref):
    return ref[...].reshape(1, ref.shape[0]).astype(f32)


def centered(hidden):
    center = hidden - jnp.mean(hidden, axis=-1, keepdims=True)
    spread = jnp.mean(center * center, axis=-1, keepdims=True)
    inverse = lax.rsqrt(spread + EPS)
    return center * inverse, inverse


def norm_pull(grad, unit, inverse, gain):
    scaled = grad * gain
    mean = jnp.mean(scaled, axis=-1, keepdims=True)
    along = jnp.mean(scaled * unit, axis=-1, keepdims=True)
    return inverse * (scaled - mean - unit * along)


def col_sum(values):
    return jnp.sum(values, axis=0, keepdims=True)


def both_halves(seq, own, came):
    low = jnp.where(seq == 0, own, came)
    high = jnp.where(seq == 0, came, own)
    return jnp.concatenate([low, high], axis=1)


def prep_kernel(runs, cot_runs, valid, out, part, mask, sems):
    x, _, _, _ = where()
    items = out.shape[0]
    feat, span = runs.shape[1:]
    theirs = pl.ds((1 - x) * items, items)
    copies = [
        pltpu.make_async_copy(runs.at[theirs], part, sems.at[0]),
        pltpu.make_async_copy(cot_runs.at[theirs], out.at[:, feat : 2 * feat], sems.at[1]),
        pltpu.make_async_copy(valid, mask, sems.at[2]),
    ]
    for copy in copies:
        copy.start()
    for copy in copies:
        copy.wait()
    out[:, :feat] = part[...].astype(f32)
    for i in range(items):
        row = mask[pl.ds((1 - x) * items + i, 1), :].astype(f32)
        out[i, 2 * feat :] = jnp.broadcast_to(row, (out.shape[1] - 2 * feat, span))


def fetch_kernel(labels, sent, runs_in, class_embed, b_patch_in, gain_in, shift_in, pos_in, w_patch_in, w_qkv_in,
                 runs, class_rows, b_patch, gain, shift, pos, w_patch, w_qkv, sems):
    x, _, _, _ = where()
    items = runs.shape[0]
    quarter = w_qkv.shape[0] // 4
    parts = [pl.ds(j * quarter, quarter) for j in range(4)]
    pairs = [(w_qkv_in.at[part], w_qkv.at[part]) for part in parts] + [(runs_in.at[pl.ds(x * items, items)], runs)]
    for i in range(items):
        tile = pl.multiple_of(labels[x * items + i] // 16 * 16, 16)
        pairs.append((class_embed.at[pl.ds(tile, 16)], class_rows.at[i]))
    pairs += [(b_patch_in, b_patch), (gain_in, gain), (shift_in, shift), (w_patch_in, w_patch), (pos_in, pos)]
    copies = [pltpu.make_async_copy(*pair, sems.at[n]) for n, pair in enumerate(pairs)]
    for copy in copies:
        copy.start()
    for copy in copies:
        copy.wait()


def front_kernel(labels, came, runs, class_rows, b_patch, gain, shift, pos, w_patch, w_qkv,
                 w_out_in, w_fc1_in, w_fc2_in,
                 hidden0, normed1, qkv, shifted_t, attended, lse, w_out, w_fc1, w_fc2, sems):
    x, _, _, _ = where()
    items = came.shape[0]
    feat = w_patch.shape[0]
    length, width = pos.shape
    copies = []
    for source, target in ((w_out_in, w_out), (w_fc1_in, w_fc1), (w_fc2_in, w_fc2)):
        copies.append(pltpu.make_async_copy(source, target, sems.at[len(copies)]))
        copies[-1].start()
    gain_row, shift_row, bias = row_of(gain), row_of(shift), row_of(b_patch)
    at_row = lax.broadcasted_iota(jnp.int32, (16, width), 0)
    for i in range(items):
        rows = slice(i * length, (i + 1) * length)
        whole = both_halves(x, runs[i].astype(f32), came[i, :feat])
        lane = lax.broadcasted_iota(jnp.int32, whole.shape, 1)
        moved = jnp.where(lane == 0, 0.0, pltpu.roll(whole, 1, 1)).astype(bf16)
        shifted_t[:, rows] = moved
        mine = at_row == labels[x * items + i] % 16
        base = bias + col_sum(jnp.where(mine, class_rows[i].astype(f32), 0.0))
        h0 = dot(moved, w_patch[...], 0, 0) + base + pos[...].astype(f32)
        hidden0[rows, :] = h0
        unit, _ = centered(h0)
        normed1[rows, :] = (unit * gain_row + shift_row).astype(bf16)
    for j in range(3):
        cols = slice(j * width, (j + 1) * width)
        qkv[:, cols] = dot(normed1[...], w_qkv[:, cols]).astype(bf16)
    mid = length // 2
    allowed = lower_keys(mid)

    def step(p, carry):
        for i in range(items):
            rows = slice(i * length, (i + 1) * length)
            at = [pl.ds(pl.multiple_of(j * width + p * 128, 128), 128) for j in range(3)]
            q, k, v = (qkv[rows, at[j]] for j in range(3))
            first = lax.broadcasted_iota(jnp.int32, q.shape, 1) < 64
            v_t = v.T
            outs = []
            for h in range(2):
                mine = first if h == 0 else ~first
                qh = jnp.where(mine, q * 0.125, jnp.zeros_like(q))
                v_h = v_t[h * 64 : (h + 1) * 64]
                s = dot(k[:mid], qh, 1, 1)
                s_a, s_b = jnp.where(allowed, s[:, :mid], -1e30), s[:, mid:]
                s_c = jnp.where(allowed, dot(k[mid:], qh[mid:], 1, 1), -1e30)
                top_a = jnp.max(s_a, axis=0, keepdims=True)
                top_b = jnp.max(jnp.maximum(s_b, s_c), axis=0, keepdims=True)
                e_a, e_b, e_c = jnp.exp(s_a - top_a), jnp.exp(s_b - top_b), jnp.exp(s_c - top_b)
                total_a = jnp.sum(e_a, axis=0, keepdims=True)
                total_b = jnp.sum(e_b + e_c, axis=0, keepdims=True)
                lse[i, pl.ds(p * 2 + h, 1), :] = jnp.concatenate(
                    [top_a + jnp.log(total_a), top_b + jnp.log(total_b)], axis=1
                )
                part_a, part_b = 1.0 / total_a, 1.0 / total_b
                p_ab = jnp.concatenate([(e_a * part_a).astype(bf16), (e_b * part_b).astype(bf16)], axis=1)
                out = dot(v_h[:, :mid], p_ab)
                late = out[:, mid:] + dot(v_h[:, mid:], (e_c * part_b).astype(bf16))
                outs.append(jnp.concatenate([out[:, :mid], late], axis=1))
            attended[rows, at[0]] = jnp.concatenate(outs, axis=0).T.astype(bf16)
        return carry

    lax.fori_loop(0, HEADS // 2, step, 0, unroll=3)
    for copy in copies:
        copy.wait()


def middle_kernel(det, labels, class_slot, hidden0, attended, w_out, gain2, shift2, w_fc1, b_fc1, w_fc2, b_fc2,
                  gainf, shiftf, w_head_t, b_head, runs, cot_runs, valid_runs, came,
                  hidden1, normed2, act, slope, d_hidden2, part_in, lat_keep, lat_send,
                  short, grad_head_t, facts):
    x, _, _, _ = where()
    items = came.shape[0]
    feat = runs.shape[1]
    width = w_out.shape[0]
    span = came.shape[2]
    length = 2 * span
    hidden1[...] = hidden0[...] + dot(attended[...], w_out[...])
    gain, shift = row_of(gain2), row_of(shift2)
    for i in range(items):
        rows = slice(i * length, (i + 1) * length)
        unit, _ = centered(hidden1[rows, :])
        normed2[rows, :] = (unit * gain + shift).astype(bf16)
    total = None
    for j in range(w_fc1.shape[1] // width):
        cols = slice(j * width, (j + 1) * width)
        up = dot(normed2[...], w_fc1[:, cols]) + b_fc1[cols].reshape(1, width).astype(f32)
        square = up * up
        half = 0.5 * jnp.tanh(up * (GELU_A + GELU_A * GELU_B * square)) + 0.5
        value = up * half
        act[:, cols] = value.astype(bf16)
        slope[:, cols] = (
            half + 2.0 * value * (1.0 - half) * (GELU_A + 3.0 * GELU_A * GELU_B * square)
        ).astype(bf16)
        part = dot(act[:, cols], w_fc2[cols, :])
        total = part if total is None else total + part
    hidden2 = hidden1[...] + total + row_of(b_fc2)
    unit, inverse_dev = centered(hidden2)
    gain = row_of(gainf)
    normed3 = (unit * gain + row_of(shiftf)).astype(bf16)
    bias = jnp.broadcast_to(row_of(b_head), (8, 2 * feat)).T[:, :1]
    head = dot(w_head_t[...], normed3, 1, 1) + bias
    short[...] = jnp.zeros(short.shape, f32)
    d_heads = []
    sums = [jnp.zeros((1, 1), f32), jnp.zeros((1, 1), f32), jnp.full((1, 1), -1e30, f32)]
    for i in range(items):
        cols = slice(i * length, (i + 1) * length)
        source = x * items + i
        given = both_halves(x, runs[source].astype(f32), came[i, :feat])
        cot = both_halves(x, cot_runs[source], came[i, feat : 2 * feat])
        valid = both_halves(
            x, valid_runs[source].astype(f32), came[i, 2 * feat : 2 * feat + 1]
        )
        shift_part = head[:feat, cols]
        log_scale = head[feat:, cols]
        inverse = jnp.exp(-log_scale)
        moved = (given - shift_part) * inverse
        latent = valid * moved + (1.0 - valid) * given
        d_moved = valid * cot
        d_heads.append(
            jnp.concatenate(
                [-d_moved * inverse, -d_moved * moved - valid * det[source]], axis=0
            ).astype(bf16)
        )
        part_in[:, cols] = cot * (1.0 - valid) + d_moved * inverse
        counted = valid * log_scale
        item_sum = jnp.sum(jnp.sum(counted, axis=1, keepdims=True), axis=0, keepdims=True)
        sums[0] = sums[0] + item_sum
        sums[1] = sums[1] + jnp.sum(valid, axis=1, keepdims=True) * feat
        tops = jnp.where(valid > 0, log_scale, -1e30)
        tops = jnp.max(jnp.max(tops, axis=1, keepdims=True), axis=0, keepdims=True)
        sums[2] = jnp.maximum(sums[2], tops)
        low, high = latent[:, :span], latent[:, span:]
        logdet = jnp.broadcast_to(-item_sum, (8, span))
        lat_keep[i, :feat] = jnp.where(x == 0, low, high)
        lat_send[i, :feat] = jnp.where(x == 0, high, low)
        lat_keep[i, feat:] = logdet
        lat_send[i, feat:] = logdet
    lane = lax.broadcasted_iota(jnp.int32, facts.shape, 1)
    row = jnp.zeros(facts.shape, f32)
    for k, value in enumerate(sums):
        for j in range(3):
            piece = value.astype(bf16).astype(f32)
            value = value - piece
            row = jnp.where(lane == 3 * k + j, piece, row)
    for i in range(items):
        slot = class_slot[labels[x * items + i]]
        row = jnp.where(lane == 9 + i, (slot // 32).astype(f32), row)
        row = jnp.where(lane == 9 + items + i, (slot % 32).astype(f32), row)
    facts[...] = row
    d_head = jnp.concatenate(d_heads, axis=1)
    grad_head_t[...] = dot(d_head, normed3)
    short[ROW["bh"] : ROW["bh"] + 1, : 2 * feat] = dot(
        jnp.ones((8, d_head.shape[1]), bf16), d_head, 1, 1
    )[:1]
    d_normed3 = dot(d_head, w_head_t[...], 0, 0)
    short[ROW["fg"] : ROW["fg"] + 1, :] = col_sum(d_normed3 * unit)
    short[ROW["fs"] : ROW["fs"] + 1, :] = col_sum(d_normed3)
    pulled = norm_pull(d_normed3, unit, inverse_dev, gain)
    d_hidden2[...] = pulled
    short[ROW["b2"] : ROW["b2"] + 1, :] = col_sum(pulled.astype(bf16).astype(f32))


def split_by(bit, block, keep, send, half):
    low, high = block[:half], block[half:]
    keep[...] = jnp.where(bit == 0, low, high).astype(keep.dtype)
    send[...] = jnp.where(bit == 0, high, low).astype(send.dtype)


def split_groups(core, block, first, keep, send):
    group = keep.shape[1]
    for k in range(block.shape[0] // (2 * group)):
        rows = block[2 * group * k : 2 * group * (k + 1)]
        split_by(core, rows, keep.at[first + k], send.at[first + k], group)


STEP = 384


def fc2_kernel(first, act, d_hidden2, keep, send):
    _, core, _, _ = where()
    d_mlp = d_hidden2[...].astype(bf16)
    for j in range(2 * keep.shape[0] * keep.shape[1] // STEP):
        at = (first + j) * STEP
        block = dot(act[:, at : at + STEP], d_mlp, 0, 0)
        split_groups(core, block, j * STEP // (2 * keep.shape[1]), keep, send)


def fc1_kernel(half, d_hidden2, w_fc2, slope, normed2, w_fc1, *refs):
    before, (keep, send, total_out, bias) = refs[:-4], refs[-4:]
    _, core, _, _ = where()
    width = normed2.shape[1]
    d_mlp = d_hidden2[...].astype(bf16)
    total = before[0][...] if before else None
    count = w_fc1.shape[1] // 2 // width
    for j in range(count):
        at = (half * count + j) * width
        cols = slice(at, at + width)
        d_up = (dot(d_mlp, w_fc2[cols, :], 1, 1) * slope[:, cols].astype(f32)).astype(bf16)
        bias[j : j + 1, :] = col_sum(d_up.astype(f32))
        for m in range(width // STEP):
            block = dot(d_up[:, m * STEP : (m + 1) * STEP], normed2[...], 0, 0)
            split_groups(core, block, (j * width + m * STEP) // (2 * keep.shape[1]), keep, send)
        part = dot(d_up, w_fc1[:, cols], 1, 1)
        total = part if total is None else total + part
    total_out[...] = total


def back_kernel(d_hidden2, total_in, hidden1, gain2, attended, w_out, short_in, bias_a, bias_b, grad_head_t,
                d_hidden1, short, out_keep, out_send, d_attended):
    _, core, _, _ = where()
    width = w_out.shape[0]
    short[...] = short_in[...]
    n = bias_a.shape[0]
    short[ROW["b1"] : ROW["b1"] + n, :] = bias_a[...]
    short[ROW["b1"] + n : ROW["b1"] + 2 * n, :] = bias_b[...]
    unit, inverse_dev = centered(hidden1[...])
    total = total_in[...]
    short[ROW["n2g"] : ROW["n2g"] + 1, :] = col_sum(total * unit)
    short[ROW["n2s"] : ROW["n2s"] + 1, :] = col_sum(total)
    h1 = d_hidden2[...] + norm_pull(total, unit, inverse_dev, row_of(gain2))
    d_hidden1[...] = h1
    d_out = h1.astype(bf16)
    d_attended[...] = dot(d_out, w_out[...], 1, 1).astype(bf16)
    grad_out = dot(attended[...], d_out, 0, 0)
    half = out_keep.shape[0]
    rest = 2 * half - grad_out.shape[0] - grad_head_t.shape[0]
    block = jnp.concatenate([grad_out, grad_head_t[...], jnp.zeros((rest, width), f32)], axis=0)
    split_by(core, block, out_keep, out_send, half)


def lower_keys(n):
    key_at = lax.broadcasted_iota(jnp.int32, (n, n), 0)
    return key_at <= lax.broadcasted_iota(jnp.int32, (n, n), 1)


def attention_back_kernel(qkv, lse, d_attended, d_qkv):
    rows_all, width = d_attended.shape
    items = lse.shape[0]
    length = rows_all // items
    mid = length // 2
    allowed = lower_keys(mid)

    def step(p, carry):
        for i in range(items):
            rows = slice(i * length, (i + 1) * length)
            at = [pl.ds(pl.multiple_of(j * width + p * 128, 128), 128) for j in range(3)]
            q, k, v = (qkv[rows, at[j]] for j in range(3))
            q = q * 0.125
            d_o = d_attended[rows, at[0]]
            first = lax.broadcasted_iota(jnp.int32, q.shape, 1) < 64
            none = jnp.zeros_like(q)
            total = [None] * 6
            for h in range(2):
                mine = first if h == 0 else ~first
                qh = jnp.where(mine, q, none)
                kh = jnp.where(mine, k * 0.125, none)
                dh = jnp.where(mine, d_o, none)
                log_sum = lse[i, pl.ds(p * 2 + h, 1), :]
                log_a, log_b = log_sum[:, :mid], log_sum[:, mid:]
                s = dot(k[:mid], qh, 1, 1)
                s_c = dot(k[mid:], qh[mid:], 1, 1)
                p_a = jnp.exp(jnp.where(allowed, s[:, :mid], -1e30) - log_a)
                p_b = jnp.exp(s[:, mid:] - log_b)
                p_c = jnp.exp(jnp.where(allowed, s_c, -1e30) - log_b)
                d_p = dot(v[:mid], dh, 1, 1)
                d_a, d_b = d_p[:, :mid], d_p[:, mid:]
                d_c = dot(v[mid:], dh[mid:], 1, 1)
                delta_a = jnp.sum(p_a * d_a, axis=0, keepdims=True)
                delta_b = jnp.sum(p_b * d_b + p_c * d_c, axis=0, keepdims=True)
                s_a = (p_a * (d_a - delta_a)).astype(bf16)
                s_b = (p_b * (d_b - delta_b)).astype(bf16)
                s_c = (p_c * (d_c - delta_b)).astype(bf16)
                s_ab = jnp.concatenate([s_a, s_b], axis=1)
                p_ab = jnp.concatenate([p_a.astype(bf16), p_b.astype(bf16)], axis=1)
                parts = [
                    dot(s_a, kh[:mid], 0, 0),
                    dot(jnp.concatenate([s_b, s_c], axis=0), kh, 0, 0),
                    dot(s_ab, qh),
                    dot(s_c, qh[mid:]),
                    dot(p_ab, dh),
                    dot(p_c.astype(bf16), dh[mid:]),
                ]
                total = [b if a is None else a + b for a, b in zip(total, parts)]
            low, high = slice(i * length, i * length + mid), slice(i * length + mid, (i + 1) * length)
            for j in range(3):
                d_qkv[low, at[j]] = total[2 * j].astype(bf16)
                d_qkv[high, at[j]] = total[2 * j + 1].astype(bf16)
        return carry

    lax.fori_loop(0, HEADS // 2, step, 0, unroll=6)


def qkv_kernel(normed1, d_qkv, keep, send):
    _, core, _, _ = where()
    width = normed1.shape[1]
    half = keep.shape[0]
    for m in range(width // STEP):
        block = dot(normed1[:, m * STEP : (m + 1) * STEP], d_qkv[...], 0, 0)
        for j in range(3):
            part = block[:, j * width : (j + 1) * width]
            at = j * width + m * STEP
            inside = at % half

            @pl.when(core == at // half)
            def _():
                keep[inside : inside + STEP, :] = part

            @pl.when(core != at // half)
            def _():
                send[inside : inside + STEP, :] = part.astype(bf16)


def rest_kernel(items, d_qkv, w_qkv, hidden0, d_hidden1, gain1, shifted_t, short_in, facts,
                keep, send, short, d_low_out, extra):
    _, core, _, _ = where()
    width = hidden0.shape[1]
    length = hidden0.shape[0] // items
    d_normed1 = dot(d_qkv[...], w_qkv[...], 1, 1)
    unit, inverse_dev = centered(hidden0[...])
    short[...] = short_in[...]
    short[ROW["n1g"] : ROW["n1g"] + 1, :] = col_sum(d_normed1 * unit)
    short[ROW["n1s"] : ROW["n1s"] + 1, :] = col_sum(d_normed1)
    d0 = d_hidden1[...] + norm_pull(d_normed1, unit, inverse_dev, row_of(gain1))
    d_low = d0.astype(bf16)
    d_low_out[...] = d_low
    extra[...] = jnp.zeros(extra.shape, bf16)
    d_pos, whole = None, None
    for i in range(items):
        mine = d0[i * length : (i + 1) * length]
        d_pos = mine if d_pos is None else d_pos + mine
        item = col_sum(mine)
        whole = item if whole is None else whole + item
        extra[i : i + 1, :] = item.astype(bf16)
    extra[items : items + 1, :] = facts[...].astype(bf16)
    short[ROW["bp"] : ROW["bp"] + 1, :] = whole
    d_patch = dot(shifted_t[...], d_low)
    half = keep.shape[0]
    rest = 2 * half - d_pos.shape[0] - d_patch.shape[0]
    block = jnp.concatenate([d_pos, d_patch, jnp.zeros((rest, width), f32)], axis=0)
    split_by(core, block, keep, send.at[:half], half)
    short[...] = put_short(send, half, short[...])


def inputs_kernel(d_low, w_patch, part_in, lat_keep, lat_send, in_keep, in_send):
    x, _, _, _ = where()
    items, done, span = lat_keep.shape
    length = 2 * span
    in_keep[:, :done] = lat_keep[...]
    in_send[:, :done] = lat_send[...]
    d_shift = dot(w_patch[...], d_low[...], 1, 1)
    for i in range(items):
        cols = slice(i * length, (i + 1) * length)
        moved = d_shift[:, cols]
        lane = lax.broadcasted_iota(jnp.int32, moved.shape, 1)
        back = jnp.where(lane == length - 1, 0.0, pltpu.roll(moved, length - 1, 1))
        grad = part_in[:, cols] + back
        in_keep[i, done:] = jnp.where(x == 0, grad[:, :span], grad[:, span:])
        in_send[i, done:] = jnp.where(x == 0, grad[:, span:], grad[:, :span])


def put_short(send, at, short):
    n = short.shape[0]
    high = short.astype(bf16)
    low = (short - high.astype(f32)).astype(bf16)
    send[at : at + n, :] = high
    send[at + n : at + 2 * n, :] = low
    return high.astype(f32) + low.astype(f32)


def take_short(came, at, n):
    return came[at : at + n, :].astype(f32) + came[at + n : at + 2 * n, :].astype(f32)


def split_sum(bit, pairs, kept, send):
    mine = my_bit(bit)
    n = 0
    for keep, came in pairs:
        for a in range(keep.shape[0]):
            kept[n] = keep[a, mine] + came[a, mine].astype(f32)
            send[n] = (keep[a, 1 - mine] + came[a, 1 - mine].astype(f32)).astype(bf16)
            n += 1


def stage_kernel(bits, counts, *refs):
    n = 2 * sum(counts)
    ins, outs = refs[:n], refs[n:]
    for i, (bit, count) in enumerate(zip(bits, counts)):
        pairs = [(ins[2 * j], ins[2 * j + 1]) for j in range(count)]
        ins = ins[2 * count :]
        split_sum(bit, pairs, outs[2 * i], outs[2 * i + 1])


def stage(line, name, *parts, after=(), cost=1):
    outs, args = [], []
    for bit, pairs in parts:
        _, _, b, w = pairs[0][0].shape
        total = sum(keep.shape[0] for keep, _ in pairs)
        outs += [((total, b, w), f32), ((total, b, w), bf16)]
        for pair in pairs:
            args += list(pair)
    bits, counts = tuple(p[0] for p in parts), tuple(len(p[1]) for p in parts)
    return line.call(partial(stage_kernel, bits, counts), outs, args, name, cost, 8, after=after, pinned=True)


def add_kernel(keep, came, *outs):
    at = 0
    for out in outs:
        n = out.shape[0]
        out[...] = keep[at : at + n, :] + came[at : at + n, :].astype(f32)
        at += n


def bulk0a_kernel(qk, qc, keep_a, send_a):
    x, _, _, _ = where()
    na = keep_a.shape[0]
    mine, away = pl.ds(pl.multiple_of(x * na, na), na), pl.ds(pl.multiple_of((1 - x) * na, na), na)
    keep_a[...] = qk[mine, :] + qc[mine, :].astype(f32)
    send_a[...] = (qk[away, :] + qc[away, :].astype(f32)).astype(bf16)


def bulk0b_kernel(low, qk, qc, ek, ec, lk, lc, short_in, keep_b, send_b, short):
    _, _, y, _ = where()
    nb = keep_b.shape[0]
    nq, nl = qk.shape[0], lk.shape[0]
    total = short_in[...] + take_short(lc, nl, short.shape[0])
    parts = [
        qk[low:nq, :] + qc[low:nq, :].astype(f32),
        ek[...] + ec[...].astype(f32),
        lk[...] + lc[:nl, :].astype(f32),
    ]
    block = jnp.concatenate(parts, axis=0)
    split_by(y, block, keep_b, send_b.at[:nb], nb)
    short[...] = put_short(send_b, nb, total)


def bulk1_kernel(ka, ca, kb, cb, short_in, keep_a, keep_b, send_a, send_b, short):
    x, _, y, _ = where()
    na, nb = keep_a.shape[0], keep_b.shape[0]
    ns = short.shape[0]
    total = short_in[...] + take_short(cb, 2 * nb, ns)
    for bit, n, k, c, keep, send in ((y, na, ka, ca, keep_a, send_a), (x, nb, kb, cb, keep_b, send_b)):
        mine, away = pl.ds(pl.multiple_of(bit * n, n), n), pl.ds(pl.multiple_of((1 - bit) * n, n), n)
        keep[...] = k[mine, :] + c[mine, :].astype(f32)
        send[:n, :] = (k[away, :] + c[away, :].astype(f32)).astype(bf16)
    short[...] = put_short(send_b, nb, total)


def quarter_of(block, at):
    out = block[0:4]
    for j in range(1, 4):
        out = jnp.where(at == j, block[4 * j : 4 * j + 4], out)
    return out


def high_low(rows):
    high = rows.astype(bf16).astype(f32)
    return jnp.concatenate([high, rows - high], axis=0).astype(bf16)


def bulk2_kernel(ka, ca, kb, cb, short_in, keep, send1, send2, send3, short):
    _, _, _, z = where()
    na, nb = ka.shape[0] // 4, kb.shape[0] // 4
    n = na + nb
    total = short_in[...] + take_short(cb, 4 * nb, short_in.shape[0])
    for m, out in enumerate((keep, send1, send2, send3)):
        at = z ^ m
        ra = pl.ds(pl.multiple_of(at * na, na), na)
        rb = pl.ds(pl.multiple_of(at * nb, nb), nb)
        out[:na, :] = (ka[ra, :] + ca[ra, :].astype(f32)).astype(out.dtype)
        out[na:n, :] = (kb[rb, :] + cb[rb, :].astype(f32)).astype(out.dtype)
        quarter = quarter_of(total, at)
        if m == 0:
            short[...] = jnp.concatenate([quarter, quarter], axis=0)
        else:
            both = high_low(quarter)
            out[n : n + 16, :] = jnp.concatenate([both, both], axis=0)


def bulk3_kernel(keep, c1, c2, c3, short_in, extra, piece):
    n = keep.shape[0]
    total = keep[...]
    quarter = short_in[0:4, :]
    for c in (c1, c2, c3):
        total = total + c[:n, :].astype(f32)
        both = c[n : n + 16, :].astype(f32)
        quarter = quarter + (both[0:4] + both[4:8])
    piece[:n, :] = total.astype(bf16)
    piece[n:, :] = jnp.concatenate([extra[...][0:8], high_low(quarter)], axis=0)


def join0_kernel(own, c1, c2, c3, part_a, part_b, short):
    _, _, _, z = where()
    na, nb = part_a.shape[0] // 4, part_b.shape[0] // 4
    quarters = []
    for m, c in enumerate((own, c1, c2, c3)):
        at = z ^ m
        part_a[pl.ds(pl.multiple_of(at * na, na), na), :] = c[:na, :]
        part_b[pl.ds(pl.multiple_of(at * nb, nb), nb), :] = c[na:, :]
        both = c[na + nb - 16 :, :].astype(f32)
        quarters.append((at, both[8:12] + both[12:16]))
    rows = []
    for j in range(4):
        row = quarters[0][1]
        for at, quarter in quarters[1:]:
            row = jnp.where(at == j, quarter, row)
        rows.append(row)
    short[...] = jnp.concatenate(rows, axis=0)


def join1_kernel(own_a, came_a, own_b, came_b, part_a, part_b):
    x, _, y, _ = where()
    n = own_a.shape[0]
    for bit, own, came, part in ((y, own_a, came_a, part_a), (x, own_b, came_b, part_b)):
        part[pl.ds(pl.multiple_of(bit * n, n), n), :] = own[...]
        part[pl.ds(pl.multiple_of((1 - bit) * n, n), n), :] = came[...]


def write_kernel(geo, first, jobs, *refs):
    n_out = 5
    quarters = refs[: len(jobs)]
    refs = refs[len(jobs) :]
    if not first:
        refs = refs[n_out:]
    write_end(write_start(geo, jobs, quarters, *refs))


def early_kernel(geo, jobs, own_a, core_a, own_b, core_b, *refs):
    refs = refs[5:]
    outs, (class_part, facts, wide, sems) = refs[:5], refs[5:]
    waits = write_start(geo, jobs, (core_a, core_b), *outs, wide, sems)
    _, core, y, _ = where()
    facts[...] = jnp.zeros(facts.shape, f32)
    class_part[...] = class_rows_of(geo, class_part.shape, [(own_b, core, y), (core_b, 1 - core, y)], facts)
    write_end(waits)


def finish_kernel(geo, jobs, *refs):
    quarters = refs[: len(jobs)]
    came_b, class_part, facts_part, fc_keep, fc_came = refs[len(jobs) : len(jobs) + 5]
    refs = refs[len(jobs) + 10 :]
    outs, (own_fc2, own_fc1, class_own, mean, top, wide, facts, sems) = refs[:5], refs[5:]
    waits = write_start(geo, jobs, quarters, *outs, wide, sems)
    _, core, y, _ = where()
    facts[...] = facts_part[...]
    class_own[...] = class_part[...] + class_rows_of(
        geo, class_own.shape, [(came_b, core, 1 - y), (quarters[1], 1 - core, 1 - y)], facts
    )
    every = facts[...]
    summed = col_sum(every)
    scale_sum = summed[:, 0:1] + summed[:, 1:2] + summed[:, 2:3]
    count = summed[:, 3:4] + summed[:, 4:5] + summed[:, 5:6]
    tops = every[:, 6:7] + every[:, 7:8] + every[:, 8:9]
    mean[...] = scale_sum / count
    top[...] = jnp.max(tops, axis=0, keepdims=True)
    add_kernel(fc_keep, fc_came, own_fc2, own_fc1)
    write_end(waits)


def write_end(waits):
    for taken, move in waits:
        if taken is None:
            move.wait()
        else:
            pl.when(taken)(move.wait)


def write_start(geo, jobs, quarters, g_qkv, g_out, g_pos, g_head, g_patch, wide, sems):
    x, core, y, _ = where()
    width = g_out.shape[0]
    half_q, half_e, half_l = geo["half_q"], geo["half_e"], geo["half_l"]
    nb, ne = geo["nb"], geo["extra"]
    feat = g_patch.shape[0]
    at, sem = 0, 0
    waits = []

    def copy(rows, target):
        nonlocal sem
        c = pltpu.make_async_copy(wide.at[rows], target, sems.at[sem])
        sem += 1
        return c

    for quarter, (part, other_core, other_half) in zip(quarters, jobs):
        c = 1 - core if other_core else core
        n = quarter.shape[0]
        if part == "a":
            h = 1 - x if other_half else x
            wide[at : at + n, :] = quarter[...].astype(f32)
            for k in range(0, n, 128):
                q = c * half_q + h * n + k
                third, row = q // width, q % width
                target = g_qkv.at[
                    pl.ds(pl.multiple_of(row, 128), 128),
                    pl.ds(pl.multiple_of(third * width, 128), width),
                ]
                waits.append((None, copy(slice(at + k, at + k + 128), target)))
                waits[-1][1].start()
            at += n
        else:
            h = 1 - y if other_half else y
            for k in range(n // (nb + ne)):
                wide[at + k * nb : at + (k + 1) * nb, :] = quarter[
                    k * (nb + ne) : k * (nb + ne) + nb, :
                ].astype(f32)
            left = half_q - 2 * geo["na"]
            rows = n // (nb + ne) * nb
            for case_c in range(2):
                for case_h in range(2):
                    spans = []
                    if case_h == 0:
                        spans.append((0, left, "q", case_c * half_q + 2 * geo["na"]))
                        spans.append((left, rows - left, "e", case_c * half_e))
                    else:
                        spans.append((0, half_e - (rows - left), "e", case_c * half_e + rows - left))
                        spans.append((half_e - (rows - left), half_l, "l", case_c * half_l))
                    moves = []
                    for start, size, kind, place in spans:
                        pieces = {
                            "q": [(case_c * half_q + 2 * geo["na"], left, g_qkv)],
                            "e": [(0, width, g_out), (width, 2 * feat, g_head)],
                            "l": [(0, g_pos.shape[0], g_pos), (g_pos.shape[0], feat, g_patch)],
                        }[kind]
                        for low, long, ref in pieces:
                            a, b = max(place, low), min(place + size, low + long)
                            if a >= b:
                                continue
                            source = slice(at + start + a - place, at + start + b - place)
                            if kind == "q":
                                third, row = a // width, a % width
                                target = g_qkv.at[row : row + b - a, third * width : (third + 1) * width]
                            else:
                                target = ref.at[a - low : b - low]
                            moves.append(copy(source, target))
                    taken = (c == case_c) & (h == case_h)

                    @pl.when(taken)
                    def _(moves=moves):
                        for move in moves:
                            move.start()

                    waits += [(taken, move) for move in moves]
            at += rows
    return waits


def class_rows_of(geo, shape, sources, facts):
    nb, ne, items = geo["nb"], geo["extra"], geo["items"]
    me = lax.axis_index("dp") * 2 + lax.axis_index("seq")
    want = (me * shape[0] + lax.broadcasted_iota(jnp.int32, (shape[0], 1), 0)).astype(f32)
    total = jnp.zeros(shape, f32)
    for q, c, h in sources:
        for k in range(8):
            block = q[k * (nb + ne) + nb : (k + 1) * (nb + ne), :].astype(f32)
            fact = block[items : items + 1]
            facts[pl.ds((c * 2 + h) * 8 + k, 1), :] = fact
            for i in range(items):
                slot = fact[:, 9 + i : 10 + i] * 32 + fact[:, 9 + items + i : 10 + items + i]
                total = total + jnp.where(want == slot, 1.0, 0.0) * block[i : i + 1]
    return total


class Cube:
    def __init__(self):
        self.size = lax.axis_size("dp") * lax.axis_size("seq")
        self.nbits = self.size.bit_length() - 1
        self.me = lax.axis_index("dp") * lax.axis_size("seq") + lax.axis_index("seq")
        self.bit = [(self.me >> k) & 1 for k in range(self.nbits)]

    def send(self, block, mask):
        return lax.ppermute(block, AXES, [(i, i ^ mask) for i in range(self.size)])

    def start(self, full, bits):
        rows = full.shape[0] >> len(bits)
        return full.reshape((2,) * len(bits) + (rows, full.shape[1])), list(bits)

    def scatter(self, block, left):
        for bit in list(left):
            axis = left.index(bit)
            mine = lax.dynamic_index_in_dim(block, self.bit[bit], axis, keepdims=False)
            away = lax.dynamic_index_in_dim(block, 1 - self.bit[bit], axis, keepdims=False)
            block = mine + self.send(away.astype(bf16), 1 << bit).astype(f32)
            left = [b for b in left if b != bit]
        return block

    def add_up(self, block, bits):
        for k in bits:
            block = block + self.send(block, 1 << k)
        return block

    def gather(self, block, bits):
        for k in reversed(bits):
            came = self.send(block, 1 << k)
            block = jnp.where(self.bit[k] == 0, jnp.stack([block, came]), jnp.stack([came, block]))
        return block


def local(
    patches, labels, valid_mask, class_slot, w_patch, b_patch, pos_embed, class_embed,
    norm1_gain, norm1_shift, w_qkv, w_out, norm2_gain, norm2_shift, w_fc1, b_fc1, w_fc2, b_fc2,
    final_gain, final_shift, w_head, b_head, cot_latent, cot_logdet,
):
    cube = Cube()
    line = Line()
    seq_n = lax.axis_size("seq")
    assert seq_n == 2
    seq = lax.axis_index("seq")
    held, span, feat = patches.shape
    items = held // seq_n
    length = span * seq_n
    width = w_out.shape[0]
    ff = w_fc1.shape[1]
    rows = items * length
    classes = class_embed.shape[0]
    chunk = ff // cube.size
    group = 2 * chunk
    fast = cube.size == 32

    runs = patches.transpose(0, 2, 1)
    cot_runs = cot_latent.transpose(0, 2, 1)
    valid_runs = valid_mask[:, None, :]
    w_head_t = w_head.T
    (packed,) = line.call(
        prep_kernel, [((items, 2 * feat + 8, span), f32)], [runs, cot_runs, valid_mask], "prep", 1, 1,
        places={0: HBM, 1: HBM, 2: HBM},
        scratch=[pltpu.VMEM((items, feat, span), bf16), pltpu.VMEM((held, span), jnp.int32),
                 pltpu.SemaphoreType.DMA((3,))],
    )
    came = cube.send(packed, 1)
    big = 2.0 * rows * width * ff
    firsts = line.call(
        fetch_kernel,
        [((items, feat, span), bf16), ((items, 16, width), bf16), ((width,), bf16), ((width,), bf16),
         ((width,), bf16), ((length, width), bf16), ((feat, width), bf16), (w_qkv.shape, bf16)],
        [labels, packed, runs, class_embed, b_patch, norm1_gain, norm1_shift, pos_embed, w_patch, w_qkv],
        "fetch", 1, 2, places={0: SMEM, 1: ANY} | {i: HBM for i in range(2, 10)},
        scratch=[pltpu.SemaphoreType.DMA((items + 10,))], tied=False,
    )
    w_qkv = firsts[-1]
    hidden0, normed1, qkv, shifted_t, attended, lse, w_out, w_fc1, w_fc2 = line.call(
        front_kernel,
        [((rows, width), f32), ((rows, width), bf16), ((rows, 3 * width), bf16), ((feat, rows), bf16),
         ((rows, width), bf16), ((items, HEADS, length), f32)]
        + [(w.shape, bf16) for w in (w_out, w_fc1, w_fc2)],
        [labels, came] + list(firsts) + [w_out, w_fc1, w_fc2],
        "front", 1, 6, places={0: SMEM} | {i: HBM for i in range(10, 13)},
        scratch=[pltpu.SemaphoreType.DMA((3,))],
    )
    n_short = 16
    (hidden1, normed2, act, slope, d_hidden2, part_in, lat_keep, lat_send, short, grad_head_t, facts) = line.call(
        middle_kernel,
        [((rows, width), f32), ((rows, width), bf16), ((rows, ff), bf16), ((rows, ff), bf16),
         ((rows, width), f32), ((feat, rows), f32), ((items, feat + 8, span), f32),
         ((items, feat + 8, span), f32), ((n_short, width), f32), ((2 * feat, width), f32),
         ((1, width), f32)],
        [cot_logdet, labels, class_slot, hidden0, attended, w_out, norm2_gain, norm2_shift, w_fc1, b_fc1,
         w_fc2, b_fc2, final_gain, final_shift, w_head_t, b_head, runs, cot_runs, valid_runs, came],
        "middle", 1, 8, places={0: SMEM, 1: SMEM, 2: SMEM},
    )
    groups = ff // (4 * group)
    pieces = [((groups, group, width), f32), ((groups, group, width), bf16)]

    def fc2_part(first, count):
        n = count * STEP // (2 * group)
        return line.call(
            partial(fc2_kernel, first), [((n, group, width), f32), ((n, group, width), bf16)],
            [act, d_hidden2], "fc2", 1, 4,
        )

    def fc1_half(h, before):
        return line.call(
            partial(fc1_kernel, h),
            pieces + [((rows, width), f32), ((ff // width // 2, width), f32)],
            [d_hidden2, w_fc2, slope, normed2, w_fc1] + before, "fc1", 1, 6,
        )

    def four(block):
        return block.reshape(-1, 2, chunk, width)

    half_e, half_l, half_q = 448, 192, 3 * width // 2
    keep20, send20 = fc2_part(0, 4)
    came20 = cube.send(send20, 2)
    keep21, send21 = fc2_part(4, 4)
    came21 = cube.send(send21, 2)
    keep10, send10, total, bias0 = fc1_half(0, [])
    came10 = cube.send(send10, 2)
    if fast:
        k20, s20 = stage(line, "fc2_core", (0, [(four(keep20), four(came20))]))
        c20 = cube.send(s20, 1)
    keep11, send11, total, bias1 = fc1_half(1, [total])
    came11 = cube.send(send11, 2)
    if fast:
        k21, s21 = stage(line, "fc2_core", (0, [(four(keep21), four(came21))]))
    def by_y(block):
        return block.reshape(2, 2, group, width)

    if fast:
        k10, s10 = stage(line, "fc1_core", (2, [(by_y(keep10), by_y(came10))]))
        c10 = cube.send(s10, 4)
    d_hidden1, short, ekeep, esend, d_attended = line.call(
        back_kernel,
        [((rows, width), f32), ((n_short, width), f32), ((half_e, width), f32), ((half_e, width), bf16),
         ((rows, width), bf16)],
        [d_hidden2, total, hidden1, norm2_gain, attended, w_out, short, bias0, bias1, grad_head_t],
        "back", 1, 6,
    )
    ecame = cube.send(esend, 2)

    if fast:
        k11, s11 = stage(line, "fc1_core", (2, [(by_y(keep11), by_y(came11))]))
    (d_qkv,) = line.call(
        attention_back_kernel, [((rows, 3 * width), bf16)], [qkv, lse, d_attended],
        "attention_back", 1, 4,
    )
    qkeep, qsend = line.call(
        qkv_kernel, [((half_q, width), f32), ((half_q, width), bf16)], [normed1, d_qkv],
        "qkv_grad", 1, 6,
    )
    qcame = cube.send(qsend, 2)
    lkeep, lsend, short, d_low, extra = line.call(
        partial(rest_kernel, items),
        [((half_l, width), f32), ((half_l + 2 * n_short, width), bf16), ((n_short, width), f32),
         ((rows, width), bf16), ((16, width), bf16)],
        [d_qkv, w_qkv, hidden0, d_hidden1, norm1_gain, shifted_t, short, facts],
        "rest", 3e10, 6, after=[c20, c10] if fast else [],
    )
    lcame = cube.send(lsend, 2)

    def swap_inputs():
        return line.call(
            inputs_kernel, [((items, 2 * feat + 8, span), f32)] * 2, [d_low, w_patch, part_in, lat_keep, lat_send],
            "inputs", 1, 4,
        )


    if fast:
        ns2 = 2 * n_short

        def two(na, nb):
            return [((na, width), f32), ((nb, width), f32), ((na, width), bf16), ((nb + ns2, width), bf16),
                    ((n_short, width), f32)]

        na, nb = 512, 384
        ka, sa = line.call(
            bulk0a_kernel, [((na, width), f32), ((na, width), bf16)], [qkeep, qcame], "bulk0a", 1, 10
        )
        ca = cube.send(sa, 1)
        kb, sb, short = line.call(
            partial(bulk0b_kernel, 2 * na),
            [((nb, width), f32), ((nb + ns2, width), bf16), ((n_short, width), f32)],
            [qkeep, qcame, ekeep, ecame, lkeep, lcame, short], "bulk0b", 1, 10,
        )
        cb = cube.send(sb, 4)
        back_keep, back_send = swap_inputs()
        ka, kb, sa, sb, short = line.call(
            bulk1_kernel, two(256, 192), [ka, ca, kb, cb, short], "bulk1", 1, 6
        )
        ca, cb = cube.send(sa, 4), cube.send(sb, 1)
        na, nb, ne = 64, 48, 16
        n = na + nb
        keep, z1, z2, z3, quarter = line.call(
            bulk2_kernel,
            [((n, width), f32)] + [((n + ne, width), bf16)] * 3 + [((8, width), f32)],
            [ka, ca, kb, cb, short], "bulk2", 1, 4,
        )
        z1, z2, z3 = cube.send(z1, 8), cube.send(z2, 16), cube.send(z3, 24)
        c21, c11 = cube.send(tie(s21, keep), 1), cube.send(tie(s11, keep), 4)
        def next_y(block):
            return block.reshape(-1, 2, chunk, width)

        k2, s2, k1, s1 = stage(
            line, "fc_second",
            (2, [(next_y(k20), next_y(c20)), (next_y(k21), next_y(c21))]),
            (0, [(next_y(k10), next_y(c10)), (next_y(k11), next_y(c11))]), cost=3e10,
        )
        c2, c1 = cube.send(s2, 4), cube.send(s1, 1)
        piece, = line.call(
            bulk3_kernel, [((n + ne, width), bf16)], [keep, z1, z2, z3, quarter, extra], "bulk3", 3e10, 4
        )
        g1, g2, g3 = cube.send(piece, 8), cube.send(piece, 16), cube.send(piece, 24)
        kf, sf = stage(
            line, "fc_third", (3, [(next_y(k2), next_y(c2)), (next_y(k1), next_y(c1))])
        )

        back_came = cube.send(tie(back_send, c2, c1), 1)
        part_a, part_b, short = line.call(
            join0_kernel, [((4 * na, width), bf16), ((4 * (nb + ne), width), bf16), ((n_short, width), f32)],
            [piece, g1, g2, g3], "join0", 1, 4, after=[back_came],
        )
        ca, cb = cube.send(part_a, 4), cube.send(part_b, 1)
        cf = cube.send(tie(sf, g1, g2, g3), 8)
        part_a, part_b = line.call(
            join1_kernel, [((8 * na, width), bf16), ((8 * (nb + ne), width), bf16)],
            [part_a, ca, part_b, cb], "join1", 1, 5,
        )
        ca, cb = cube.send(part_a, 1), cube.send(part_b, 4)
        xa, xb = cube.send(part_a, 2), cube.send(part_b, 2)
        geo = dict(na=8 * na, nb=nb, extra=ne, half_q=half_q, half_e=half_e, half_l=half_l, items=items)
        grads = write(
            line, geo, [("a", 0, 0), ("b", 0, 0)], [part_a, part_b], None, width, length, feat,
        )

        kf, sf = stage(line, "fc_fourth", (4, [(next_y(kf), next_y(cf))]))
        cf = cube.send(sf, 16)
        ya, yb = cube.send(ca, 2), cube.send(cb, 2)
        class_shape, fact_shape = (classes // cube.size, width), (cube.size, width)
        *grads, class_part, facts_part = finish(
            line, "early", early_kernel, geo, [("a", 1, 0), ("b", 1, 0)], [part_a, xa, part_b, xb], grads,
            [class_shape, fact_shape], 2, [], 10**10,
        )
        grads = write(line, geo, [("a", 0, 1), ("b", 0, 1)], [ca, cb], grads, width, length, feat)
        g_qkv, g_out, g_pos, g_head_t, g_patch, own_fc2, own_fc1, class_own, mean, top = finish(
            line, "finish", finish_kernel, geo, [("a", 1, 1), ("b", 1, 1)],
            [ya, yb, cb, class_part, facts_part, kf.reshape(2 * chunk, width), cf.reshape(2 * chunk, width)], grads,
            [(chunk, width), (chunk, width), class_shape, (1, 1), (1, 1)], 2, [pltpu.VMEM(fact_shape, f32)], 1,
        )
        mean, top = mean.reshape(()), top.reshape(())
    else:
        rest = [0] + list(range(2, cube.nbits))
        upper = list(range(cube.nbits - 1, 1, -1)) + [0]
        back_keep, back_send = swap_inputs()
        back_came = cube.send(back_send, 1)

        def owned(*parts):
            total = jnp.concatenate([k + c.astype(f32) for k, c in parts]).reshape(-1, width)
            return cube.scatter(*cube.start(total, upper))

        own_fc2 = owned((keep20, came20), (keep21, came21))
        own_fc1 = owned((keep10, came10), (keep11, came11))
        full = jnp.concatenate(
            [qkeep + qcame.astype(f32), ekeep + ecame.astype(f32), lkeep + lcame[:half_l].astype(f32)]
        )
        n_full = full.shape[0]
        full = jnp.pad(full, ((0, -n_full % (cube.size * 8)), (0, 0)))
        own = cube.scatter(*cube.start(full, upper))
        n_own = own.shape[0]
        got = cube.gather(jnp.concatenate([own.astype(bf16), extra]), [1] + upper)
        halves = got[..., :n_own, :].reshape(2, -1, width)[:, :n_full].astype(f32)
        short = cube.add_up(short, [1] + rest)
        q = halves[:, :half_q].reshape(3, width, width)
        g_qkv = jnp.concatenate([q[0], q[1], q[2]], axis=1)
        e = halves[:, half_q : half_q + half_e].reshape(-1, width)
        g_out, g_head_t = e[:width], e[width : width + 2 * feat]
        later = halves[:, half_q + half_e :].reshape(-1, width)
        g_pos, g_patch = later[:length], later[length : length + feat]
        extras = got[..., n_own : n_own + items + 1, :].reshape(cube.size, items + 1, width).astype(f32)
        sums = extras[:, :items].reshape(-1, width)
        facts = extras[:, items]
        mean = jnp.sum(facts[:, :3]) / jnp.sum(facts[:, 3:6])
        top = jnp.max(facts[:, 6] + facts[:, 7] + facts[:, 8])
        all_slots = (facts[:, 9 : 9 + items] * 32 + facts[:, 9 + items : 9 + 2 * items]).reshape(-1)
        own_rows = classes // cube.size
        wanted = (cube.me * own_rows + jnp.arange(own_rows)).astype(f32)
        hot = (wanted[:, None] == all_slots[None, :]).astype(bf16)
        class_own = dot(hot, sums.astype(bf16))

    out = jnp.where(
        seq == 0, jnp.concatenate([back_keep, back_came]), jnp.concatenate([back_came, back_keep])
    )
    latent_out = out[:, :feat].transpose(0, 2, 1)
    logdet_out = out[:, feat, 0]
    grad_in_out = out[:, feat + 8 :].transpose(0, 2, 1)
    b1_all = short[ROW["b1"] : ROW["b1"] + ff // width].reshape(-1)
    b1_own = lax.dynamic_slice_in_dim(b1_all, cube.me * chunk, chunk, 0)
    vec = {name: short[at] for name, at in ROW.items()}
    return (
        latent_out, logdet_out, grad_in_out, g_patch, vec["bp"], g_pos, class_own,
        vec["n1g"], vec["n1s"], g_qkv, g_out, vec["n2g"], vec["n2s"], own_fc1.T, b1_own, own_fc2,
        vec["b2"], vec["fg"], vec["fs"], g_head_t.T, vec["bh"][: 2 * feat], mean, top,
    )


def finish(line, name, body, geo, jobs, args, grads, shapes, n, scratch, cost):
    args = list(args)
    args[0] = tie(args[0], line.last)
    vmem, hbm = pl.BlockSpec(memory_space=VMEM), pl.BlockSpec(memory_space=ANY)
    width = grads[1].shape[0]
    got = pl.pallas_call(
        partial(body, geo, jobs),
        out_shape=[jax.ShapeDtypeStruct(g.shape, f32) for g in grads]
        + [jax.ShapeDtypeStruct(shape, f32) for shape in shapes],
        in_specs=[vmem] * len(args) + [hbm] * len(grads),
        out_specs=[hbm] * len(grads) + [vmem] * len(shapes),
        scratch_shapes=[pltpu.VMEM((512 * n, width), f32)] + scratch + [pltpu.SemaphoreType.DMA((16 * n,))],
        input_output_aliases={len(args) + i: i for i in range(len(grads))},
        compiler_params=pltpu.CompilerParams(vmem_limit_bytes=14 * 2**20),
        cost_estimate=pl.CostEstimate(flops=cost, bytes_accessed=1, transcendentals=0),
        name=name,
    )(*args, *grads)
    line.last = got[len(grads) - 1]
    return got


def write(line, geo, jobs, quarters, grads, width, length, feat, after=()):
    shapes = [(width, 3 * width), (width, width), (length, width), (2 * feat, width), (feat, width)]
    n = len(quarters)
    args = list(quarters)
    args[0] = tie(args[0], line.last, *after)
    aliases = {}
    if grads is not None:
        aliases = {n + i: i for i in range(len(shapes))}
        args += list(grads)
    grads = pl.pallas_call(
        partial(write_kernel, geo, grads is None, jobs),
        out_shape=[jax.ShapeDtypeStruct(s, f32) for s in shapes],
        in_specs=[pl.BlockSpec(memory_space=VMEM)] * n + [pl.BlockSpec(memory_space=ANY)] * len(aliases),
        out_specs=[pl.BlockSpec(memory_space=ANY)] * len(shapes),
        scratch_shapes=[pltpu.VMEM((512 * n, width), f32), pltpu.SemaphoreType.DMA((16 * n,))],
        input_output_aliases=aliases,
        compiler_params=pltpu.CompilerParams(vmem_limit_bytes=(2 * n + 4) * 2**20),
        cost_estimate=pl.CostEstimate(flops=10**10, bytes_accessed=1, transcendentals=0),
        name="write",
    )(*args)
    line.last = grads[-1]
    return grads


def solution(mesh):
    run, item, whole = P("dp", "seq", None), P("dp"), P()
    placed = (run, item, P("dp", "seq")) + (whole,) * 19 + (run, item)
    owned = P(AXES)
    return jax.shard_map(
        local,
        mesh=mesh,
        in_specs=placed,
        out_specs=(run, item, run, whole, whole, whole, P(AXES, None), whole, whole, whole, whole,
                   whole, whole, P(None, AXES), owned, P(AXES, None)) + (whole,) * 7,
        check_vma=False,
    )
```

```python
import math
from functools import partial

import jax
import jax.numpy as jnp
from jax import lax
from jax.experimental import pallas as pl
from jax.experimental.pallas import tpu as pltpu
from jax.sharding import PartitionSpec as P

HEADS = 12
EPS = 1e-05
GELU_A = math.sqrt(2.0 / math.pi)
GELU_B = 0.044715
bf16 = jnp.bfloat16
f32 = jnp.float32
AXES = ("dp", "seq")
ROW = dict(bp=0, n1g=1, n1s=2, n2g=3, n2s=4, b2=5, fg=6, fs=7, bh=8, b1=9)


def dot(left, right, a=1, b=0):
    return lax.dot_general(
        left, right, (((a,), (b,)), ((), ())), preferred_element_type=f32
    )


SMEM, VMEM, ANY, HBM = pltpu.SMEM, pltpu.VMEM, pl.ANY, pltpu.HBM


class Line:
    def __init__(self):
        self.last = None

    def call(self, body, outs, args, name, flops, limit, places=None, scratch=(), after=(), tied=True, pinned=True):
        places = places or {}
        args = list(args)
        after = tuple(after) + ((self.last,) if self.last is not None else ())
        if after and tied:
            at = max(i for i in range(len(args)) if places.get(i, VMEM) is VMEM)
            args[at] = tie(args[at], *after)
        specs = [pl.BlockSpec(memory_space=places.get(i, VMEM)) for i in range(len(args))]
        for i, place in places.items():
            if place is HBM:
                args[i] = pltpu.with_memory_space_constraint(args[i], HBM)
        got = pl.pallas_call(
            body,
            out_shape=[pltpu.VMEM(s, d) if pinned else jax.ShapeDtypeStruct(s, d) for s, d in outs],
            in_specs=specs,
            out_specs=[pl.BlockSpec(memory_space=VMEM)] * len(outs),
            scratch_shapes=list(scratch),
            compiler_params=pltpu.CompilerParams(vmem_limit_bytes=int(limit * 2**20)),
            cost_estimate=pl.CostEstimate(flops=int(flops), bytes_accessed=1, transcendentals=0),
            name=name,
        )(*args)
        self.last = got[0]
        return got


def tie(value, *others):
    return lax.optimization_barrier((value,) + others)[0]


def where():
    dp = lax.axis_index("dp")
    return lax.axis_index("seq"), dp & 1, (dp >> 1) & 1, dp >> 2


def my_bit(bit):
    return lax.axis_index("seq") if bit == 0 else (lax.axis_index("dp") >> (bit - 1)) & 1


def row_of(ref):
    return ref[...].reshape(1, ref.shape[0]).astype(f32)


def centered(hidden):
    center = hidden - jnp.mean(hidden, axis=-1, keepdims=True)
    spread = jnp.mean(center * center, axis=-1, keepdims=True)
    inverse = lax.rsqrt(spread + EPS)
    return center * inverse, inverse


def norm_pull(grad, unit, inverse, gain):
    scaled = grad * gain
    mean = jnp.mean(scaled, axis=-1, keepdims=True)
    along = jnp.mean(scaled * unit, axis=-1, keepdims=True)
    return inverse * (scaled - mean - unit * along)


def col_sum(values):
    return jnp.sum(values, axis=0, keepdims=True)


def both_halves(seq, own, came):
    low = jnp.where(seq == 0, own, came)
    high = jnp.where(seq == 0, came, own)
    return jnp.concatenate([low, high], axis=1)


def prep_kernel(runs, cot_runs, valid, out, part, mask, sems):
    x, _, _, _ = where()
    items = out.shape[0]
    feat, span = runs.shape[1:]
    theirs = pl.ds((1 - x) * items, items)
    copies = [
        pltpu.make_async_copy(runs.at[theirs], part, sems.at[0]),
        pltpu.make_async_copy(cot_runs.at[theirs], out.at[:, feat : 2 * feat], sems.at[1]),
        pltpu.make_async_copy(valid, mask, sems.at[2]),
    ]
    for copy in copies:
        copy.start()
    for copy in copies:
        copy.wait()
    out[:, :feat] = part[...].astype(f32)
    for i in range(items):
        row = mask[pl.ds((1 - x) * items + i, 1), :].astype(f32)
        out[i, 2 * feat :] = jnp.broadcast_to(row, (out.shape[1] - 2 * feat, span))


def fetch_kernel(labels, sent, runs_in, class_embed, b_patch_in, gain_in, shift_in, pos_in, w_patch_in, w_qkv_in,
                 runs, class_rows, b_patch, gain, shift, pos, w_patch, w_qkv, sems):
    x, _, _, _ = where()
    items = runs.shape[0]
    quarter = w_qkv.shape[0] // 4
    parts = [pl.ds(j * quarter, quarter) for j in range(4)]
    pairs = [(w_qkv_in.at[part], w_qkv.at[part]) for part in parts] + [(runs_in.at[pl.ds(x * items, items)], runs)]
    for i in range(items):
        tile = pl.multiple_of(labels[x * items + i] // 16 * 16, 16)
        pairs.append((class_embed.at[pl.ds(tile, 16)], class_rows.at[i]))
    pairs += [(b_patch_in, b_patch), (gain_in, gain), (shift_in, shift), (w_patch_in, w_patch), (pos_in, pos)]
    copies = [pltpu.make_async_copy(*pair, sems.at[n]) for n, pair in enumerate(pairs)]
    for copy in copies:
        copy.start()
    for copy in copies:
        copy.wait()


def front_kernel(labels, came, runs, class_rows, b_patch, gain, shift, pos, w_patch, w_qkv,
                 w_out_in, w_fc1_in, w_fc2_in,
                 hidden0, normed1, qkv, shifted_t, attended, lse, w_out, w_fc1, w_fc2, sems):
    x, _, _, _ = where()
    items = came.shape[0]
    feat = w_patch.shape[0]
    length, width = pos.shape
    copies = []
    for source, target in ((w_out_in, w_out), (w_fc1_in, w_fc1), (w_fc2_in, w_fc2)):
        copies.append(pltpu.make_async_copy(source, target, sems.at[len(copies)]))
        copies[-1].start()
    gain_row, shift_row, bias = row_of(gain), row_of(shift), row_of(b_patch)
    at_row = lax.broadcasted_iota(jnp.int32, (16, width), 0)
    for i in range(items):
        rows = slice(i * length, (i + 1) * length)
        whole = both_halves(x, runs[i].astype(f32), came[i, :feat])
        lane = lax.broadcasted_iota(jnp.int32, whole.shape, 1)
        moved = jnp.where(lane == 0, 0.0, pltpu.roll(whole, 1, 1)).astype(bf16)
        shifted_t[:, rows] = moved
        mine = at_row == labels[x * items + i] % 16
        base = bias + col_sum(jnp.where(mine, class_rows[i].astype(f32), 0.0))
        h0 = dot(moved, w_patch[...], 0, 0) + base + pos[...].astype(f32)
        hidden0[rows, :] = h0
        unit, _ = centered(h0)
        normed1[rows, :] = (unit * gain_row + shift_row).astype(bf16)
    for j in range(3):
        cols = slice(j * width, (j + 1) * width)
        qkv[:, cols] = dot(normed1[...], w_qkv[:, cols]).astype(bf16)
    mid = length // 2
    allowed = lower_keys(mid)

    def step(p, carry):
        for i in range(items):
            rows = slice(i * length, (i + 1) * length)
            at = [pl.ds(pl.multiple_of(j * width + p * 128, 128), 128) for j in range(3)]
            q, k, v = (qkv[rows, at[j]] for j in range(3))
            first = lax.broadcasted_iota(jnp.int32, q.shape, 1) < 64
            v_t = v.T
            outs = []
            for h in range(2):
                mine = first if h == 0 else ~first
                qh = jnp.where(mine, q * 0.125, jnp.zeros_like(q))
                v_h = v_t[h * 64 : (h + 1) * 64]
                s = dot(k[:mid], qh, 1, 1)
                s_a, s_b = jnp.where(allowed, s[:, :mid], -1e30), s[:, mid:]
                s_c = jnp.where(allowed, dot(k[mid:], qh[mid:], 1, 1), -1e30)
                top_a = jnp.max(s_a, axis=0, keepdims=True)
                top_b = jnp.max(jnp.maximum(s_b, s_c), axis=0, keepdims=True)
                e_a, e_b, e_c = jnp.exp(s_a - top_a), jnp.exp(s_b - top_b), jnp.exp(s_c - top_b)
                total_a = jnp.sum(e_a, axis=0, keepdims=True)
                total_b = jnp.sum(e_b + e_c, axis=0, keepdims=True)
                lse[i, pl.ds(p * 2 + h, 1), :] = jnp.concatenate(
                    [top_a + jnp.log(total_a), top_b + jnp.log(total_b)], axis=1
                )
                part_a, part_b = 1.0 / total_a, 1.0 / total_b
                p_ab = jnp.concatenate([(e_a * part_a).astype(bf16), (e_b * part_b).astype(bf16)], axis=1)
                out = dot(v_h[:, :mid], p_ab)
                late = out[:, mid:] + dot(v_h[:, mid:], (e_c * part_b).astype(bf16))
                outs.append(jnp.concatenate([out[:, :mid], late], axis=1))
            attended[rows, at[0]] = jnp.concatenate(outs, axis=0).T.astype(bf16)
        return carry

    lax.fori_loop(0, HEADS // 2, step, 0, unroll=3)
    for copy in copies:
        copy.wait()


def middle_kernel(det, labels, class_slot, hidden0, attended, w_out, gain2, shift2, w_fc1, b_fc1, w_fc2, b_fc2,
                  gainf, shiftf, w_head_t, b_head, runs, cot_runs, valid_runs, came,
                  hidden1, normed2, act, slope, d_hidden2, part_in, lat_keep, lat_send,
                  short, grad_head_t, facts):
    x, _, _, _ = where()
    items = came.shape[0]
    feat = runs.shape[1]
    width = w_out.shape[0]
    span = came.shape[2]
    length = 2 * span
    hidden1[...] = hidden0[...] + dot(attended[...], w_out[...])
    gain, shift = row_of(gain2), row_of(shift2)
    for i in range(items):
        rows = slice(i * length, (i + 1) * length)
        unit, _ = centered(hidden1[rows, :])
        normed2[rows, :] = (unit * gain + shift).astype(bf16)
    total = None
    for j in range(w_fc1.shape[1] // width):
        cols = slice(j * width, (j + 1) * width)
        up = dot(normed2[...], w_fc1[:, cols]) + b_fc1[cols].reshape(1, width).astype(f32)
        square = up * up
        half = 0.5 * jnp.tanh(up * (GELU_A + GELU_A * GELU_B * square)) + 0.5
        value = up * half
        act[:, cols] = value.astype(bf16)
        slope[:, cols] = (
            half + 2.0 * value * (1.0 - half) * (GELU_A + 3.0 * GELU_A * GELU_B * square)
        ).astype(bf16)
        part = dot(act[:, cols], w_fc2[cols, :])
        total = part if total is None else total + part
    hidden2 = hidden1[...] + total + row_of(b_fc2)
    unit, inverse_dev = centered(hidden2)
    gain = row_of(gainf)
    normed3 = (unit * gain + row_of(shiftf)).astype(bf16)
    bias = jnp.broadcast_to(row_of(b_head), (8, 2 * feat)).T[:, :1]
    head = dot(w_head_t[...], normed3, 1, 1) + bias
    short[...] = jnp.zeros(short.shape, f32)
    d_heads = []
    sums = [jnp.zeros((1, 1), f32), jnp.zeros((1, 1), f32), jnp.full((1, 1), -1e30, f32)]
    for i in range(items):
        cols = slice(i * length, (i + 1) * length)
        source = x * items + i
        given = both_halves(x, runs[source].astype(f32), came[i, :feat])
        cot = both_halves(x, cot_runs[source], came[i, feat : 2 * feat])
        valid = both_halves(
            x, valid_runs[source].astype(f32), came[i, 2 * feat : 2 * feat + 1]
        )
        shift_part = head[:feat, cols]
        log_scale = head[feat:, cols]
        inverse = jnp.exp(-log_scale)
        moved = (given - shift_part) * inverse
        latent = valid * moved + (1.0 - valid) * given
        d_moved = valid * cot
        d_heads.append(
            jnp.concatenate(
                [-d_moved * inverse, -d_moved * moved - valid * det[source]], axis=0
            ).astype(bf16)
        )
        part_in[:, cols] = cot * (1.0 - valid) + d_moved * inverse
        counted = valid * log_scale
        item_sum = jnp.sum(jnp.sum(counted, axis=1, keepdims=True), axis=0, keepdims=True)
        sums[0] = sums[0] + item_sum
        sums[1] = sums[1] + jnp.sum(valid, axis=1, keepdims=True) * feat
        tops = jnp.where(valid > 0, log_scale, -1e30)
        tops = jnp.max(jnp.max(tops, axis=1, keepdims=True), axis=0, keepdims=True)
        sums[2] = jnp.maximum(sums[2], tops)
        low, high = latent[:, :span], latent[:, span:]
        logdet = jnp.broadcast_to(-item_sum, (8, span))
        lat_keep[i, :feat] = jnp.where(x == 0, low, high)
        lat_send[i, :feat] = jnp.where(x == 0, high, low)
        lat_keep[i, feat:] = logdet
        lat_send[i, feat:] = logdet
    lane = lax.broadcasted_iota(jnp.int32, facts.shape, 1)
    row = jnp.zeros(facts.shape, f32)
    for k, value in enumerate(sums):
        for j in range(3):
            piece = value.astype(bf16).astype(f32)
            value = value - piece
            row = jnp.where(lane == 3 * k + j, piece, row)
    for i in range(items):
        slot = class_slot[labels[x * items + i]]
        row = jnp.where(lane == 9 + i, (slot // 32).astype(f32), row)
        row = jnp.where(lane == 9 + items + i, (slot % 32).astype(f32), row)
    facts[...] = row
    d_head = jnp.concatenate(d_heads, axis=1)
    grad_head_t[...] = dot(d_head, normed3)
    short[ROW["bh"] : ROW["bh"] + 1, : 2 * feat] = dot(
        jnp.ones((8, d_head.shape[1]), bf16), d_head, 1, 1
    )[:1]
    d_normed3 = dot(d_head, w_head_t[...], 0, 0)
    short[ROW["fg"] : ROW["fg"] + 1, :] = col_sum(d_normed3 * unit)
    short[ROW["fs"] : ROW["fs"] + 1, :] = col_sum(d_normed3)
    pulled = norm_pull(d_normed3, unit, inverse_dev, gain)
    d_hidden2[...] = pulled
    short[ROW["b2"] : ROW["b2"] + 1, :] = col_sum(pulled.astype(bf16).astype(f32))


def split_by(bit, block, keep, send, half):
    low, high = block[:half], block[half:]
    keep[...] = jnp.where(bit == 0, low, high).astype(keep.dtype)
    send[...] = jnp.where(bit == 0, high, low).astype(send.dtype)


def split_groups(core, block, first, keep, send):
    group = keep.shape[1]
    for k in range(block.shape[0] // (2 * group)):
        rows = block[2 * group * k : 2 * group * (k + 1)]
        split_by(core, rows, keep.at[first + k], send.at[first + k], group)


STEP = 384


def fc2_kernel(first, act, d_hidden2, keep, send):
    _, core, _, _ = where()
    d_mlp = d_hidden2[...].astype(bf16)
    for j in range(2 * keep.shape[0] * keep.shape[1] // STEP):
        at = (first + j) * STEP
        block = dot(act[:, at : at + STEP], d_mlp, 0, 0)
        split_groups(core, block, j * STEP // (2 * keep.shape[1]), keep, send)


def fc1_kernel(half, d_hidden2, w_fc2, slope, normed2, w_fc1, *refs):
    before, (keep, send, total_out, bias) = refs[:-4], refs[-4:]
    _, core, _, _ = where()
    width = normed2.shape[1]
    d_mlp = d_hidden2[...].astype(bf16)
    total = before[0][...] if before else None
    count = w_fc1.shape[1] // 2 // width
    for j in range(count):
        at = (half * count + j) * width
        cols = slice(at, at + width)
        d_up = (dot(d_mlp, w_fc2[cols, :], 1, 1) * slope[:, cols].astype(f32)).astype(bf16)
        bias[j : j + 1, :] = col_sum(d_up.astype(f32))
        for m in range(width // STEP):
            block = dot(d_up[:, m * STEP : (m + 1) * STEP], normed2[...], 0, 0)
            split_groups(core, block, (j * width + m * STEP) // (2 * keep.shape[1]), keep, send)
        part = dot(d_up, w_fc1[:, cols], 1, 1)
        total = part if total is None else total + part
    total_out[...] = total


def back_kernel(d_hidden2, total_in, hidden1, gain2, w_out, short_in, bias_a, bias_b,
                d_hidden1, short, d_out, d_attended):
    short[...] = short_in[...]
    n = bias_a.shape[0]
    short[ROW["b1"] : ROW["b1"] + n, :] = bias_a[...]
    short[ROW["b1"] + n : ROW["b1"] + 2 * n, :] = bias_b[...]
    unit, inverse_dev = centered(hidden1[...])
    total = total_in[...]
    short[ROW["n2g"] : ROW["n2g"] + 1, :] = col_sum(total * unit)
    short[ROW["n2s"] : ROW["n2s"] + 1, :] = col_sum(total)
    h1 = d_hidden2[...] + norm_pull(total, unit, inverse_dev, row_of(gain2))
    d_hidden1[...] = h1
    low = h1.astype(bf16)
    d_out[...] = low
    d_attended[...] = dot(low, w_out[...], 1, 1).astype(bf16)


def out_kernel(attended, d_out, grad_head_t, keep, send):
    _, core, _, _ = where()
    grad_out = dot(attended[...], d_out[...], 0, 0)
    half, width = keep.shape
    rest = 2 * half - grad_out.shape[0] - grad_head_t.shape[0]
    block = jnp.concatenate([grad_out, grad_head_t[...], jnp.zeros((rest, width), f32)], axis=0)
    split_by(core, block, keep, send, half)


def lower_keys(n):
    key_at = lax.broadcasted_iota(jnp.int32, (n, n), 0)
    return key_at <= lax.broadcasted_iota(jnp.int32, (n, n), 1)


def attention_back_kernel(qkv, lse, d_attended, d_qkv):
    rows_all, width = d_attended.shape
    items = lse.shape[0]
    length = rows_all // items
    mid = length // 2
    allowed = lower_keys(mid)

    def step(p, carry):
        for i in range(items):
            rows = slice(i * length, (i + 1) * length)
            at = [pl.ds(pl.multiple_of(j * width + p * 128, 128), 128) for j in range(3)]
            q, k, v = (qkv[rows, at[j]] for j in range(3))
            q = q * 0.125
            d_o = d_attended[rows, at[0]]
            first = lax.broadcasted_iota(jnp.int32, q.shape, 1) < 64
            none = jnp.zeros_like(q)
            total = [None] * 6
            for h in range(2):
                mine = first if h == 0 else ~first
                qh = jnp.where(mine, q, none)
                kh = jnp.where(mine, k * 0.125, none)
                dh = jnp.where(mine, d_o, none)
                log_sum = lse[i, pl.ds(p * 2 + h, 1), :]
                log_a, log_b = log_sum[:, :mid], log_sum[:, mid:]
                s = dot(k[:mid], qh, 1, 1)
                s_c = dot(k[mid:], qh[mid:], 1, 1)
                p_a = jnp.exp(jnp.where(allowed, s[:, :mid], -1e30) - log_a)
                p_b = jnp.exp(s[:, mid:] - log_b)
                p_c = jnp.exp(jnp.where(allowed, s_c, -1e30) - log_b)
                d_p = dot(v[:mid], dh, 1, 1)
                d_a, d_b = d_p[:, :mid], d_p[:, mid:]
                d_c = dot(v[mid:], dh[mid:], 1, 1)
                delta_a = jnp.sum(p_a * d_a, axis=0, keepdims=True)
                delta_b = jnp.sum(p_b * d_b + p_c * d_c, axis=0, keepdims=True)
                s_a = (p_a * (d_a - delta_a)).astype(bf16)
                s_b = (p_b * (d_b - delta_b)).astype(bf16)
                s_c = (p_c * (d_c - delta_b)).astype(bf16)
                s_ab = jnp.concatenate([s_a, s_b], axis=1)
                p_ab = jnp.concatenate([p_a.astype(bf16), p_b.astype(bf16)], axis=1)
                parts = [
                    dot(s_a, kh[:mid], 0, 0),
                    dot(jnp.concatenate([s_b, s_c], axis=0), kh, 0, 0),
                    dot(s_ab, qh),
                    dot(s_c, qh[mid:]),
                    dot(p_ab, dh),
                    dot(p_c.astype(bf16), dh[mid:]),
                ]
                total = [b if a is None else a + b for a, b in zip(total, parts)]
            low, high = slice(i * length, i * length + mid), slice(i * length + mid, (i + 1) * length)
            for j in range(3):
                d_qkv[low, at[j]] = total[2 * j].astype(bf16)
                d_qkv[high, at[j]] = total[2 * j + 1].astype(bf16)
        return carry

    lax.fori_loop(0, HEADS // 2, step, 0, unroll=6)


def qkv_kernel(normed1, d_qkv, keep, send):
    _, core, _, _ = where()
    width = normed1.shape[1]
    half = keep.shape[0]
    for m in range(width // STEP):
        block = dot(normed1[:, m * STEP : (m + 1) * STEP], d_qkv[...], 0, 0)
        for j in range(3):
            part = block[:, j * width : (j + 1) * width]
            at = j * width + m * STEP
            inside = at % half

            @pl.when(core == at // half)
            def _():
                keep[inside : inside + STEP, :] = part

            @pl.when(core != at // half)
            def _():
                send[inside : inside + STEP, :] = part.astype(bf16)


def rest_kernel(items, d_qkv, w_qkv, hidden0, d_hidden1, gain1, shifted_t, short_in, facts,
                keep, send, short, d_low_out, extra):
    _, core, _, _ = where()
    width = hidden0.shape[1]
    length = hidden0.shape[0] // items
    d_normed1 = dot(d_qkv[...], w_qkv[...], 1, 1)
    unit, inverse_dev = centered(hidden0[...])
    short[...] = short_in[...]
    short[ROW["n1g"] : ROW["n1g"] + 1, :] = col_sum(d_normed1 * unit)
    short[ROW["n1s"] : ROW["n1s"] + 1, :] = col_sum(d_normed1)
    d0 = d_hidden1[...] + norm_pull(d_normed1, unit, inverse_dev, row_of(gain1))
    d_low = d0.astype(bf16)
    d_low_out[...] = d_low
    extra[...] = jnp.zeros(extra.shape, bf16)
    d_pos, whole = None, None
    for i in range(items):
        mine = d0[i * length : (i + 1) * length]
        d_pos = mine if d_pos is None else d_pos + mine
        item = col_sum(mine)
        whole = item if whole is None else whole + item
        extra[i : i + 1, :] = item.astype(bf16)
    extra[items : items + 1, :] = facts[...].astype(bf16)
    short[ROW["bp"] : ROW["bp"] + 1, :] = whole
    d_patch = dot(shifted_t[...], d_low)
    half = keep.shape[0]
    rest = 2 * half - d_pos.shape[0] - d_patch.shape[0]
    block = jnp.concatenate([d_pos, d_patch, jnp.zeros((rest, width), f32)], axis=0)
    split_by(core, block, keep, send.at[:half], half)
    short[...] = put_short(send, half, short[...])


def inputs_kernel(d_low, w_patch, part_in, lat_keep, lat_send, in_keep, in_send):
    x, _, _, _ = where()
    items, done, span = lat_keep.shape
    length = 2 * span
    in_keep[:, :done] = lat_keep[...]
    in_send[:, :done] = lat_send[...]
    d_shift = dot(w_patch[...], d_low[...], 1, 1)
    for i in range(items):
        cols = slice(i * length, (i + 1) * length)
        moved = d_shift[:, cols]
        lane = lax.broadcasted_iota(jnp.int32, moved.shape, 1)
        back = jnp.where(lane == length - 1, 0.0, pltpu.roll(moved, length - 1, 1))
        grad = part_in[:, cols] + back
        in_keep[i, done:] = jnp.where(x == 0, grad[:, :span], grad[:, span:])
        in_send[i, done:] = jnp.where(x == 0, grad[:, span:], grad[:, :span])


def put_short(send, at, short):
    n = short.shape[0]
    high = short.astype(bf16)
    low = (short - high.astype(f32)).astype(bf16)
    send[at : at + n, :] = high
    send[at + n : at + 2 * n, :] = low
    return high.astype(f32) + low.astype(f32)


def take_short(came, at, n):
    return came[at : at + n, :].astype(f32) + came[at + n : at + 2 * n, :].astype(f32)


def split_sum(bit, pairs, kept, send):
    mine = my_bit(bit)
    n = 0
    for keep, came in pairs:
        for a in range(keep.shape[0]):
            kept[n] = keep[a, mine] + came[a, mine].astype(f32)
            send[n] = (keep[a, 1 - mine] + came[a, 1 - mine].astype(f32)).astype(bf16)
            n += 1


def stage_kernel(bits, counts, *refs):
    n = 2 * sum(counts)
    ins, outs = refs[:n], refs[n:]
    for i, (bit, count) in enumerate(zip(bits, counts)):
        pairs = [(ins[2 * j], ins[2 * j + 1]) for j in range(count)]
        ins = ins[2 * count :]
        split_sum(bit, pairs, outs[2 * i], outs[2 * i + 1])


def stage(line, name, *parts, after=(), cost=1):
    outs, args = [], []
    for bit, pairs in parts:
        _, _, b, w = pairs[0][0].shape
        total = sum(keep.shape[0] for keep, _ in pairs)
        outs += [((total, b, w), f32), ((total, b, w), bf16)]
        for pair in pairs:
            args += list(pair)
    bits, counts = tuple(p[0] for p in parts), tuple(len(p[1]) for p in parts)
    return line.call(partial(stage_kernel, bits, counts), outs, args, name, cost, 8, after=after, pinned=True)


def add_kernel(keep, came, *outs):
    at = 0
    for out in outs:
        n = out.shape[0]
        out[...] = keep[at : at + n, :] + came[at : at + n, :].astype(f32)
        at += n


def bulk0a_kernel(qk, qc, keep_a, send_a):
    x, _, _, _ = where()
    na = keep_a.shape[0]
    mine, away = pl.ds(pl.multiple_of(x * na, na), na), pl.ds(pl.multiple_of((1 - x) * na, na), na)
    keep_a[...] = qk[mine, :] + qc[mine, :].astype(f32)
    send_a[...] = (qk[away, :] + qc[away, :].astype(f32)).astype(bf16)


def bulk0b_kernel(low, qk, qc, ek, ec, lk, lc, short_in, keep_b, send_b, short):
    _, _, y, _ = where()
    nb = keep_b.shape[0]
    nq, nl = qk.shape[0], lk.shape[0]
    total = short_in[...] + take_short(lc, nl, short.shape[0])
    parts = [
        qk[low:nq, :] + qc[low:nq, :].astype(f32),
        ek[...] + ec[...].astype(f32),
        lk[...] + lc[:nl, :].astype(f32),
    ]
    block = jnp.concatenate(parts, axis=0)
    split_by(y, block, keep_b, send_b.at[:nb], nb)
    short[...] = put_short(send_b, nb, total)


def bulk1_kernel(ka, ca, kb, cb, short_in, keep_a, keep_b, send_a, send_b, short):
    x, _, y, _ = where()
    na, nb = keep_a.shape[0], keep_b.shape[0]
    ns = short.shape[0]
    total = short_in[...] + take_short(cb, 2 * nb, ns)
    for bit, n, k, c, keep, send in ((y, na, ka, ca, keep_a, send_a), (x, nb, kb, cb, keep_b, send_b)):
        mine, away = pl.ds(pl.multiple_of(bit * n, n), n), pl.ds(pl.multiple_of((1 - bit) * n, n), n)
        keep[...] = k[mine, :] + c[mine, :].astype(f32)
        send[:n, :] = (k[away, :] + c[away, :].astype(f32)).astype(bf16)
    short[...] = put_short(send_b, nb, total)


def quarter_of(block, at):
    out = block[0:4]
    for j in range(1, 4):
        out = jnp.where(at == j, block[4 * j : 4 * j + 4], out)
    return out


def high_low(rows):
    high = rows.astype(bf16).astype(f32)
    return jnp.concatenate([high, rows - high], axis=0).astype(bf16)


def bulk2_kernel(ka, ca, kb, cb, short_in, keep, send1, send2, send3, short):
    _, _, _, z = where()
    na, nb = ka.shape[0] // 4, kb.shape[0] // 4
    n = na + nb
    total = short_in[...] + take_short(cb, 4 * nb, short_in.shape[0])
    for m, out in enumerate((keep, send1, send2, send3)):
        at = z ^ m
        ra = pl.ds(pl.multiple_of(at * na, na), na)
        rb = pl.ds(pl.multiple_of(at * nb, nb), nb)
        out[:na, :] = (ka[ra, :] + ca[ra, :].astype(f32)).astype(out.dtype)
        out[na:n, :] = (kb[rb, :] + cb[rb, :].astype(f32)).astype(out.dtype)
        quarter = quarter_of(total, at)
        if m == 0:
            short[...] = jnp.concatenate([quarter, quarter], axis=0)
        else:
            both = high_low(quarter)
            out[n : n + 16, :] = jnp.concatenate([both, both], axis=0)


def bulk3_kernel(keep, c1, c2, c3, short_in, extra, piece):
    n = keep.shape[0]
    total = keep[...]
    quarter = short_in[0:4, :]
    for c in (c1, c2, c3):
        total = total + c[:n, :].astype(f32)
        both = c[n : n + 16, :].astype(f32)
        quarter = quarter + (both[0:4] + both[4:8])
    piece[:n, :] = total.astype(bf16)
    piece[n:, :] = jnp.concatenate([extra[...][0:8], high_low(quarter)], axis=0)


def join0_kernel(own, c1, c2, c3, part_a, part_b, short):
    _, _, _, z = where()
    na, nb = part_a.shape[0] // 4, part_b.shape[0] // 4
    quarters = []
    for m, c in enumerate((own, c1, c2, c3)):
        at = z ^ m
        part_a[pl.ds(pl.multiple_of(at * na, na), na), :] = c[:na, :]
        part_b[pl.ds(pl.multiple_of(at * nb, nb), nb), :] = c[na:, :]
        both = c[na + nb - 16 :, :].astype(f32)
        quarters.append((at, both[8:12] + both[12:16]))
    rows = []
    for j in range(4):
        row = quarters[0][1]
        for at, quarter in quarters[1:]:
            row = jnp.where(at == j, quarter, row)
        rows.append(row)
    short[...] = jnp.concatenate(rows, axis=0)


def join1_kernel(own_a, came_a, own_b, came_b, part_a, part_b):
    x, _, y, _ = where()
    n = own_a.shape[0]
    for bit, own, came, part in ((y, own_a, came_a, part_a), (x, own_b, came_b, part_b)):
        part[pl.ds(pl.multiple_of(bit * n, n), n), :] = own[...]
        part[pl.ds(pl.multiple_of((1 - bit) * n, n), n), :] = came[...]


def write_kernel(geo, first, jobs, *refs):
    n_out = 5
    quarters = refs[: len(jobs)]
    refs = refs[len(jobs) :]
    if not first:
        refs = refs[n_out:]
    write_end(write_start(geo, jobs, quarters, *refs))


def early_kernel(geo, jobs, own_a, core_a, own_b, core_b, *refs):
    refs = refs[5:]
    outs, (class_part, facts, wide, sems) = refs[:5], refs[5:]
    waits = write_start(geo, jobs, (core_a, core_b), *outs, wide, sems)
    _, core, y, _ = where()
    facts[...] = jnp.zeros(facts.shape, f32)
    class_part[...] = class_rows_of(geo, class_part.shape, [(own_b, core, y), (core_b, 1 - core, y)], facts)
    write_end(waits)


def finish_kernel(geo, jobs, *refs):
    quarters = refs[: len(jobs)]
    came_b, class_part, facts_part, fc_keep, fc_came = refs[len(jobs) : len(jobs) + 5]
    refs = refs[len(jobs) + 10 :]
    outs, (own_fc2, own_fc1, class_own, mean, top, wide, facts, sems) = refs[:5], refs[5:]
    waits = write_start(geo, jobs, quarters, *outs, wide, sems)
    _, core, y, _ = where()
    facts[...] = facts_part[...]
    class_own[...] = class_part[...] + class_rows_of(
        geo, class_own.shape, [(came_b, core, 1 - y), (quarters[1], 1 - core, 1 - y)], facts
    )
    every = facts[...]
    summed = col_sum(every)
    scale_sum = summed[:, 0:1] + summed[:, 1:2] + summed[:, 2:3]
    count = summed[:, 3:4] + summed[:, 4:5] + summed[:, 5:6]
    tops = every[:, 6:7] + every[:, 7:8] + every[:, 8:9]
    mean[...] = scale_sum / count
    top[...] = jnp.max(tops, axis=0, keepdims=True)
    add_kernel(fc_keep, fc_came, own_fc2, own_fc1)
    write_end(waits)


def write_end(waits):
    for taken, move in waits:
        if taken is None:
            move.wait()
        else:
            pl.when(taken)(move.wait)


def write_start(geo, jobs, quarters, g_qkv, g_out, g_pos, g_head, g_patch, wide, sems):
    x, core, y, _ = where()
    width = g_out.shape[0]
    half_q, half_e, half_l = geo["half_q"], geo["half_e"], geo["half_l"]
    nb, ne = geo["nb"], geo["extra"]
    feat = g_patch.shape[0]
    at, sem = 0, 0
    waits = []

    def copy(rows, target):
        nonlocal sem
        c = pltpu.make_async_copy(wide.at[rows], target, sems.at[sem])
        sem += 1
        return c

    for quarter, (part, other_core, other_half) in zip(quarters, jobs):
        c = 1 - core if other_core else core
        n = quarter.shape[0]
        if part == "a":
            h = 1 - x if other_half else x
            wide[at : at + n, :] = quarter[...].astype(f32)
            for k in range(0, n, 128):
                q = c * half_q + h * n + k
                third, row = q // width, q % width
                target = g_qkv.at[
                    pl.ds(pl.multiple_of(row, 128), 128),
                    pl.ds(pl.multiple_of(third * width, 128), width),
                ]
                waits.append((None, copy(slice(at + k, at + k + 128), target)))
                waits[-1][1].start()
            at += n
        else:
            h = 1 - y if other_half else y
            for k in range(n // (nb + ne)):
                wide[at + k * nb : at + (k + 1) * nb, :] = quarter[
                    k * (nb + ne) : k * (nb + ne) + nb, :
                ].astype(f32)
            left = half_q - 2 * geo["na"]
            rows = n // (nb + ne) * nb
            for case_c in range(2):
                for case_h in range(2):
                    spans = []
                    if case_h == 0:
                        spans.append((0, left, "q", case_c * half_q + 2 * geo["na"]))
                        spans.append((left, rows - left, "e", case_c * half_e))
                    else:
                        spans.append((0, half_e - (rows - left), "e", case_c * half_e + rows - left))
                        spans.append((half_e - (rows - left), half_l, "l", case_c * half_l))
                    moves = []
                    for start, size, kind, place in spans:
                        pieces = {
                            "q": [(case_c * half_q + 2 * geo["na"], left, g_qkv)],
                            "e": [(0, width, g_out), (width, 2 * feat, g_head)],
                            "l": [(0, g_pos.shape[0], g_pos), (g_pos.shape[0], feat, g_patch)],
                        }[kind]
                        for low, long, ref in pieces:
                            a, b = max(place, low), min(place + size, low + long)
                            if a >= b:
                                continue
                            source = slice(at + start + a - place, at + start + b - place)
                            if kind == "q":
                                third, row = a // width, a % width
                                target = g_qkv.at[row : row + b - a, third * width : (third + 1) * width]
                            else:
                                target = ref.at[a - low : b - low]
                            moves.append(copy(source, target))
                    taken = (c == case_c) & (h == case_h)

                    @pl.when(taken)
                    def _(moves=moves):
                        for move in moves:
                            move.start()

                    waits += [(taken, move) for move in moves]
            at += rows
    return waits


def class_rows_of(geo, shape, sources, facts):
    nb, ne, items = geo["nb"], geo["extra"], geo["items"]
    me = lax.axis_index("dp") * 2 + lax.axis_index("seq")
    want = (me * shape[0] + lax.broadcasted_iota(jnp.int32, (shape[0], 1), 0)).astype(f32)
    total = jnp.zeros(shape, f32)
    for q, c, h in sources:
        for k in range(8):
            block = q[k * (nb + ne) + nb : (k + 1) * (nb + ne), :].astype(f32)
            fact = block[items : items + 1]
            facts[pl.ds((c * 2 + h) * 8 + k, 1), :] = fact
            for i in range(items):
                slot = fact[:, 9 + i : 10 + i] * 32 + fact[:, 9 + items + i : 10 + items + i]
                total = total + jnp.where(want == slot, 1.0, 0.0) * block[i : i + 1]
    return total


class Cube:
    def __init__(self):
        self.size = lax.axis_size("dp") * lax.axis_size("seq")
        self.nbits = self.size.bit_length() - 1
        self.me = lax.axis_index("dp") * lax.axis_size("seq") + lax.axis_index("seq")
        self.bit = [(self.me >> k) & 1 for k in range(self.nbits)]

    def send(self, block, mask):
        return lax.ppermute(block, AXES, [(i, i ^ mask) for i in range(self.size)])

    def start(self, full, bits):
        rows = full.shape[0] >> len(bits)
        return full.reshape((2,) * len(bits) + (rows, full.shape[1])), list(bits)

    def scatter(self, block, left):
        for bit in list(left):
            axis = left.index(bit)
            mine = lax.dynamic_index_in_dim(block, self.bit[bit], axis, keepdims=False)
            away = lax.dynamic_index_in_dim(block, 1 - self.bit[bit], axis, keepdims=False)
            block = mine + self.send(away.astype(bf16), 1 << bit).astype(f32)
            left = [b for b in left if b != bit]
        return block

    def add_up(self, block, bits):
        for k in bits:
            block = block + self.send(block, 1 << k)
        return block

    def gather(self, block, bits):
        for k in reversed(bits):
            came = self.send(block, 1 << k)
            block = jnp.where(self.bit[k] == 0, jnp.stack([block, came]), jnp.stack([came, block]))
        return block


def local(
    patches, labels, valid_mask, class_slot, w_patch, b_patch, pos_embed, class_embed,
    norm1_gain, norm1_shift, w_qkv, w_out, norm2_gain, norm2_shift, w_fc1, b_fc1, w_fc2, b_fc2,
    final_gain, final_shift, w_head, b_head, cot_latent, cot_logdet,
):
    cube = Cube()
    line = Line()
    seq_n = lax.axis_size("seq")
    assert seq_n == 2
    seq = lax.axis_index("seq")
    held, span, feat = patches.shape
    items = held // seq_n
    length = span * seq_n
    width = w_out.shape[0]
    ff = w_fc1.shape[1]
    rows = items * length
    classes = class_embed.shape[0]
    chunk = ff // cube.size
    group = 2 * chunk
    fast = cube.size == 32

    runs = patches.transpose(0, 2, 1)
    cot_runs = cot_latent.transpose(0, 2, 1)
    valid_runs = valid_mask[:, None, :]
    w_head_t = w_head.T
    (packed,) = line.call(
        prep_kernel, [((items, 2 * feat + 8, span), f32)], [runs, cot_runs, valid_mask], "prep", 1, 1,
        places={0: HBM, 1: HBM, 2: HBM},
        scratch=[pltpu.VMEM((items, feat, span), bf16), pltpu.VMEM((held, span), jnp.int32),
                 pltpu.SemaphoreType.DMA((3,))],
    )
    came = cube.send(packed, 1)
    big = 2.0 * rows * width * ff
    firsts = line.call(
        fetch_kernel,
        [((items, feat, span), bf16), ((items, 16, width), bf16), ((width,), bf16), ((width,), bf16),
         ((width,), bf16), ((length, width), bf16), ((feat, width), bf16), (w_qkv.shape, bf16)],
        [labels, packed, runs, class_embed, b_patch, norm1_gain, norm1_shift, pos_embed, w_patch, w_qkv],
        "fetch", 1, 2, places={0: SMEM, 1: ANY} | {i: HBM for i in range(2, 10)},
        scratch=[pltpu.SemaphoreType.DMA((items + 10,))], tied=False,
    )
    w_qkv = firsts[-1]
    hidden0, normed1, qkv, shifted_t, attended, lse, w_out, w_fc1, w_fc2 = line.call(
        front_kernel,
        [((rows, width), f32), ((rows, width), bf16), ((rows, 3 * width), bf16), ((feat, rows), bf16),
         ((rows, width), bf16), ((items, HEADS, length), f32)]
        + [(w.shape, bf16) for w in (w_out, w_fc1, w_fc2)],
        [labels, came] + list(firsts) + [w_out, w_fc1, w_fc2],
        "front", 1, 6, places={0: SMEM} | {i: HBM for i in range(10, 13)},
        scratch=[pltpu.SemaphoreType.DMA((3,))],
    )
    n_short = 16
    (hidden1, normed2, act, slope, d_hidden2, part_in, lat_keep, lat_send, short, grad_head_t, facts) = line.call(
        middle_kernel,
        [((rows, width), f32), ((rows, width), bf16), ((rows, ff), bf16), ((rows, ff), bf16),
         ((rows, width), f32), ((feat, rows), f32), ((items, feat + 8, span), f32),
         ((items, feat + 8, span), f32), ((n_short, width), f32), ((2 * feat, width), f32),
         ((1, width), f32)],
        [cot_logdet, labels, class_slot, hidden0, attended, w_out, norm2_gain, norm2_shift, w_fc1, b_fc1,
         w_fc2, b_fc2, final_gain, final_shift, w_head_t, b_head, runs, cot_runs, valid_runs, came],
        "middle", 1, 8, places={0: SMEM, 1: SMEM, 2: SMEM},
    )
    groups = ff // (4 * group)
    pieces = [((groups, group, width), f32), ((groups, group, width), bf16)]

    def fc2_part(first, count):
        n = count * STEP // (2 * group)
        return line.call(
            partial(fc2_kernel, first), [((n, group, width), f32), ((n, group, width), bf16)],
            [act, d_hidden2], "fc2", 1, 4,
        )

    def fc1_half(h, before):
        return line.call(
            partial(fc1_kernel, h),
            pieces + [((rows, width), f32), ((ff // width // 2, width), f32)],
            [d_hidden2, w_fc2, slope, normed2, w_fc1] + before, "fc1", 1, 6,
        )

    def four(block):
        return block.reshape(-1, 2, chunk, width)

    half_e, half_l, half_q = 448, 192, 3 * width // 2
    keep20, send20 = fc2_part(0, 4)
    came20 = cube.send(send20, 2)
    keep21, send21 = fc2_part(4, 4)
    came21 = cube.send(send21, 2)
    keep10, send10, total, bias0 = fc1_half(0, [])
    came10 = cube.send(send10, 2)
    if fast:
        k20, s20 = stage(line, "fc2_core", (0, [(four(keep20), four(came20))]))
        c20 = cube.send(s20, 1)
    keep11, send11, total, bias1 = fc1_half(1, [total])
    came11 = cube.send(send11, 2)
    if fast:
        k21, s21 = stage(line, "fc2_core", (0, [(four(keep21), four(came21))]))
    def by_y(block):
        return block.reshape(2, 2, group, width)

    if fast:
        k10, s10 = stage(line, "fc1_core", (2, [(by_y(keep10), by_y(came10))]))
        c10 = cube.send(s10, 4)
    d_hidden1, short, d_out, d_attended = line.call(
        back_kernel,
        [((rows, width), f32), ((n_short, width), f32), ((rows, width), bf16), ((rows, width), bf16)],
        [d_hidden2, total, hidden1, norm2_gain, w_out, short, bias0, bias1],
        "back", 1, 6,
    )

    if fast:
        k11, s11 = stage(line, "fc1_core", (2, [(by_y(keep11), by_y(came11))]))
    (d_qkv,) = line.call(
        attention_back_kernel, [((rows, 3 * width), bf16)], [qkv, lse, d_attended],
        "attention_back", 1, 4,
    )
    qkeep, qsend = line.call(
        qkv_kernel, [((half_q, width), f32), ((half_q, width), bf16)], [normed1, d_qkv],
        "qkv_grad", 1, 6,
    )
    qcame = cube.send(qsend, 2)
    ekeep, esend = line.call(
        out_kernel, [((half_e, width), f32), ((half_e, width), bf16)], [attended, d_out, grad_head_t], "out", 1, 5
    )
    ecame = cube.send(esend, 2)
    lkeep, lsend, short, d_low, extra = line.call(
        partial(rest_kernel, items),
        [((half_l, width), f32), ((half_l + 2 * n_short, width), bf16), ((n_short, width), f32),
         ((rows, width), bf16), ((16, width), bf16)],
        [d_qkv, w_qkv, hidden0, d_hidden1, norm1_gain, shifted_t, short, facts],
        "rest", 3e10, 6, after=[c20, c10] if fast else [],
    )
    lcame = cube.send(lsend, 2)

    def swap_inputs():
        return line.call(
            inputs_kernel, [((items, 2 * feat + 8, span), f32)] * 2, [d_low, w_patch, part_in, lat_keep, lat_send],
            "inputs", 1, 4,
        )


    if fast:
        ns2 = 2 * n_short

        def two(na, nb):
            return [((na, width), f32), ((nb, width), f32), ((na, width), bf16), ((nb + ns2, width), bf16),
                    ((n_short, width), f32)]

        na, nb = 512, 384
        ka, sa = line.call(
            bulk0a_kernel, [((na, width), f32), ((na, width), bf16)], [qkeep, qcame], "bulk0a", 1, 10
        )
        ca = cube.send(sa, 1)
        kb, sb, short = line.call(
            partial(bulk0b_kernel, 2 * na),
            [((nb, width), f32), ((nb + ns2, width), bf16), ((n_short, width), f32)],
            [qkeep, qcame, ekeep, ecame, lkeep, lcame, short], "bulk0b", 1, 10,
        )
        cb = cube.send(sb, 4)
        back_keep, back_send = swap_inputs()
        ka, kb, sa, sb, short = line.call(
            bulk1_kernel, two(256, 192), [ka, ca, kb, cb, short], "bulk1", 1, 6
        )
        ca, cb = cube.send(sa, 4), cube.send(sb, 1)
        na, nb, ne = 64, 48, 16
        n = na + nb
        keep, z1, z2, z3, quarter = line.call(
            bulk2_kernel,
            [((n, width), f32)] + [((n + ne, width), bf16)] * 3 + [((8, width), f32)],
            [ka, ca, kb, cb, short], "bulk2", 1, 4,
        )
        z1, z2, z3 = cube.send(z1, 8), cube.send(z2, 16), cube.send(z3, 24)
        c21, c11 = cube.send(tie(s21, keep), 1), cube.send(tie(s11, keep), 4)
        def next_y(block):
            return block.reshape(-1, 2, chunk, width)

        k2, s2, k1, s1 = stage(
            line, "fc_second",
            (2, [(next_y(k20), next_y(c20)), (next_y(k21), next_y(c21))]),
            (0, [(next_y(k10), next_y(c10)), (next_y(k11), next_y(c11))]), cost=3e10,
        )
        c2, c1 = cube.send(s2, 4), cube.send(s1, 1)
        piece, = line.call(
            bulk3_kernel, [((n + ne, width), bf16)], [keep, z1, z2, z3, quarter, extra], "bulk3", 3e10, 4
        )
        g1, g2, g3 = cube.send(piece, 8), cube.send(piece, 16), cube.send(piece, 24)
        kf, sf = stage(
            line, "fc_third", (3, [(next_y(k2), next_y(c2)), (next_y(k1), next_y(c1))])
        )

        back_came = cube.send(tie(back_send, c2, c1), 1)
        part_a, part_b, short = line.call(
            join0_kernel, [((4 * na, width), bf16), ((4 * (nb + ne), width), bf16), ((n_short, width), f32)],
            [piece, g1, g2, g3], "join0", 1, 4, after=[back_came],
        )
        ca, cb = cube.send(part_a, 4), cube.send(part_b, 1)
        cf = cube.send(tie(sf, g1, g2, g3), 8)
        part_a, part_b = line.call(
            join1_kernel, [((8 * na, width), bf16), ((8 * (nb + ne), width), bf16)],
            [part_a, ca, part_b, cb], "join1", 1, 5,
        )
        ca, cb = cube.send(part_a, 1), cube.send(part_b, 4)
        xa, xb = cube.send(part_a, 2), cube.send(part_b, 2)
        geo = dict(na=8 * na, nb=nb, extra=ne, half_q=half_q, half_e=half_e, half_l=half_l, items=items)
        grads = write(
            line, geo, [("a", 0, 0), ("b", 0, 0)], [part_a, part_b], None, width, length, feat,
        )

        kf, sf = stage(line, "fc_fourth", (4, [(next_y(kf), next_y(cf))]))
        cf = cube.send(sf, 16)
        ya, yb = cube.send(ca, 2), cube.send(cb, 2)
        class_shape, fact_shape = (classes // cube.size, width), (cube.size, width)
        *grads, class_part, facts_part = finish(
            line, "early", early_kernel, geo, [("a", 1, 0), ("b", 1, 0)], [part_a, xa, part_b, xb], grads,
            [class_shape, fact_shape], 2, [], 10**10,
        )
        grads = write(line, geo, [("a", 0, 1), ("b", 0, 1)], [ca, cb], grads, width, length, feat)
        g_qkv, g_out, g_pos, g_head_t, g_patch, own_fc2, own_fc1, class_own, mean, top = finish(
            line, "finish", finish_kernel, geo, [("a", 1, 1), ("b", 1, 1)],
            [ya, yb, cb, class_part, facts_part, kf.reshape(2 * chunk, width), cf.reshape(2 * chunk, width)], grads,
            [(chunk, width), (chunk, width), class_shape, (1, 1), (1, 1)], 2, [pltpu.VMEM(fact_shape, f32)], 1,
        )
        mean, top = mean.reshape(()), top.reshape(())
    else:
        rest = [0] + list(range(2, cube.nbits))
        upper = list(range(cube.nbits - 1, 1, -1)) + [0]
        back_keep, back_send = swap_inputs()
        back_came = cube.send(back_send, 1)

        def owned(*parts):
            total = jnp.concatenate([k + c.astype(f32) for k, c in parts]).reshape(-1, width)
            return cube.scatter(*cube.start(total, upper))

        own_fc2 = owned((keep20, came20), (keep21, came21))
        own_fc1 = owned((keep10, came10), (keep11, came11))
        full = jnp.concatenate(
            [qkeep + qcame.astype(f32), ekeep + ecame.astype(f32), lkeep + lcame[:half_l].astype(f32)]
        )
        n_full = full.shape[0]
        full = jnp.pad(full, ((0, -n_full % (cube.size * 8)), (0, 0)))
        own = cube.scatter(*cube.start(full, upper))
        n_own = own.shape[0]
        got = cube.gather(jnp.concatenate([own.astype(bf16), extra]), [1] + upper)
        halves = got[..., :n_own, :].reshape(2, -1, width)[:, :n_full].astype(f32)
        short = cube.add_up(short, [1] + rest)
        q = halves[:, :half_q].reshape(3, width, width)
        g_qkv = jnp.concatenate([q[0], q[1], q[2]], axis=1)
        e = halves[:, half_q : half_q + half_e].reshape(-1, width)
        g_out, g_head_t = e[:width], e[width : width + 2 * feat]
        later = halves[:, half_q + half_e :].reshape(-1, width)
        g_pos, g_patch = later[:length], later[length : length + feat]
        extras = got[..., n_own : n_own + items + 1, :].reshape(cube.size, items + 1, width).astype(f32)
        sums = extras[:, :items].reshape(-1, width)
        facts = extras[:, items]
        mean = jnp.sum(facts[:, :3]) / jnp.sum(facts[:, 3:6])
        top = jnp.max(facts[:, 6] + facts[:, 7] + facts[:, 8])
        all_slots = (facts[:, 9 : 9 + items] * 32 + facts[:, 9 + items : 9 + 2 * items]).reshape(-1)
        own_rows = classes // cube.size
        wanted = (cube.me * own_rows + jnp.arange(own_rows)).astype(f32)
        hot = (wanted[:, None] == all_slots[None, :]).astype(bf16)
        class_own = dot(hot, sums.astype(bf16))

    out = jnp.where(
        seq == 0, jnp.concatenate([back_keep, back_came]), jnp.concatenate([back_came, back_keep])
    )
    latent_out = out[:, :feat].transpose(0, 2, 1)
    logdet_out = out[:, feat, 0]
    grad_in_out = out[:, feat + 8 :].transpose(0, 2, 1)
    b1_all = short[ROW["b1"] : ROW["b1"] + ff // width].reshape(-1)
    b1_own = lax.dynamic_slice_in_dim(b1_all, cube.me * chunk, chunk, 0)
    vec = {name: short[at] for name, at in ROW.items()}
    return (
        latent_out, logdet_out, grad_in_out, g_patch, vec["bp"], g_pos, class_own,
        vec["n1g"], vec["n1s"], g_qkv, g_out, vec["n2g"], vec["n2s"], own_fc1.T, b1_own, own_fc2,
        vec["b2"], vec["fg"], vec["fs"], g_head_t.T, vec["bh"][: 2 * feat], mean, top,
    )


def finish(line, name, body, geo, jobs, args, grads, shapes, n, scratch, cost):
    args = list(args)
    args[0] = tie(args[0], line.last)
    vmem, hbm = pl.BlockSpec(memory_space=VMEM), pl.BlockSpec(memory_space=ANY)
    width = grads[1].shape[0]
    got = pl.pallas_call(
        partial(body, geo, jobs),
        out_shape=[jax.ShapeDtypeStruct(g.shape, f32) for g in grads]
        + [jax.ShapeDtypeStruct(shape, f32) for shape in shapes],
        in_specs=[vmem] * len(args) + [hbm] * len(grads),
        out_specs=[hbm] * len(grads) + [vmem] * len(shapes),
        scratch_shapes=[pltpu.VMEM((512 * n, width), f32)] + scratch + [pltpu.SemaphoreType.DMA((16 * n,))],
        input_output_aliases={len(args) + i: i for i in range(len(grads))},
        compiler_params=pltpu.CompilerParams(vmem_limit_bytes=14 * 2**20),
        cost_estimate=pl.CostEstimate(flops=cost, bytes_accessed=1, transcendentals=0),
        name=name,
    )(*args, *grads)
    line.last = got[len(grads) - 1]
    return got


def write(line, geo, jobs, quarters, grads, width, length, feat, after=()):
    shapes = [(width, 3 * width), (width, width), (length, width), (2 * feat, width), (feat, width)]
    n = len(quarters)
    args = list(quarters)
    args[0] = tie(args[0], line.last, *after)
    aliases = {}
    if grads is not None:
        aliases = {n + i: i for i in range(len(shapes))}
        args += list(grads)
    grads = pl.pallas_call(
        partial(write_kernel, geo, grads is None, jobs),
        out_shape=[jax.ShapeDtypeStruct(s, f32) for s in shapes],
        in_specs=[pl.BlockSpec(memory_space=VMEM)] * n + [pl.BlockSpec(memory_space=ANY)] * len(aliases),
        out_specs=[pl.BlockSpec(memory_space=ANY)] * len(shapes),
        scratch_shapes=[pltpu.VMEM((512 * n, width), f32), pltpu.SemaphoreType.DMA((16 * n,))],
        input_output_aliases=aliases,
        compiler_params=pltpu.CompilerParams(vmem_limit_bytes=(2 * n + 4) * 2**20),
        cost_estimate=pl.CostEstimate(flops=10**10, bytes_accessed=1, transcendentals=0),
        name="write",
    )(*args)
    line.last = grads[-1]
    return grads


def solution(mesh):
    run, item, whole = P("dp", "seq", None), P("dp"), P()
    placed = (run, item, P("dp", "seq")) + (whole,) * 19 + (run, item)
    owned = P(AXES)
    return jax.shard_map(
        local,
        mesh=mesh,
        in_specs=placed,
        out_specs=(run, item, run, whole, whole, whole, P(AXES, None), whole, whole, whole, whole,
                   whole, whole, P(None, AXES), owned, P(AXES, None)) + (whole,) * 7,
        check_vma=False,
    )
```

```python
import math
from functools import partial

import jax
import jax.numpy as jnp
from jax import lax
from jax.experimental import pallas as pl
from jax.experimental.pallas import tpu as pltpu
from jax.sharding import PartitionSpec as P

HEADS = 12
EPS = 1e-05
GELU_A = math.sqrt(2.0 / math.pi)
GELU_B = 0.044715
bf16 = jnp.bfloat16
f32 = jnp.float32
AXES = ("dp", "seq")
ROW = dict(bp=0, n1g=1, n1s=2, n2g=3, n2s=4, b2=5, fg=6, fs=7, bh=8, b1=9)


def dot(left, right, a=1, b=0):
    return lax.dot_general(
        left, right, (((a,), (b,)), ((), ())), preferred_element_type=f32
    )


SMEM, VMEM, ANY, HBM = pltpu.SMEM, pltpu.VMEM, pl.ANY, pltpu.HBM


class Line:
    def __init__(self):
        self.last = None

    def call(self, body, outs, args, name, flops, limit, places=None, scratch=(), after=(), tied=True, pinned=True):
        places = places or {}
        args = list(args)
        after = tuple(after) + ((self.last,) if self.last is not None else ())
        if after and tied:
            at = max(i for i in range(len(args)) if places.get(i, VMEM) is VMEM)
            args[at] = tie(args[at], *after)
        specs = [pl.BlockSpec(memory_space=places.get(i, VMEM)) for i in range(len(args))]
        for i, place in places.items():
            if place is HBM:
                args[i] = pltpu.with_memory_space_constraint(args[i], HBM)
        got = pl.pallas_call(
            body,
            out_shape=[pltpu.VMEM(s, d) if pinned else jax.ShapeDtypeStruct(s, d) for s, d in outs],
            in_specs=specs,
            out_specs=[pl.BlockSpec(memory_space=VMEM)] * len(outs),
            scratch_shapes=list(scratch),
            compiler_params=pltpu.CompilerParams(vmem_limit_bytes=int(limit * 2**20)),
            cost_estimate=pl.CostEstimate(flops=int(flops), bytes_accessed=1, transcendentals=0),
            name=name,
        )(*args)
        self.last = got[0]
        return got


def tie(value, *others):
    return lax.optimization_barrier((value,) + others)[0]


def where():
    dp = lax.axis_index("dp")
    return lax.axis_index("seq"), dp & 1, (dp >> 1) & 1, dp >> 2


def my_bit(bit):
    return lax.axis_index("seq") if bit == 0 else (lax.axis_index("dp") >> (bit - 1)) & 1


def row_of(ref):
    return ref[...].reshape(1, ref.shape[0]).astype(f32)


def centered(hidden):
    center = hidden - jnp.mean(hidden, axis=-1, keepdims=True)
    spread = jnp.mean(center * center, axis=-1, keepdims=True)
    inverse = lax.rsqrt(spread + EPS)
    return center * inverse, inverse


def norm_pull(grad, unit, inverse, gain):
    scaled = grad * gain
    mean = jnp.mean(scaled, axis=-1, keepdims=True)
    along = jnp.mean(scaled * unit, axis=-1, keepdims=True)
    return inverse * (scaled - mean - unit * along)


def col_sum(values):
    return jnp.sum(values, axis=0, keepdims=True)


def both_halves(seq, own, came):
    low = jnp.where(seq == 0, own, came)
    high = jnp.where(seq == 0, came, own)
    return jnp.concatenate([low, high], axis=1)


def prep_kernel(runs, cot_runs, valid, out, part, mask, sems):
    x, _, _, _ = where()
    items = out.shape[0]
    feat, span = runs.shape[1:]
    theirs = pl.ds((1 - x) * items, items)
    copies = [
        pltpu.make_async_copy(runs.at[theirs], part, sems.at[0]),
        pltpu.make_async_copy(cot_runs.at[theirs], out.at[:, feat : 2 * feat], sems.at[1]),
        pltpu.make_async_copy(valid, mask, sems.at[2]),
    ]
    for copy in copies:
        copy.start()
    for copy in copies:
        copy.wait()
    out[:, :feat] = part[...].astype(f32)
    for i in range(items):
        row = mask[pl.ds((1 - x) * items + i, 1), :].astype(f32)
        out[i, 2 * feat :] = jnp.broadcast_to(row, (out.shape[1] - 2 * feat, span))


def fetch_kernel(labels, sent, runs_in, class_embed, b_patch_in, gain_in, shift_in, pos_in, w_patch_in, w_qkv_in,
                 runs, class_rows, b_patch, gain, shift, pos, w_patch, w_qkv, sems):
    x, _, _, _ = where()
    items = runs.shape[0]
    quarter = w_qkv.shape[0] // 4
    parts = [pl.ds(j * quarter, quarter) for j in range(4)]
    pairs = [(w_qkv_in.at[part], w_qkv.at[part]) for part in parts] + [(runs_in.at[pl.ds(x * items, items)], runs)]
    for i in range(items):
        tile = pl.multiple_of(labels[x * items + i] // 16 * 16, 16)
        pairs.append((class_embed.at[pl.ds(tile, 16)], class_rows.at[i]))
    pairs += [(b_patch_in, b_patch), (gain_in, gain), (shift_in, shift), (w_patch_in, w_patch), (pos_in, pos)]
    copies = [pltpu.make_async_copy(*pair, sems.at[n]) for n, pair in enumerate(pairs)]
    for copy in copies:
        copy.start()
    for copy in copies:
        copy.wait()


def front_kernel(labels, came, runs, class_rows, b_patch, gain, shift, pos, w_patch, w_qkv,
                 w_out_in, w_fc1_in, w_fc2_in,
                 hidden0, normed1, qkv, shifted_t, attended, lse, w_out, w_fc1, w_fc2, sems):
    x, _, _, _ = where()
    items = came.shape[0]
    feat = w_patch.shape[0]
    length, width = pos.shape
    copies = []
    for source, target in ((w_out_in, w_out), (w_fc1_in, w_fc1), (w_fc2_in, w_fc2)):
        copies.append(pltpu.make_async_copy(source, target, sems.at[len(copies)]))
        copies[-1].start()
    gain_row, shift_row, bias = row_of(gain), row_of(shift), row_of(b_patch)
    at_row = lax.broadcasted_iota(jnp.int32, (16, width), 0)
    for i in range(items):
        rows = slice(i * length, (i + 1) * length)
        whole = both_halves(x, runs[i].astype(f32), came[i, :feat])
        lane = lax.broadcasted_iota(jnp.int32, whole.shape, 1)
        moved = jnp.where(lane == 0, 0.0, pltpu.roll(whole, 1, 1)).astype(bf16)
        shifted_t[:, rows] = moved
        mine = at_row == labels[x * items + i] % 16
        base = bias + col_sum(jnp.where(mine, class_rows[i].astype(f32), 0.0))
        h0 = dot(moved, w_patch[...], 0, 0) + base + pos[...].astype(f32)
        hidden0[rows, :] = h0
        unit, _ = centered(h0)
        normed1[rows, :] = (unit * gain_row + shift_row).astype(bf16)
    for j in range(3):
        cols = slice(j * width, (j + 1) * width)
        qkv[:, cols] = dot(normed1[...], w_qkv[:, cols]).astype(bf16)
    mid = length // 2
    allowed = lower_keys(mid)

    def step(p, carry):
        for i in range(items):
            rows = slice(i * length, (i + 1) * length)
            at = [pl.ds(pl.multiple_of(j * width + p * 128, 128), 128) for j in range(3)]
            q, k, v = (qkv[rows, at[j]] for j in range(3))
            first = lax.broadcasted_iota(jnp.int32, q.shape, 1) < 64
            v_t = v.T
            outs = []
            for h in range(2):
                mine = first if h == 0 else ~first
                qh = jnp.where(mine, q * 0.125, jnp.zeros_like(q))
                v_h = v_t[h * 64 : (h + 1) * 64]
                s = dot(k[:mid], qh, 1, 1)
                s_a, s_b = jnp.where(allowed, s[:, :mid], -1e30), s[:, mid:]
                s_c = jnp.where(allowed, dot(k[mid:], qh[mid:], 1, 1), -1e30)
                top_a = jnp.max(s_a, axis=0, keepdims=True)
                top_b = jnp.max(jnp.maximum(s_b, s_c), axis=0, keepdims=True)
                e_a, e_b, e_c = jnp.exp(s_a - top_a), jnp.exp(s_b - top_b), jnp.exp(s_c - top_b)
                total_a = jnp.sum(e_a, axis=0, keepdims=True)
                total_b = jnp.sum(e_b + e_c, axis=0, keepdims=True)
                lse[i, pl.ds(p * 2 + h, 1), :] = jnp.concatenate(
                    [top_a + jnp.log(total_a), top_b + jnp.log(total_b)], axis=1
                )
                part_a, part_b = 1.0 / total_a, 1.0 / total_b
                p_ab = jnp.concatenate([(e_a * part_a).astype(bf16), (e_b * part_b).astype(bf16)], axis=1)
                out = dot(v_h[:, :mid], p_ab)
                late = out[:, mid:] + dot(v_h[:, mid:], (e_c * part_b).astype(bf16))
                outs.append(jnp.concatenate([out[:, :mid], late], axis=1))
            attended[rows, at[0]] = jnp.concatenate(outs, axis=0).T.astype(bf16)
        return carry

    lax.fori_loop(0, HEADS // 2, step, 0, unroll=3)
    for copy in copies:
        copy.wait()


def middle_kernel(det, labels, class_slot, hidden0, attended, w_out, gain2, shift2, w_fc1, b_fc1, w_fc2, b_fc2,
                  gainf, shiftf, w_head_t, b_head, runs, cot_runs, valid_runs, came,
                  hidden1, normed2, act, slope, d_hidden2, part_in, lat_keep, lat_send,
                  short, grad_head_t, facts):
    x, _, _, _ = where()
    items = came.shape[0]
    feat = runs.shape[1]
    width = w_out.shape[0]
    span = came.shape[2]
    length = 2 * span
    hidden1[...] = hidden0[...] + dot(attended[...], w_out[...])
    gain, shift = row_of(gain2), row_of(shift2)
    for i in range(items):
        rows = slice(i * length, (i + 1) * length)
        unit, _ = centered(hidden1[rows, :])
        normed2[rows, :] = (unit * gain + shift).astype(bf16)
    total = None
    for j in range(w_fc1.shape[1] // width):
        cols = slice(j * width, (j + 1) * width)
        up = dot(normed2[...], w_fc1[:, cols]) + b_fc1[cols].reshape(1, width).astype(f32)
        square = up * up
        half = 0.5 * jnp.tanh(up * (GELU_A + GELU_A * GELU_B * square)) + 0.5
        value = up * half
        act[:, cols] = value.astype(bf16)
        slope[:, cols] = (
            half + 2.0 * value * (1.0 - half) * (GELU_A + 3.0 * GELU_A * GELU_B * square)
        ).astype(bf16)
        part = dot(act[:, cols], w_fc2[cols, :])
        total = part if total is None else total + part
    hidden2 = hidden1[...] + total + row_of(b_fc2)
    unit, inverse_dev = centered(hidden2)
    gain = row_of(gainf)
    normed3 = (unit * gain + row_of(shiftf)).astype(bf16)
    bias = jnp.broadcast_to(row_of(b_head), (8, 2 * feat)).T[:, :1]
    head = dot(w_head_t[...], normed3, 1, 1) + bias
    short[...] = jnp.zeros(short.shape, f32)
    d_heads = []
    sums = [jnp.zeros((1, 1), f32), jnp.zeros((1, 1), f32), jnp.full((1, 1), -1e30, f32)]
    for i in range(items):
        cols = slice(i * length, (i + 1) * length)
        source = x * items + i
        given = both_halves(x, runs[source].astype(f32), came[i, :feat])
        cot = both_halves(x, cot_runs[source], came[i, feat : 2 * feat])
        valid = both_halves(
            x, valid_runs[source].astype(f32), came[i, 2 * feat : 2 * feat + 1]
        )
        shift_part = head[:feat, cols]
        log_scale = head[feat:, cols]
        inverse = jnp.exp(-log_scale)
        moved = (given - shift_part) * inverse
        latent = valid * moved + (1.0 - valid) * given
        d_moved = valid * cot
        d_heads.append(
            jnp.concatenate(
                [-d_moved * inverse, -d_moved * moved - valid * det[source]], axis=0
            ).astype(bf16)
        )
        part_in[:, cols] = cot * (1.0 - valid) + d_moved * inverse
        counted = valid * log_scale
        item_sum = jnp.sum(jnp.sum(counted, axis=1, keepdims=True), axis=0, keepdims=True)
        sums[0] = sums[0] + item_sum
        sums[1] = sums[1] + jnp.sum(valid, axis=1, keepdims=True) * feat
        tops = jnp.where(valid > 0, log_scale, -1e30)
        tops = jnp.max(jnp.max(tops, axis=1, keepdims=True), axis=0, keepdims=True)
        sums[2] = jnp.maximum(sums[2], tops)
        low, high = latent[:, :span], latent[:, span:]
        logdet = jnp.broadcast_to(-item_sum, (8, span))
        lat_keep[i, :feat] = jnp.where(x == 0, low, high)
        lat_send[i, :feat] = jnp.where(x == 0, high, low)
        lat_keep[i, feat:] = logdet
        lat_send[i, feat:] = logdet
    lane = lax.broadcasted_iota(jnp.int32, facts.shape, 1)
    row = jnp.zeros(facts.shape, f32)
    for k, value in enumerate(sums):
        for j in range(3):
            piece = value.astype(bf16).astype(f32)
            value = value - piece
            row = jnp.where(lane == 3 * k + j, piece, row)
    for i in range(items):
        slot = class_slot[labels[x * items + i]]
        row = jnp.where(lane == 9 + i, (slot // 32).astype(f32), row)
        row = jnp.where(lane == 9 + items + i, (slot % 32).astype(f32), row)
    facts[...] = row
    d_head = jnp.concatenate(d_heads, axis=1)
    grad_head_t[...] = dot(d_head, normed3)
    short[ROW["bh"] : ROW["bh"] + 1, : 2 * feat] = dot(
        jnp.ones((8, d_head.shape[1]), bf16), d_head, 1, 1
    )[:1]
    d_normed3 = dot(d_head, w_head_t[...], 0, 0)
    short[ROW["fg"] : ROW["fg"] + 1, :] = col_sum(d_normed3 * unit)
    short[ROW["fs"] : ROW["fs"] + 1, :] = col_sum(d_normed3)
    pulled = norm_pull(d_normed3, unit, inverse_dev, gain)
    d_hidden2[...] = pulled
    short[ROW["b2"] : ROW["b2"] + 1, :] = col_sum(pulled.astype(bf16).astype(f32))


def split_by(bit, block, keep, send, half):
    low, high = block[:half], block[half:]
    keep[...] = jnp.where(bit == 0, low, high).astype(keep.dtype)
    send[...] = jnp.where(bit == 0, high, low).astype(send.dtype)


def split_groups(core, block, first, keep, send):
    group = keep.shape[1]
    for k in range(block.shape[0] // (2 * group)):
        rows = block[2 * group * k : 2 * group * (k + 1)]
        split_by(core, rows, keep.at[first + k], send.at[first + k], group)


STEP = 384


def fc2_kernel(first, act, d_hidden2, keep, send):
    _, core, _, _ = where()
    d_mlp = d_hidden2[...].astype(bf16)
    for j in range(2 * keep.shape[0] * keep.shape[1] // STEP):
        at = (first + j) * STEP
        block = dot(act[:, at : at + STEP], d_mlp, 0, 0)
        split_groups(core, block, j * STEP // (2 * keep.shape[1]), keep, send)


def fc1_kernel(half, d_hidden2, w_fc2, slope, normed2, w_fc1, *refs):
    before, (keep, send, total_out, bias) = refs[:-4], refs[-4:]
    _, core, _, _ = where()
    width = normed2.shape[1]
    d_mlp = d_hidden2[...].astype(bf16)
    total = before[0][...] if before else None
    count = w_fc1.shape[1] // 2 // width
    for j in range(count):
        at = (half * count + j) * width
        cols = slice(at, at + width)
        d_up = (dot(d_mlp, w_fc2[cols, :], 1, 1) * slope[:, cols].astype(f32)).astype(bf16)
        bias[j : j + 1, :] = col_sum(d_up.astype(f32))
        for m in range(width // STEP):
            block = dot(d_up[:, m * STEP : (m + 1) * STEP], normed2[...], 0, 0)
            split_groups(core, block, (j * width + m * STEP) // (2 * keep.shape[1]), keep, send)
        part = dot(d_up, w_fc1[:, cols], 1, 1)
        total = part if total is None else total + part
    total_out[...] = total


def back_kernel(d_hidden2, total_in, hidden1, gain2, w_out, short_in, bias_a, bias_b,
                d_hidden1, short, d_out, d_attended):
    short[...] = short_in[...]
    n = bias_a.shape[0]
    short[ROW["b1"] : ROW["b1"] + n, :] = bias_a[...]
    short[ROW["b1"] + n : ROW["b1"] + 2 * n, :] = bias_b[...]
    unit, inverse_dev = centered(hidden1[...])
    total = total_in[...]
    short[ROW["n2g"] : ROW["n2g"] + 1, :] = col_sum(total * unit)
    short[ROW["n2s"] : ROW["n2s"] + 1, :] = col_sum(total)
    h1 = d_hidden2[...] + norm_pull(total, unit, inverse_dev, row_of(gain2))
    d_hidden1[...] = h1
    low = h1.astype(bf16)
    d_out[...] = low
    d_attended[...] = dot(low, w_out[...], 1, 1).astype(bf16)


def out_kernel(attended, d_out, grad_head_t, keep, send):
    _, core, _, _ = where()
    grad_out = dot(attended[...], d_out[...], 0, 0)
    half, width = keep.shape
    rest = 2 * half - grad_out.shape[0] - grad_head_t.shape[0]
    block = jnp.concatenate([grad_out, grad_head_t[...], jnp.zeros((rest, width), f32)], axis=0)
    split_by(core, block, keep, send, half)


def lower_keys(n):
    key_at = lax.broadcasted_iota(jnp.int32, (n, n), 0)
    return key_at <= lax.broadcasted_iota(jnp.int32, (n, n), 1)


def attention_back_kernel(qkv, lse, d_attended, d_qkv):
    rows_all, width = d_attended.shape
    items = lse.shape[0]
    length = rows_all // items
    mid = length // 2
    allowed = lower_keys(mid)

    def step(p, carry):
        for i in range(items):
            rows = slice(i * length, (i + 1) * length)
            at = [pl.ds(pl.multiple_of(j * width + p * 128, 128), 128) for j in range(3)]
            q, k, v = (qkv[rows, at[j]] for j in range(3))
            q = q * 0.125
            d_o = d_attended[rows, at[0]]
            first = lax.broadcasted_iota(jnp.int32, q.shape, 1) < 64
            none = jnp.zeros_like(q)
            total = [None] * 6
            for h in range(2):
                mine = first if h == 0 else ~first
                qh = jnp.where(mine, q, none)
                kh = jnp.where(mine, k * 0.125, none)
                dh = jnp.where(mine, d_o, none)
                log_sum = lse[i, pl.ds(p * 2 + h, 1), :]
                log_a, log_b = log_sum[:, :mid], log_sum[:, mid:]
                s = dot(k[:mid], qh, 1, 1)
                s_c = dot(k[mid:], qh[mid:], 1, 1)
                p_a = jnp.exp(jnp.where(allowed, s[:, :mid], -1e30) - log_a)
                p_b = jnp.exp(s[:, mid:] - log_b)
                p_c = jnp.exp(jnp.where(allowed, s_c, -1e30) - log_b)
                d_p = dot(v[:mid], dh, 1, 1)
                d_a, d_b = d_p[:, :mid], d_p[:, mid:]
                d_c = dot(v[mid:], dh[mid:], 1, 1)
                delta_a = jnp.sum(p_a * d_a, axis=0, keepdims=True)
                delta_b = jnp.sum(p_b * d_b + p_c * d_c, axis=0, keepdims=True)
                s_a = (p_a * (d_a - delta_a)).astype(bf16)
                s_b = (p_b * (d_b - delta_b)).astype(bf16)
                s_c = (p_c * (d_c - delta_b)).astype(bf16)
                s_ab = jnp.concatenate([s_a, s_b], axis=1)
                p_ab = jnp.concatenate([p_a.astype(bf16), p_b.astype(bf16)], axis=1)
                parts = [
                    dot(s_a, kh[:mid], 0, 0),
                    dot(jnp.concatenate([s_b, s_c], axis=0), kh, 0, 0),
                    dot(s_ab, qh),
                    dot(s_c, qh[mid:]),
                    dot(p_ab, dh),
                    dot(p_c.astype(bf16), dh[mid:]),
                ]
                total = [b if a is None else a + b for a, b in zip(total, parts)]
            low, high = slice(i * length, i * length + mid), slice(i * length + mid, (i + 1) * length)
            for j in range(3):
                d_qkv[low, at[j]] = total[2 * j].astype(bf16)
                d_qkv[high, at[j]] = total[2 * j + 1].astype(bf16)
        return carry

    lax.fori_loop(0, HEADS // 2, step, 0, unroll=6)


def qkv_kernel(normed1, d_qkv, keep, send):
    _, core, _, _ = where()
    width = normed1.shape[1]
    half = keep.shape[0]
    for m in range(width // STEP):
        block = dot(normed1[:, m * STEP : (m + 1) * STEP], d_qkv[...], 0, 0)
        for j in range(3):
            part = block[:, j * width : (j + 1) * width]
            at = j * width + m * STEP
            inside = at % half

            @pl.when(core == at // half)
            def _():
                keep[inside : inside + STEP, :] = part

            @pl.when(core != at // half)
            def _():
                send[inside : inside + STEP, :] = part.astype(bf16)


def rest_kernel(items, d_qkv, w_qkv, hidden0, d_hidden1, gain1, shifted_t, short_in, facts,
                keep, send, short, d_low_out, extra):
    _, core, _, _ = where()
    width = hidden0.shape[1]
    length = hidden0.shape[0] // items
    d_normed1 = dot(d_qkv[...], w_qkv[...], 1, 1)
    unit, inverse_dev = centered(hidden0[...])
    short[...] = short_in[...]
    short[ROW["n1g"] : ROW["n1g"] + 1, :] = col_sum(d_normed1 * unit)
    short[ROW["n1s"] : ROW["n1s"] + 1, :] = col_sum(d_normed1)
    d0 = d_hidden1[...] + norm_pull(d_normed1, unit, inverse_dev, row_of(gain1))
    d_low = d0.astype(bf16)
    d_low_out[...] = d_low
    extra[...] = jnp.zeros(extra.shape, bf16)
    d_pos, whole = None, None
    for i in range(items):
        mine = d0[i * length : (i + 1) * length]
        d_pos = mine if d_pos is None else d_pos + mine
        item = col_sum(mine)
        whole = item if whole is None else whole + item
        extra[i : i + 1, :] = item.astype(bf16)
    extra[items : items + 1, :] = facts[...].astype(bf16)
    short[ROW["bp"] : ROW["bp"] + 1, :] = whole
    d_patch = dot(shifted_t[...], d_low)
    half = keep.shape[0]
    rest = 2 * half - d_pos.shape[0] - d_patch.shape[0]
    block = jnp.concatenate([d_pos, d_patch, jnp.zeros((rest, width), f32)], axis=0)
    split_by(core, block, keep, send.at[:half], half)
    short[...] = put_short(send, half, short[...])


def inputs_kernel(d_low, w_patch, part_in, lat_keep, lat_send, in_keep, in_send):
    x, _, _, _ = where()
    items, done, span = lat_keep.shape
    length = 2 * span
    in_keep[:, :done] = lat_keep[...]
    in_send[:, :done] = lat_send[...]
    d_shift = dot(w_patch[...], d_low[...], 1, 1)
    for i in range(items):
        cols = slice(i * length, (i + 1) * length)
        moved = d_shift[:, cols]
        lane = lax.broadcasted_iota(jnp.int32, moved.shape, 1)
        back = jnp.where(lane == length - 1, 0.0, pltpu.roll(moved, length - 1, 1))
        grad = part_in[:, cols] + back
        in_keep[i, done:] = jnp.where(x == 0, grad[:, :span], grad[:, span:])
        in_send[i, done:] = jnp.where(x == 0, grad[:, span:], grad[:, :span])


def put_short(send, at, short):
    n = short.shape[0]
    high = short.astype(bf16)
    low = (short - high.astype(f32)).astype(bf16)
    send[at : at + n, :] = high
    send[at + n : at + 2 * n, :] = low
    return high.astype(f32) + low.astype(f32)


def take_short(came, at, n):
    return came[at : at + n, :].astype(f32) + came[at + n : at + 2 * n, :].astype(f32)


def split_sum(bit, pairs, kept, send):
    mine = my_bit(bit)
    n = 0
    for keep, came in pairs:
        for a in range(keep.shape[0]):
            kept[n] = keep[a, mine] + came[a, mine].astype(f32)
            send[n] = (keep[a, 1 - mine] + came[a, 1 - mine].astype(f32)).astype(bf16)
            n += 1


def stage_kernel(bits, counts, *refs):
    n = 2 * sum(counts)
    ins, outs = refs[:n], refs[n:]
    for i, (bit, count) in enumerate(zip(bits, counts)):
        pairs = [(ins[2 * j], ins[2 * j + 1]) for j in range(count)]
        ins = ins[2 * count :]
        split_sum(bit, pairs, outs[2 * i], outs[2 * i + 1])


def stage(line, name, *parts, after=(), cost=1):
    outs, args = [], []
    for bit, pairs in parts:
        _, _, b, w = pairs[0][0].shape
        total = sum(keep.shape[0] for keep, _ in pairs)
        outs += [((total, b, w), f32), ((total, b, w), bf16)]
        for pair in pairs:
            args += list(pair)
    bits, counts = tuple(p[0] for p in parts), tuple(len(p[1]) for p in parts)
    return line.call(partial(stage_kernel, bits, counts), outs, args, name, cost, 8, after=after, pinned=True)


def add_kernel(keep, came, *outs):
    at = 0
    for out in outs:
        n = out.shape[0]
        out[...] = keep[at : at + n, :] + came[at : at + n, :].astype(f32)
        at += n


def bulk0a_kernel(qk, qc, keep_a, send_a):
    x, _, _, _ = where()
    na = keep_a.shape[0]
    mine, away = pl.ds(pl.multiple_of(x * na, na), na), pl.ds(pl.multiple_of((1 - x) * na, na), na)
    keep_a[...] = qk[mine, :] + qc[mine, :].astype(f32)
    send_a[...] = (qk[away, :] + qc[away, :].astype(f32)).astype(bf16)


def bulk0b_kernel(low, qk, qc, ek, ec, lk, lc, short_in, keep_b, send_b, short):
    _, _, y, _ = where()
    nb = keep_b.shape[0]
    nq, nl = qk.shape[0], lk.shape[0]
    total = short_in[...] + take_short(lc, nl, short.shape[0])
    parts = [
        qk[low:nq, :] + qc[low:nq, :].astype(f32),
        ek[...] + ec[...].astype(f32),
        lk[...] + lc[:nl, :].astype(f32),
    ]
    block = jnp.concatenate(parts, axis=0)
    split_by(y, block, keep_b, send_b.at[:nb], nb)
    short[...] = put_short(send_b, nb, total)


def bulk1_kernel(ka, ca, kb, cb, short_in, keep_a, keep_b, send_a, send_b, short):
    x, _, y, _ = where()
    na, nb = keep_a.shape[0], keep_b.shape[0]
    ns = short.shape[0]
    total = short_in[...] + take_short(cb, 2 * nb, ns)
    for bit, n, k, c, keep, send in ((y, na, ka, ca, keep_a, send_a), (x, nb, kb, cb, keep_b, send_b)):
        mine, away = pl.ds(pl.multiple_of(bit * n, n), n), pl.ds(pl.multiple_of((1 - bit) * n, n), n)
        keep[...] = k[mine, :] + c[mine, :].astype(f32)
        send[:n, :] = (k[away, :] + c[away, :].astype(f32)).astype(bf16)
    short[...] = put_short(send_b, nb, total)


def quarter_of(block, at):
    out = block[0:4]
    for j in range(1, 4):
        out = jnp.where(at == j, block[4 * j : 4 * j + 4], out)
    return out


def high_low(rows):
    high = rows.astype(bf16).astype(f32)
    return jnp.concatenate([high, rows - high], axis=0).astype(bf16)


def bulk2_kernel(ka, ca, kb, cb, short_in, keep, send1, send2, send3, short):
    _, _, _, z = where()
    na, nb = ka.shape[0] // 4, kb.shape[0] // 4
    n = na + nb
    total = short_in[...] + take_short(cb, 4 * nb, short_in.shape[0])
    for m, out in enumerate((keep, send1, send2, send3)):
        at = z ^ m
        ra = pl.ds(pl.multiple_of(at * na, na), na)
        rb = pl.ds(pl.multiple_of(at * nb, nb), nb)
        out[:na, :] = (ka[ra, :] + ca[ra, :].astype(f32)).astype(out.dtype)
        out[na:n, :] = (kb[rb, :] + cb[rb, :].astype(f32)).astype(out.dtype)
        quarter = quarter_of(total, at)
        if m == 0:
            short[...] = jnp.concatenate([quarter, quarter], axis=0)
        else:
            both = high_low(quarter)
            out[n : n + 16, :] = jnp.concatenate([both, both], axis=0)


def bulk3_kernel(keep, c1, c2, c3, short_in, extra, piece):
    n = keep.shape[0]
    total = keep[...]
    quarter = short_in[0:4, :]
    for c in (c1, c2, c3):
        total = total + c[:n, :].astype(f32)
        both = c[n : n + 16, :].astype(f32)
        quarter = quarter + (both[0:4] + both[4:8])
    piece[:n, :] = total.astype(bf16)
    piece[n:, :] = jnp.concatenate([extra[...][0:8], high_low(quarter)], axis=0)


def join0_kernel(own, c1, c2, c3, part_a, part_b, short):
    _, _, _, z = where()
    na, nb = part_a.shape[0] // 4, part_b.shape[0] // 4
    quarters = []
    for m, c in enumerate((own, c1, c2, c3)):
        at = z ^ m
        part_a[pl.ds(pl.multiple_of(at * na, na), na), :] = c[:na, :]
        part_b[pl.ds(pl.multiple_of(at * nb, nb), nb), :] = c[na:, :]
        both = c[na + nb - 16 :, :].astype(f32)
        quarters.append((at, both[8:12] + both[12:16]))
    rows = []
    for j in range(4):
        row = quarters[0][1]
        for at, quarter in quarters[1:]:
            row = jnp.where(at == j, quarter, row)
        rows.append(row)
    short[...] = jnp.concatenate(rows, axis=0)


def join1_kernel(own_a, came_a, own_b, came_b, part_a, part_b):
    x, _, y, _ = where()
    n = own_a.shape[0]
    for bit, own, came, part in ((y, own_a, came_a, part_a), (x, own_b, came_b, part_b)):
        part[pl.ds(pl.multiple_of(bit * n, n), n), :] = own[...]
        part[pl.ds(pl.multiple_of((1 - bit) * n, n), n), :] = came[...]


def write_kernel(geo, first, jobs, *refs):
    n_out = 5
    quarters = refs[: len(jobs)]
    refs = refs[len(jobs) :]
    if not first:
        refs = refs[n_out:]
    write_end(write_start(geo, jobs, quarters, *refs))


def early_kernel(geo, jobs, own_a, core_a, own_b, core_b, *refs):
    refs = refs[5:]
    outs, (class_part, facts, wide, sems) = refs[:5], refs[5:]
    waits = write_start(geo, jobs, (core_a, core_b), *outs, wide, sems)
    _, core, y, _ = where()
    facts[...] = jnp.zeros(facts.shape, f32)
    class_part[...] = class_rows_of(geo, class_part.shape, [(own_b, core, y), (core_b, 1 - core, y)], facts)
    write_end(waits)


def finish_kernel(geo, jobs, *refs):
    quarters = refs[: len(jobs)]
    came_b, class_part, facts_part, fc_keep, fc_came = refs[len(jobs) : len(jobs) + 5]
    refs = refs[len(jobs) + 10 :]
    outs, (own_fc2, own_fc1, class_own, mean, top, wide, facts, sems) = refs[:5], refs[5:]
    waits = write_start(geo, jobs, quarters, *outs, wide, sems)
    _, core, y, _ = where()
    facts[...] = facts_part[...]
    class_own[...] = class_part[...] + class_rows_of(
        geo, class_own.shape, [(came_b, core, 1 - y), (quarters[1], 1 - core, 1 - y)], facts
    )
    every = facts[...]
    summed = col_sum(every)
    scale_sum = summed[:, 0:1] + summed[:, 1:2] + summed[:, 2:3]
    count = summed[:, 3:4] + summed[:, 4:5] + summed[:, 5:6]
    tops = every[:, 6:7] + every[:, 7:8] + every[:, 8:9]
    mean[...] = scale_sum / count
    top[...] = jnp.max(tops, axis=0, keepdims=True)
    add_kernel(fc_keep, fc_came, own_fc2, own_fc1)
    write_end(waits)


def write_end(waits):
    for taken, move in waits:
        if taken is None:
            move.wait()
        else:
            pl.when(taken)(move.wait)


def write_start(geo, jobs, quarters, g_qkv, g_out, g_pos, g_head, g_patch, wide, sems):
    x, core, y, _ = where()
    width = g_out.shape[0]
    half_q, half_e, half_l = geo["half_q"], geo["half_e"], geo["half_l"]
    nb, ne = geo["nb"], geo["extra"]
    feat = g_patch.shape[0]
    at, sem = 0, 0
    waits = []

    def copy(rows, target):
        nonlocal sem
        c = pltpu.make_async_copy(wide.at[rows], target, sems.at[sem])
        sem += 1
        return c

    for quarter, (part, other_core, other_half) in zip(quarters, jobs):
        c = 1 - core if other_core else core
        n = quarter.shape[0]
        if part == "a":
            h = 1 - x if other_half else x
            wide[at : at + n, :] = quarter[...].astype(f32)
            for k in range(0, n, 128):
                q = c * half_q + h * n + k
                third, row = q // width, q % width
                target = g_qkv.at[
                    pl.ds(pl.multiple_of(row, 128), 128),
                    pl.ds(pl.multiple_of(third * width, 128), width),
                ]
                waits.append((None, copy(slice(at + k, at + k + 128), target)))
                waits[-1][1].start()
            at += n
        else:
            h = 1 - y if other_half else y
            for k in range(n // (nb + ne)):
                wide[at + k * nb : at + (k + 1) * nb, :] = quarter[
                    k * (nb + ne) : k * (nb + ne) + nb, :
                ].astype(f32)
            left = half_q - 2 * geo["na"]
            rows = n // (nb + ne) * nb
            for case_c in range(2):
                for case_h in range(2):
                    spans = []
                    if case_h == 0:
                        spans.append((0, left, "q", case_c * half_q + 2 * geo["na"]))
                        spans.append((left, rows - left, "e", case_c * half_e))
                    else:
                        spans.append((0, half_e - (rows - left), "e", case_c * half_e + rows - left))
                        spans.append((half_e - (rows - left), half_l, "l", case_c * half_l))
                    moves = []
                    for start, size, kind, place in spans:
                        pieces = {
                            "q": [(case_c * half_q + 2 * geo["na"], left, g_qkv)],
                            "e": [(0, width, g_out), (width, 2 * feat, g_head)],
                            "l": [(0, g_pos.shape[0], g_pos), (g_pos.shape[0], feat, g_patch)],
                        }[kind]
                        for low, long, ref in pieces:
                            a, b = max(place, low), min(place + size, low + long)
                            if a >= b:
                                continue
                            source = slice(at + start + a - place, at + start + b - place)
                            if kind == "q":
                                third, row = a // width, a % width
                                target = g_qkv.at[row : row + b - a, third * width : (third + 1) * width]
                            else:
                                target = ref.at[a - low : b - low]
                            moves.append(copy(source, target))
                    taken = (c == case_c) & (h == case_h)

                    @pl.when(taken)
                    def _(moves=moves):
                        for move in moves:
                            move.start()

                    waits += [(taken, move) for move in moves]
            at += rows
    return waits


def class_rows_of(geo, shape, sources, facts):
    nb, ne, items = geo["nb"], geo["extra"], geo["items"]
    me = lax.axis_index("dp") * 2 + lax.axis_index("seq")
    want = (me * shape[0] + lax.broadcasted_iota(jnp.int32, (shape[0], 1), 0)).astype(f32)
    total = jnp.zeros(shape, f32)
    for q, c, h in sources:
        for k in range(8):
            block = q[k * (nb + ne) + nb : (k + 1) * (nb + ne), :].astype(f32)
            fact = block[items : items + 1]
            facts[pl.ds((c * 2 + h) * 8 + k, 1), :] = fact
            for i in range(items):
                slot = fact[:, 9 + i : 10 + i] * 32 + fact[:, 9 + items + i : 10 + items + i]
                total = total + jnp.where(want == slot, 1.0, 0.0) * block[i : i + 1]
    return total


class Cube:
    def __init__(self):
        self.size = lax.axis_size("dp") * lax.axis_size("seq")
        self.nbits = self.size.bit_length() - 1
        self.me = lax.axis_index("dp") * lax.axis_size("seq") + lax.axis_index("seq")
        self.bit = [(self.me >> k) & 1 for k in range(self.nbits)]

    def send(self, block, mask):
        return lax.ppermute(block, AXES, [(i, i ^ mask) for i in range(self.size)])

    def start(self, full, bits):
        rows = full.shape[0] >> len(bits)
        return full.reshape((2,) * len(bits) + (rows, full.shape[1])), list(bits)

    def scatter(self, block, left):
        for bit in list(left):
            axis = left.index(bit)
            mine = lax.dynamic_index_in_dim(block, self.bit[bit], axis, keepdims=False)
            away = lax.dynamic_index_in_dim(block, 1 - self.bit[bit], axis, keepdims=False)
            block = mine + self.send(away.astype(bf16), 1 << bit).astype(f32)
            left = [b for b in left if b != bit]
        return block

    def add_up(self, block, bits):
        for k in bits:
            block = block + self.send(block, 1 << k)
        return block

    def gather(self, block, bits):
        for k in reversed(bits):
            came = self.send(block, 1 << k)
            block = jnp.where(self.bit[k] == 0, jnp.stack([block, came]), jnp.stack([came, block]))
        return block


def local(
    patches, labels, valid_mask, class_slot, w_patch, b_patch, pos_embed, class_embed,
    norm1_gain, norm1_shift, w_qkv, w_out, norm2_gain, norm2_shift, w_fc1, b_fc1, w_fc2, b_fc2,
    final_gain, final_shift, w_head, b_head, cot_latent, cot_logdet,
):
    cube = Cube()
    line = Line()
    seq_n = lax.axis_size("seq")
    assert seq_n == 2
    seq = lax.axis_index("seq")
    held, span, feat = patches.shape
    items = held // seq_n
    length = span * seq_n
    width = w_out.shape[0]
    ff = w_fc1.shape[1]
    rows = items * length
    classes = class_embed.shape[0]
    chunk = ff // cube.size
    group = 2 * chunk
    fast = cube.size == 32

    runs = patches.transpose(0, 2, 1)
    cot_runs = cot_latent.transpose(0, 2, 1)
    valid_runs = valid_mask[:, None, :]
    w_head_t = w_head.T
    (packed,) = line.call(
        prep_kernel, [((items, 2 * feat + 8, span), f32)], [runs, cot_runs, valid_mask], "prep", 1, 1,
        places={0: HBM, 1: HBM, 2: HBM},
        scratch=[pltpu.VMEM((items, feat, span), bf16), pltpu.VMEM((held, span), jnp.int32),
                 pltpu.SemaphoreType.DMA((3,))],
    )
    came = cube.send(packed, 1)
    big = 2.0 * rows * width * ff
    firsts = line.call(
        fetch_kernel,
        [((items, feat, span), bf16), ((items, 16, width), bf16), ((width,), bf16), ((width,), bf16),
         ((width,), bf16), ((length, width), bf16), ((feat, width), bf16), (w_qkv.shape, bf16)],
        [labels, packed, runs, class_embed, b_patch, norm1_gain, norm1_shift, pos_embed, w_patch, w_qkv],
        "fetch", 1, 2, places={0: SMEM, 1: ANY} | {i: HBM for i in range(2, 10)},
        scratch=[pltpu.SemaphoreType.DMA((items + 10,))], tied=False,
    )
    w_qkv = firsts[-1]
    hidden0, normed1, qkv, shifted_t, attended, lse, w_out, w_fc1, w_fc2 = line.call(
        front_kernel,
        [((rows, width), f32), ((rows, width), bf16), ((rows, 3 * width), bf16), ((feat, rows), bf16),
         ((rows, width), bf16), ((items, HEADS, length), f32)]
        + [(w.shape, bf16) for w in (w_out, w_fc1, w_fc2)],
        [labels, came] + list(firsts) + [w_out, w_fc1, w_fc2],
        "front", 1, 6, places={0: SMEM} | {i: HBM for i in range(10, 13)},
        scratch=[pltpu.SemaphoreType.DMA((3,))],
    )
    n_short = 16
    (hidden1, normed2, act, slope, d_hidden2, part_in, lat_keep, lat_send, short, grad_head_t, facts) = line.call(
        middle_kernel,
        [((rows, width), f32), ((rows, width), bf16), ((rows, ff), bf16), ((rows, ff), bf16),
         ((rows, width), f32), ((feat, rows), f32), ((items, feat + 8, span), f32),
         ((items, feat + 8, span), f32), ((n_short, width), f32), ((2 * feat, width), f32),
         ((1, width), f32)],
        [cot_logdet, labels, class_slot, hidden0, attended, w_out, norm2_gain, norm2_shift, w_fc1, b_fc1,
         w_fc2, b_fc2, final_gain, final_shift, w_head_t, b_head, runs, cot_runs, valid_runs, came],
        "middle", 1, 8, places={0: SMEM, 1: SMEM, 2: SMEM},
    )
    groups = ff // (4 * group)
    pieces = [((groups, group, width), f32), ((groups, group, width), bf16)]

    def fc2_part(first, count):
        n = count * STEP // (2 * group)
        return line.call(
            partial(fc2_kernel, first), [((n, group, width), f32), ((n, group, width), bf16)],
            [act, d_hidden2], "fc2", 1, 4,
        )

    def fc1_half(h, before):
        return line.call(
            partial(fc1_kernel, h),
            pieces + [((rows, width), f32), ((ff // width // 2, width), f32)],
            [d_hidden2, w_fc2, slope, normed2, w_fc1] + before, "fc1", 1, 6,
        )

    def four(block):
        return block.reshape(-1, 2, chunk, width)

    half_e, half_l, half_q = 448, 192, 3 * width // 2
    keep20, send20 = fc2_part(0, 4)
    came20 = cube.send(send20, 2)
    keep21, send21 = fc2_part(4, 4)
    came21 = cube.send(send21, 2)
    keep10, send10, total, bias0 = fc1_half(0, [])
    came10 = cube.send(send10, 2)
    if fast:
        k20, s20 = stage(line, "fc2_core", (0, [(four(keep20), four(came20))]))
        c20 = cube.send(s20, 1)
    keep11, send11, total, bias1 = fc1_half(1, [total])
    came11 = cube.send(send11, 2)
    if fast:
        k21, s21 = stage(line, "fc2_core", (0, [(four(keep21), four(came21))]))
    def by_y(block):
        return block.reshape(2, 2, group, width)

    if fast:
        k10, s10 = stage(line, "fc1_core", (2, [(by_y(keep10), by_y(came10))]))
        c10 = cube.send(s10, 4)
    d_hidden1, short, d_out, d_attended = line.call(
        back_kernel,
        [((rows, width), f32), ((n_short, width), f32), ((rows, width), bf16), ((rows, width), bf16)],
        [d_hidden2, total, hidden1, norm2_gain, w_out, short, bias0, bias1],
        "back", 1, 6,
    )

    if fast:
        k11, s11 = stage(line, "fc1_core", (2, [(by_y(keep11), by_y(came11))]))
    (d_qkv,) = line.call(
        attention_back_kernel, [((rows, 3 * width), bf16)], [qkv, lse, d_attended],
        "attention_back", 1, 4,
    )
    qkeep, qsend = line.call(
        qkv_kernel, [((half_q, width), f32), ((half_q, width), bf16)], [normed1, d_qkv],
        "qkv_grad", 1, 6,
    )
    qcame = cube.send(qsend, 2)
    ekeep, esend = line.call(
        out_kernel, [((half_e, width), f32), ((half_e, width), bf16)], [attended, d_out, grad_head_t], "out", 1, 5
    )
    ecame = cube.send(esend, 2)
    lkeep, lsend, short, d_low, extra = line.call(
        partial(rest_kernel, items),
        [((half_l, width), f32), ((half_l + 2 * n_short, width), bf16), ((n_short, width), f32),
         ((rows, width), bf16), ((16, width), bf16)],
        [d_qkv, w_qkv, hidden0, d_hidden1, norm1_gain, shifted_t, short, facts],
        "rest", 3e10, 6, after=[c20, c10] if fast else [],
    )
    lcame = cube.send(lsend, 2)

    def swap_inputs():
        return line.call(
            inputs_kernel, [((items, 2 * feat + 8, span), f32)] * 2, [d_low, w_patch, part_in, lat_keep, lat_send],
            "inputs", 1, 4,
        )


    if fast:
        ns2 = 2 * n_short

        def two(na, nb):
            return [((na, width), f32), ((nb, width), f32), ((na, width), bf16), ((nb + ns2, width), bf16),
                    ((n_short, width), f32)]

        na, nb = 512, 384
        ka, sa = line.call(
            bulk0a_kernel, [((na, width), f32), ((na, width), bf16)], [qkeep, qcame], "bulk0a", 1, 10
        )
        ca = cube.send(sa, 1)
        kb, sb, short = line.call(
            partial(bulk0b_kernel, 2 * na),
            [((nb, width), f32), ((nb + ns2, width), bf16), ((n_short, width), f32)],
            [qkeep, qcame, ekeep, ecame, lkeep, lcame, short], "bulk0b", 1, 10,
        )
        cb = cube.send(sb, 4)
        back_keep, back_send = swap_inputs()
        ka, kb, sa, sb, short = line.call(
            bulk1_kernel, two(256, 192), [ka, ca, kb, cb, short], "bulk1", 1, 6
        )
        ca, cb = cube.send(sa, 4), cube.send(sb, 1)
        na, nb, ne = 64, 48, 16
        n = na + nb
        keep, z1, z2, z3, quarter = line.call(
            bulk2_kernel,
            [((n, width), f32)] + [((n + ne, width), bf16)] * 3 + [((8, width), f32)],
            [ka, ca, kb, cb, short], "bulk2", 1, 4,
        )
        z1, z2, z3 = cube.send(z1, 8), cube.send(z2, 16), cube.send(z3, 24)
        c21, c11 = cube.send(tie(s21, keep), 1), cube.send(tie(s11, keep), 4)
        def next_y(block):
            return block.reshape(-1, 2, chunk, width)

        k2, s2, k1, s1 = stage(
            line, "fc_second",
            (2, [(next_y(k20), next_y(c20)), (next_y(k21), next_y(c21))]),
            (0, [(next_y(k10), next_y(c10)), (next_y(k11), next_y(c11))]), cost=3e10,
        )
        c2, c1 = cube.send(s2, 4), cube.send(s1, 1)
        piece, = line.call(
            bulk3_kernel, [((n + ne, width), bf16)], [keep, z1, z2, z3, quarter, extra], "bulk3", 3e10, 4
        )
        g1, g2, g3 = cube.send(piece, 8), cube.send(piece, 16), cube.send(piece, 24)
        kf, sf = stage(
            line, "fc_third", (3, [(next_y(k2), next_y(c2)), (next_y(k1), next_y(c1))])
        )

        back_came = cube.send(tie(back_send, c2, c1), 1)
        part_a, part_b, short = line.call(
            join0_kernel, [((4 * na, width), bf16), ((4 * (nb + ne), width), bf16), ((n_short, width), f32)],
            [piece, g1, g2, g3], "join0", 1, 4, after=[back_came],
        )
        ca, cb = cube.send(part_a, 4), cube.send(part_b, 1)
        cf = cube.send(tie(sf, g1, g2, g3), 8)
        part_a, part_b = line.call(
            join1_kernel, [((8 * na, width), bf16), ((8 * (nb + ne), width), bf16)],
            [part_a, ca, part_b, cb], "join1", 1, 5,
        )
        short, back_came = tie(short, part_a), tie(back_came, part_a)
        ca, cb = cube.send(part_a, 1), cube.send(part_b, 4)
        xa, xb = cube.send(part_a, 2), cube.send(part_b, 2)
        geo = dict(na=8 * na, nb=nb, extra=ne, half_q=half_q, half_e=half_e, half_l=half_l, items=items)
        grads = write(
            line, geo, [("a", 0, 0), ("b", 0, 0)], [part_a, part_b], None, width, length, feat,
        )

        kf, sf = stage(line, "fc_fourth", (4, [(next_y(kf), next_y(cf))]))
        cf = cube.send(sf, 16)
        ya, yb = cube.send(ca, 2), cube.send(cb, 2)
        class_shape, fact_shape = (classes // cube.size, width), (cube.size, width)
        *grads, class_part, facts_part = finish(
            line, "early", early_kernel, geo, [("a", 1, 0), ("b", 1, 0)], [part_a, xa, part_b, xb], grads,
            [class_shape, fact_shape], 2, [], 10**10,
        )
        grads = write(line, geo, [("a", 0, 1), ("b", 0, 1)], [ca, cb], grads, width, length, feat)
        g_qkv, g_out, g_pos, g_head_t, g_patch, own_fc2, own_fc1, class_own, mean, top = finish(
            line, "finish", finish_kernel, geo, [("a", 1, 1), ("b", 1, 1)],
            [ya, yb, cb, class_part, facts_part, kf.reshape(2 * chunk, width), cf.reshape(2 * chunk, width)], grads,
            [(chunk, width), (chunk, width), class_shape, (1, 1), (1, 1)], 2, [pltpu.VMEM(fact_shape, f32)], 1,
        )
        mean, top = mean.reshape(()), top.reshape(())
    else:
        rest = [0] + list(range(2, cube.nbits))
        upper = list(range(cube.nbits - 1, 1, -1)) + [0]
        back_keep, back_send = swap_inputs()
        back_came = cube.send(back_send, 1)

        def owned(*parts):
            total = jnp.concatenate([k + c.astype(f32) for k, c in parts]).reshape(-1, width)
            return cube.scatter(*cube.start(total, upper))

        own_fc2 = owned((keep20, came20), (keep21, came21))
        own_fc1 = owned((keep10, came10), (keep11, came11))
        full = jnp.concatenate(
            [qkeep + qcame.astype(f32), ekeep + ecame.astype(f32), lkeep + lcame[:half_l].astype(f32)]
        )
        n_full = full.shape[0]
        full = jnp.pad(full, ((0, -n_full % (cube.size * 8)), (0, 0)))
        own = cube.scatter(*cube.start(full, upper))
        n_own = own.shape[0]
        got = cube.gather(jnp.concatenate([own.astype(bf16), extra]), [1] + upper)
        halves = got[..., :n_own, :].reshape(2, -1, width)[:, :n_full].astype(f32)
        short = cube.add_up(short, [1] + rest)
        q = halves[:, :half_q].reshape(3, width, width)
        g_qkv = jnp.concatenate([q[0], q[1], q[2]], axis=1)
        e = halves[:, half_q : half_q + half_e].reshape(-1, width)
        g_out, g_head_t = e[:width], e[width : width + 2 * feat]
        later = halves[:, half_q + half_e :].reshape(-1, width)
        g_pos, g_patch = later[:length], later[length : length + feat]
        extras = got[..., n_own : n_own + items + 1, :].reshape(cube.size, items + 1, width).astype(f32)
        sums = extras[:, :items].reshape(-1, width)
        facts = extras[:, items]
        mean = jnp.sum(facts[:, :3]) / jnp.sum(facts[:, 3:6])
        top = jnp.max(facts[:, 6] + facts[:, 7] + facts[:, 8])
        all_slots = (facts[:, 9 : 9 + items] * 32 + facts[:, 9 + items : 9 + 2 * items]).reshape(-1)
        own_rows = classes // cube.size
        wanted = (cube.me * own_rows + jnp.arange(own_rows)).astype(f32)
        hot = (wanted[:, None] == all_slots[None, :]).astype(bf16)
        class_own = dot(hot, sums.astype(bf16))

    out = jnp.where(
        seq == 0, jnp.concatenate([back_keep, back_came]), jnp.concatenate([back_came, back_keep])
    )
    latent_out = out[:, :feat].transpose(0, 2, 1)
    logdet_out = out[:, feat, 0]
    grad_in_out = out[:, feat + 8 :].transpose(0, 2, 1)
    b1_all = short[ROW["b1"] : ROW["b1"] + ff // width].reshape(-1)
    b1_own = lax.dynamic_slice_in_dim(b1_all, cube.me * chunk, chunk, 0)
    vec = {name: short[at] for name, at in ROW.items()}
    return (
        latent_out, logdet_out, grad_in_out, g_patch, vec["bp"], g_pos, class_own,
        vec["n1g"], vec["n1s"], g_qkv, g_out, vec["n2g"], vec["n2s"], own_fc1.T, b1_own, own_fc2,
        vec["b2"], vec["fg"], vec["fs"], g_head_t.T, vec["bh"][: 2 * feat], mean, top,
    )


def finish(line, name, body, geo, jobs, args, grads, shapes, n, scratch, cost):
    args = list(args)
    args[0] = tie(args[0], line.last)
    vmem, hbm = pl.BlockSpec(memory_space=VMEM), pl.BlockSpec(memory_space=ANY)
    width = grads[1].shape[0]
    got = pl.pallas_call(
        partial(body, geo, jobs),
        out_shape=[jax.ShapeDtypeStruct(g.shape, f32) for g in grads]
        + [jax.ShapeDtypeStruct(shape, f32) for shape in shapes],
        in_specs=[vmem] * len(args) + [hbm] * len(grads),
        out_specs=[hbm] * len(grads) + [vmem] * len(shapes),
        scratch_shapes=[pltpu.VMEM((512 * n, width), f32)] + scratch + [pltpu.SemaphoreType.DMA((16 * n,))],
        input_output_aliases={len(args) + i: i for i in range(len(grads))},
        compiler_params=pltpu.CompilerParams(vmem_limit_bytes=14 * 2**20),
        cost_estimate=pl.CostEstimate(flops=cost, bytes_accessed=1, transcendentals=0),
        name=name,
    )(*args, *grads)
    line.last = got[len(grads) - 1]
    return got


def write(line, geo, jobs, quarters, grads, width, length, feat, after=()):
    shapes = [(width, 3 * width), (width, width), (length, width), (2 * feat, width), (feat, width)]
    n = len(quarters)
    args = list(quarters)
    args[0] = tie(args[0], line.last, *after)
    aliases = {}
    if grads is not None:
        aliases = {n + i: i for i in range(len(shapes))}
        args += list(grads)
    grads = pl.pallas_call(
        partial(write_kernel, geo, grads is None, jobs),
        out_shape=[jax.ShapeDtypeStruct(s, f32) for s in shapes],
        in_specs=[pl.BlockSpec(memory_space=VMEM)] * n + [pl.BlockSpec(memory_space=ANY)] * len(aliases),
        out_specs=[pl.BlockSpec(memory_space=ANY)] * len(shapes),
        scratch_shapes=[pltpu.VMEM((512 * n, width), f32), pltpu.SemaphoreType.DMA((16 * n,))],
        input_output_aliases=aliases,
        compiler_params=pltpu.CompilerParams(vmem_limit_bytes=(2 * n + 4) * 2**20),
        cost_estimate=pl.CostEstimate(flops=10**10, bytes_accessed=1, transcendentals=0),
        name="write",
    )(*args)
    line.last = grads[-1]
    return grads


def solution(mesh):
    run, item, whole = P("dp", "seq", None), P("dp"), P()
    placed = (run, item, P("dp", "seq")) + (whole,) * 19 + (run, item)
    owned = P(AXES)
    return jax.shard_map(
        local,
        mesh=mesh,
        in_specs=placed,
        out_specs=(run, item, run, whole, whole, whole, P(AXES, None), whole, whole, whole, whole,
                   whole, whole, P(None, AXES), owned, P(AXES, None)) + (whole,) * 7,
        check_vma=False,
    )
```
